32 devices in a mesh: rows: 8 (over y, x, core), heads: 4 (over z).
Axes of the slice: x: 2, y: 2, z: 4, core: 2. Of those that a mesh axis runs over, the one named last changes fastest.
Arguments:
- token_ids: int32 [32, 1024], P('rows'), may hold values from 0 to 50271
- segment_ids: int32 [32, 1024], P('rows'), may hold values from 0 to 7, never falling along the last dimension, each value on 1 to 256 neighbouring positions
- row_fill: int32 [32], P('rows'), may hold values from 512 to 1024
- task_ids: int32 [32, 8], P('rows'), may hold values from 0 to 7
- labels: int32 [32, 8], P('rows'), may hold values from 0 to 2
- task_weights: int32 [8], replicated, may hold values from 1 to 4
- word_table: bfloat16 [50272, 1024], P('heads'), may hold values from -6 to 6
- position_table: bfloat16 [258, 1024], replicated, may hold values from -6 to 6
- norm_gains: float32 [3, 1024], replicated, may hold values from 0.5 to 1.5
- norm_biases: float32 [3, 1024], replicated, may hold values from -2 to 2
- dense_biases: float32 [4, 1024], replicated, may hold values from -2 to 2
- qkv_weight: bfloat16 [1024, 3072], replicated, may hold values from -0.1875 to 0.1875
- out_weight: bfloat16 [1024, 1024], replicated, may hold values from -0.5 to 0.5
- ffn_in: bfloat16 [1024, 4096], replicated, may hold values from -0.1875 to 0.1875
- ffn_bias: float32 [4096], replicated, may hold values from -2 to 2
- ffn_out: bfloat16 [4096, 1024], replicated, may hold values from -0.09375 to 0.09375
- vera_a: bfloat16 [1024, 1024], replicated, may hold values from -0.1875 to 0.1875
- vera_b: bfloat16 [1024, 1024], replicated, may hold values from -0.1875 to 0.1875
- scale_d: float32 [2, 1024], replicated, may hold values from 0.05 to 0.5
- scale_b: float32 [2, 1024], replicated, may hold values from -4 to 4
- task_heads: float32 [8, 3, 1024], replicated, may hold values from -0.1875 to 0.1875
- mom_d: float32 [2, 1024], replicated, may hold values from -0.75 to 0.75
- mom_b: float32 [2, 1024], replicated, may hold values from -0.75 to 0.75
- mom_heads: float32 [8, 3, 1024], replicated, may hold values from -4 to 4
- avg_d: float32 [2, 1024], replicated, may hold values from 0.05 to 0.5
- avg_b: float32 [2, 1024], replicated, may hold values from -4 to 4
- avg_heads: float32 [8, 3, 1024], replicated, may hold values from -0.1875 to 0.1875
Outputs:
- loss: float32 [], replicated
- new_mom_d: float32 [2, 1024], replicated
- new_mom_b: float32 [2, 1024], replicated
- new_mom_heads: float32 [8, 3, 1024], replicated
- new_d: float32 [2, 1024], replicated
- new_b: float32 [2, 1024], replicated
- new_heads: float32 [8, 3, 1024], replicated
- new_avg_d: float32 [2, 1024], replicated
- new_avg_b: float32 [2, 1024], replicated
- new_avg_heads: float32 [8, 3, 1024], replicated
- heads_low: bfloat16 [8, 3, 1024], replicated
- stats: float32 [2], replicated
The draws below stay inside these ranges and needn't reach their ends.
Inputs may be any that keep to these rules, and one draw needn't show every extreme that they name: `segment_ids`: in each row segment numbers start at 0, never fall, take every value below 8 and no segment has more than 256 slots.
All inputs are finite; a program needn't handle non-finite values.
Results may differ from the reference program's by a relative error of at most 0.008.
Values may be sent and summed in bfloat16 or wider, within the bound.
A program may use at most 256 MiB of HBM per device.

```python
import math
import jax
import jax.numpy as jnp
import numpy as np
from jax import lax

D = 1024
HEADS = 16
HDIM = 64
FF = 4096
RANK = 1024
VOCAB = 50272
TASKS = 8
CLASSES = 3
SLOTS = 1024
SEGS = 8
MOST = 256
POSN = 258
ROWS = 32


def plant(drawn, stream_key, smallest, largest):
    extent = drawn.shape
    spot = [jax.random.randint(jax.random.fold_in(stream_key, axis), (), 0, extent[axis]) for axis in range(len(extent))]
    drawn = drawn.at[tuple(spot)].set(smallest)
    longest = extent.index(max(extent))
    spot[longest] = (spot[longest] + 1) % extent[longest]
    return drawn.at[tuple(spot)].set(largest)


def block_scale(stream_key, extent, shards, least, high):
    factor_of = 1.0
    for dim, shards_of in shards:
        steps = jax.random.uniform(jax.random.fold_in(jax.random.fold_in(stream_key, 6), dim), (shards_of,), jnp.float32, least / len(shards), high / len(shards))
        factor_of = factor_of * jnp.repeat(jnp.exp(steps), extent[dim] // shards_of).reshape((-1,) + (1,) * (len(extent) - 1 - dim))
    return factor_of


def rank_bounds(count, skew):
    weights = [(1 << 20) // math.isqrt(grade ** skew) + 1 for grade in range(1, count + 1)]
    deviation = 1 + sum(weights) // (1 << 30)
    return np.cumsum(np.array([max(1, weight // deviation) for weight in weights]))


def ranked_ids(rng, dims, count, skew):
    grid = rank_bounds(count, skew)
    lot = jax.random.randint(jax.random.fold_in(rng, 1), dims, 0, int(grid[count - 1]))
    rank = jnp.searchsorted(jnp.asarray(grid, jnp.int32), lot, side="right")
    return jax.random.permutation(jax.random.fold_in(rng, 2), count)[rank].astype(jnp.int32)


def split_up(number_of, total, most, slope):
    portions = [(1 << 20) // math.isqrt(standing ** slope) + 1 for standing in range(2, number_of + 1)]
    rest, given = total - most - (number_of - 1), [1] * (number_of - 1)
    while rest > 0:
        movable = [i for i in range(number_of - 1) if given[i] < most]
        pool, remaining = sum([portions[i] for i in movable]), rest
        for i in movable:
            addition = min(most - given[i], max(1, remaining * portions[i] // pool), rest)
            given[i] = given[i] + addition
            rest = rest - addition
    return np.array([most] + given)


def ragged_sizes(stream_key, number_of, total, limit, lean):
    if number_of == 2:
        one = jax.random.randint(stream_key, (), max(1, total - limit), min(limit, total - 1) + 1)
        return jnp.stack([one, total - one])
    tallies = jnp.asarray(split_up(number_of, total, limit, lean), jnp.int32)
    couples = (number_of - 1) // 2
    source_of, sink = tallies[1:1 + 2 * couples:2], tallies[2:2 + 2 * couples:2]
    slack = jnp.minimum(source_of - 1, limit - sink)
    shifted = jax.random.randint(jax.random.fold_in(stream_key, 1), (couples,), 0, 1 << 20) % (slack + 1)
    tallies = tallies.at[1:1 + 2 * couples:2].set(source_of - shifted).at[2:2 + 2 * couples:2].set(sink + shifted)
    return tallies[jax.random.permutation(jax.random.fold_in(stream_key, 2), number_of)]


def bell_draw(rng, dims, deviation, reach, pieces=(), kind=jnp.bfloat16):
    array = deviation * jax.random.normal(rng, dims, jnp.float32)
    if pieces:
        array = array * block_scale(rng, dims, pieces, -0.22, 0.18)
    return jnp.clip(array, -reach, reach).astype(kind)


def setup_inputs(seed: int = 0) -> dict:
    seeds = jax.random.split(jax.random.key(seed), 28)
    token_ids = plant(ranked_ids(seeds[0], (ROWS, SLOTS), VOCAB, 2), jax.random.fold_in(seeds[0], 3), 0, VOCAB - 1).astype(jnp.int32)
    segment_ids = jax.vmap(lambda own: jnp.searchsorted(jnp.cumsum(ragged_sizes(own, SEGS, SLOTS, MOST, 1)), jnp.arange(SLOTS), side="right"))(jax.random.split(seeds[1], ROWS)).reshape((ROWS, SLOTS)).astype(jnp.int32)
    row_fill = plant(jax.random.randint(seeds[2], (ROWS,), SLOTS // 2, SLOTS + 1), jax.random.fold_in(seeds[2], 1), SLOTS // 2, SLOTS).astype(jnp.int32)
    task_ids = plant(jax.random.randint(seeds[3], (ROWS, SEGS), 0, TASKS), jax.random.fold_in(seeds[3], 1), 0, TASKS - 1).astype(jnp.int32)
    labels = plant(jax.random.randint(seeds[4], (ROWS, SEGS), 0, CLASSES), jax.random.fold_in(seeds[4], 1), 0, CLASSES - 1).astype(jnp.int32)
    task_weights = plant(jax.random.randint(seeds[5], (TASKS,), 1, 5), jax.random.fold_in(seeds[5], 1), 1, 4).astype(jnp.int32)
    word_table = bell_draw(seeds[6], (VOCAB, D), 1.0, 6.0, ((0, 4),))
    position_table = bell_draw(seeds[7], (POSN, D), 1.0, 6.0)
    norm_gains = jnp.clip(1.0 + 0.1 * jax.random.normal(seeds[8], (3, D), jnp.float32), 0.5, 1.5)
    norm_biases = bell_draw(seeds[9], (3, D), 0.3, 2.0, (), jnp.float32)
    dense_biases = bell_draw(seeds[10], (4, D), 0.3, 2.0, (), jnp.float32)
    qkv_weight = bell_draw(seeds[11], (D, 3 * D), D ** -0.5, 0.1875)
    out_weight = bell_draw(seeds[12], (D, D), (D // 8) ** -0.5, 0.5)
    ffn_in = bell_draw(seeds[13], (D, FF), D ** -0.5, 0.1875)
    ffn_bias = bell_draw(seeds[14], (FF,), 0.3, 2.0, (), jnp.float32)
    ffn_out = bell_draw(seeds[15], (FF, D), FF ** -0.5, 0.09375)
    vera_a = bell_draw(seeds[16], (D, RANK), D ** -0.5, 0.1875)
    vera_b = bell_draw(seeds[17], (RANK, D), RANK ** -0.5, 0.1875)
    scale_d = jnp.clip(jnp.exp(jax.random.uniform(seeds[18], (2, RANK), jnp.float32, math.log(0.05), math.log(0.5))), 0.05, 0.5)
    scale_b = bell_draw(seeds[19], (2, D), 1.0, 4.0, (), jnp.float32)
    task_heads = bell_draw(seeds[20], (TASKS, CLASSES, D), D ** -0.5, 0.1875, (), jnp.float32)
    mom_d = bell_draw(seeds[21], (2, RANK), (0.3 * (TASKS / (ROWS * SEGS)) ** 0.5), 0.75, (), jnp.float32)
    mom_b = bell_draw(seeds[22], (2, D), (0.3 * (TASKS / (ROWS * SEGS)) ** 0.5), 0.75, (), jnp.float32)
    mom_heads = bell_draw(seeds[23], (TASKS, CLASSES, D), (1.5 * (TASKS / (ROWS * SEGS)) ** 0.5), 4.0, (), jnp.float32)
    avg_d = jnp.clip(jnp.exp(jax.random.uniform(seeds[24], (2, RANK), jnp.float32, math.log(0.05), math.log(0.5))), 0.05, 0.5)
    avg_b = bell_draw(seeds[25], (2, D), 1.0, 4.0, (), jnp.float32)
    avg_heads = bell_draw(seeds[26], (TASKS, CLASSES, D), D ** -0.5, 0.1875, (), jnp.float32)
    return dict(token_ids=token_ids, segment_ids=segment_ids, row_fill=row_fill, task_ids=task_ids, labels=labels, task_weights=task_weights, word_table=word_table, position_table=position_table, norm_gains=norm_gains, norm_biases=norm_biases, dense_biases=dense_biases, qkv_weight=qkv_weight, out_weight=out_weight, ffn_in=ffn_in, ffn_bias=ffn_bias, ffn_out=ffn_out, vera_a=vera_a, vera_b=vera_b, scale_d=scale_d, scale_b=scale_b, task_heads=task_heads, mom_d=mom_d, mom_b=mom_b, mom_heads=mom_heads, avg_d=avg_d, avg_b=avg_b, avg_heads=avg_heads)


@jax.custom_vjp
def low(v):
    return lax.optimization_barrier(v.astype(jnp.bfloat16)).astype(jnp.float32)

@jax.custom_vjp
def low_back(v):
    return v

def low_keep(v):
    return (low(v), None)

def low_pass(kept, grad):
    return (grad,)

def back_keep(v):
    return (v, None)

def back_low(kept, grad):
    return (low(grad),)
low.defvjp(low_keep, low_pass)
low_back.defvjp(back_keep, back_low)
EPSILON = 1e-05
MOMENTUM = 0.9
AVERAGE = 0.8
RATE_D = 5.0
RATE_B = 20.0
RATE_HEADS = 0.3
HIGHEST = lax.Precision.HIGHEST

def hi_dot(left, right):
    return jnp.dot(left, right, precision=HIGHEST)

def layer_norm(values, gain, shift):
    centred = values - lax.optimization_barrier(jnp.mean(values, -1, keepdims=True))
    spread = lax.optimization_barrier(jnp.mean(centred * centred, -1, keepdims=True))
    return centred * lax.rsqrt(spread + EPSILON) * gain + shift

def round_both(values):
    return low_back(low(values))

def row_tables(seg_row, fill_row, task_row, label_row):
    slot = jnp.arange(seg_row.shape[0], dtype=jnp.int32)
    numbers = jnp.arange(task_row.shape[0], dtype=jnp.int32)
    starts = lax.optimization_barrier(jnp.sum((seg_row[None, :] < numbers[:, None]).astype(jnp.int32), 1))
    member = (seg_row[:, None] == numbers[None, :]).astype(jnp.int32)
    first_slot = lax.optimization_barrier(jnp.sum(member * starts[None, :], 1))
    position = 2 + slot - first_slot
    leading = ((slot == first_slot) & (slot < fill_row)).astype(jnp.int32)
    task = lax.optimization_barrier(jnp.sum(member * task_row[None, :], 1))
    label = lax.optimization_barrier(jnp.sum(member * label_row[None, :], 1))
    return (position, leading, task, label)

def row_mask(seg_row, fill_row):
    slot = jnp.arange(seg_row.shape[0], dtype=jnp.int32)
    same = seg_row[:, None] == seg_row[None, :]
    return same & ((slot[None, :] < fill_row) | (slot[:, None] == slot[None, :]))

def row_loss(scale_d, scale_b, heads, frozen, row, coef):
    word, place, gains, shifts, biases, qkv_w, out_w, w_in, bias_in, w_out, proj_a, proj_b = frozen
    ids, seg_row, fill_row, task_row, label_row = row
    position, leading, task, label = row_tables(seg_row, fill_row, task_row, label_row)
    slots = ids.shape[0]
    x_zero = layer_norm(word[ids] + place[position], gains[0], shifts[0])
    x_low = low(x_zero)
    latent = hi_dot(x_low, proj_a)
    extra_q = low_back(hi_dot(low(latent * scale_d[0]), proj_b))
    extra_v = low_back(hi_dot(low(latent * scale_d[1]), proj_b))
    proj = hi_dot(x_low, qkv_w).reshape(slots, HEADS, 3, HDIM)
    query = round_both(proj[:, :, 0] + (biases[0] + scale_b[0] * extra_q).reshape(slots, HEADS, HDIM))
    key = low(proj[:, :, 1])
    value = round_both(proj[:, :, 2] + (biases[1] + scale_b[1] * extra_v).reshape(slots, HEADS, HDIM))
    scores = low_back(jnp.einsum('qhe,khe->hqk', query, key, precision=HIGHEST) * 0.125)
    scores = jnp.where(row_mask(seg_row, fill_row)[None], scores, -1000000000.0)
    probs = low(jax.nn.softmax(scores, -1))
    mixed = round_both(jnp.einsum('hqk,khe->qhe', probs, value, precision=HIGHEST)).reshape(slots, HEADS * HDIM)
    x_one = layer_norm(x_zero + low_back(hi_dot(mixed, out_w) + biases[2]), gains[1], shifts[1])
    hidden = low_back(hi_dot(low(x_one), w_in) + bias_in)
    active = low(jax.nn.gelu(hidden, approximate=False))
    x_two = layer_norm(x_one + low_back(hi_dot(active, w_out) + biases[3]), gains[2], shifts[2])
    table = low(heads).reshape(TASKS * CLASSES, -1)
    logits = low_back(hi_dot(low(x_two), table.T)).reshape(slots, TASKS, CLASSES)
    pick = (task[:, None] == jnp.arange(TASKS, dtype=jnp.int32)[None, :]).astype(jnp.float32)
    chosen = lax.optimization_barrier(jnp.sum(pick[:, :, None] * logits, 1))
    target = (label[:, None] == jnp.arange(CLASSES, dtype=jnp.int32)[None, :]).astype(jnp.float32)
    terms = jax.nn.logsumexp(chosen, -1) - lax.optimization_barrier(jnp.sum(target * chosen, -1))
    weight = leading.astype(jnp.float32) * lax.optimization_barrier(jnp.sum(pick * coef[None, :], 1))
    return jnp.sum(weight * terms)

def update(weight, grad, moment, average, rate):
    moment_new = MOMENTUM * moment + grad
    weight_new = weight - rate * (grad + MOMENTUM * moment_new)
    return (moment_new, weight_new, AVERAGE * average + (1.0 - AVERAGE) * weight_new)

def reference(token_ids, segment_ids, row_fill, task_ids, labels, task_weights, word_table, position_table, norm_gains, norm_biases, dense_biases, qkv_weight, out_weight, ffn_in, ffn_bias, ffn_out, vera_a, vera_b, scale_d, scale_b, task_heads, mom_d, mom_b, mom_heads, avg_d, avg_b, avg_heads):
    frozen = tuple((item.astype(jnp.float32) for item in (word_table, position_table, norm_gains, norm_biases, dense_biases, qkv_weight, out_weight, ffn_in, ffn_bias, ffn_out, vera_a, vera_b)))
    position, leading, task, label = jax.vmap(row_tables)(segment_ids, row_fill, task_ids, labels)
    pick = (task[:, :, None] == jnp.arange(TASKS, dtype=jnp.int32)).astype(jnp.float32)
    counts = lax.optimization_barrier(jnp.sum(pick * leading[:, :, None].astype(jnp.float32), (0, 1)))
    coef = task_weights.astype(jnp.float32) / jnp.maximum(counts, 1.0)

    def step(carry, row):

        def loss_fn(dvec, bvec, hvec):
            return row_loss(dvec, bvec, hvec, frozen, row, coef)
        value, pull = jax.vjp(loss_fn, scale_d, scale_b, task_heads)
        grads = pull(jnp.ones((), jnp.float32))
        return ((carry[0] + value, carry[1] + grads[0], carry[2] + grads[1], carry[3] + grads[2]), None)
    start = (jnp.zeros((), jnp.float32), jnp.zeros_like(scale_d), jnp.zeros_like(scale_b), jnp.zeros_like(task_heads))
    (loss, grad_d, grad_b, grad_heads), _ = lax.scan(step, start, (token_ids, segment_ids, row_fill, task_ids, labels))
    m_d, w_d, a_d = update(scale_d, grad_d, mom_d, avg_d, RATE_D)
    m_b, w_b, a_b = update(scale_b, grad_b, mom_b, avg_b, RATE_B)
    m_h, w_h, a_h = update(task_heads, grad_heads, mom_heads, avg_heads, RATE_HEADS)
    stats = jnp.stack([jnp.sqrt(jnp.mean(w_d * w_d)), jnp.sqrt(jnp.mean(w_b * w_b))])
    return (loss, m_d, m_b, m_h, w_d, w_b, w_h, a_d, a_b, a_h, w_h.astype(jnp.bfloat16), stats)
```

```python
import functools

import jax
import jax.numpy as jnp
from jax import lax
from jax.experimental import pallas as pl
from jax.experimental.pallas import tpu as pltpu
from jax.sharding import PartitionSpec as P

HEADS = 16
HDIM = 64
TASKS = 8
CLASSES = 3
SEGS = 8
LANES = 128
CHUNKS = 4
EPSILON = 1e-05
MOMENTUM = 0.9
AVERAGE = 0.8
RATE_D = 5.0
RATE_B = 20.0
RATE_HEADS = 0.3
NEG = -1e30
BF = jnp.bfloat16
F32 = jnp.float32
MESH = pl.DeviceIdType.MESH


def mm(left, right):
    return jnp.dot(left, right, preferred_element_type=F32)


def mm_t(left, right):
    return lax.dot_general(left, right, (((1,), (1,)), ((), ())), preferred_element_type=F32)


def mm_l(left, right):
    return lax.dot_general(left, right, (((0,), (0,)), ((), ())), preferred_element_type=F32)


def normed(values):
    centred = values - jnp.mean(values, -1, keepdims=True)
    rstd = lax.rsqrt(jnp.mean(centred * centred, -1, keepdims=True) + EPSILON)
    return centred * rstd, rstd


def norm_back(hat, rstd, gain, grad):
    scaled = grad * gain
    return rstd * (
        scaled
        - jnp.mean(scaled, -1, keepdims=True)
        - hat * jnp.mean(scaled * hat, -1, keepdims=True)
    )


def iota(shape, dim):
    return lax.broadcasted_iota(jnp.int32, shape, dim)


def update(weight, grad, moment, average, rate):
    moment_new = MOMENTUM * moment + grad
    weight_new = weight - rate * (grad + MOMENTUM * moment_new)
    return (moment_new, weight_new, AVERAGE * average + (1.0 - AVERAGE) * weight_new)


def step_kernel(
    cfg,
    fill, task_w, ids, seg, tasks, labels, places, gains, shifts, biases, bias_in, scale_d, scale_b, table,
    raw, qkv_h, out_h, fin_h, fout_h, va_h, vb_h,
    heads_sum, small_sum,
    x, qkv, outw, fin, fout, va, vb,
    lead_out, lead_in, seg_eff, starts_s, xz_s, latent_s, eq_s, qk, expo, ub, ua, ev, pack, rs_in,
    act, slope, gh, tab, gpack, g_in, zq, zacc, zb, gq_s, fx,
    cnt_out, cnt_in, hs, h_in, hr, hr_in, ag, late, lz_in, lr, lr_in,
    load_sem, x_sem, e1_s, e1_r, cnt_ss, cnt_rs, rs_s, rs_r, g_s, g_r, h_ss, h_rs, hr_ss, hr_rs, ag_ss, ag_rs,
    lz_ss, lz_rs, lr_ss, lr_rs,
):
    R, S, G, NR, V = cfg
    D = x.shape[1]
    FF = fin.shape[1]
    PAIRS = HEADS // 2
    L = R * SEGS
    z = lax.axis_index("heads")
    rw = lax.axis_index("rows")
    own_r = lax.rem(z, R)

    loads = [
        pltpu.make_async_copy(src, dst, load_sem.at[i])
        for i, (src, dst) in enumerate(
            ((va_h, va), (vb_h, vb), (qkv_h, qkv), (out_h, outw), (fin_h, fin), (fout_h, fout))
        )
    ]
    x_loads = [
        pltpu.make_async_copy(raw.at[pl.ds(r * S, S)], x.at[pl.ds(r * S, S)], x_sem.at[r]) for r in range(R)
    ]
    for copy in x_loads + loads:
        copy.start()

    barrier = pltpu.get_barrier_semaphore()
    for d in range(1, G):
        pl.semaphore_signal(barrier, inc=1, device_id={"heads": lax.rem(z + d, G)}, device_id_type=MESH)
    for d in range(1, NR):
        pl.semaphore_signal(barrier, inc=1, device_id={"rows": lax.rem(rw + d, NR)}, device_id_type=MESH)
    pl.semaphore_wait(barrier, G - 1 + NR - 1)

    def over(axis, d, src, dst, send, recv):
        me, size = (z, G) if axis == "heads" else (rw, NR)
        return pltpu.make_async_remote_copy(
            src_ref=src, dst_ref=dst, send_sem=send, recv_sem=recv,
            device_id={axis: lax.rem(me + d, size)}, device_id_type=MESH,
        )

    lane = iota((1, LANES), 1)
    low_half = lane < HDIM
    jcol = iota((SEGS, 1), 0)
    slot = iota((1, S), 1)

    def expand(f):
        tiles = [jnp.where(low_half, f[:, 2 * t : 2 * t + 1], f[:, 2 * t + 1 : 2 * t + 2]) for t in range(PAIRS)]
        return jnp.concatenate(tiles, 1)

    def compress(v):
        out = jnp.zeros((v.shape[0], LANES), F32)
        for t in range(PAIRS):
            tile = v[:, LANES * t : LANES * (t + 1)]
            a = jnp.sum(jnp.where(low_half, tile, 0.0), -1, keepdims=True)
            b = jnp.sum(jnp.where(low_half, 0.0, tile), -1, keepdims=True)
            out = jnp.where(lane == 2 * t, a, jnp.where(lane == 2 * t + 1, b, out))
        return out

    eye = iota((SEGS, SEGS), 0) == iota((SEGS, SEGS), 1)
    task_lane = lax.div(lane, CLASSES)
    counts = jnp.zeros((SEGS, LANES), F32)
    for r in range(R):
        seg_row = seg[r : r + 1, :]
        local = ids[r : r + 1, :] - z * V
        own = (local >= 0) & (local < V)
        first = (slot == 0) | (seg_row != pltpu.roll(seg_row, 1, 1))
        seg_eff[r : r + 1, :] = jnp.where(own & (first | (slot < fill[r])), seg_row, -1)
        pick = (seg_row == jcol) & first & own
        starts = jnp.sum((seg_row < jcol).astype(jnp.int32), 1, keepdims=True)
        starts_s[r] = jnp.broadcast_to(starts, (SEGS, LANES))
        lead = (starts < fill[r]).astype(F32)
        task = jnp.sum(jnp.where(eye, tasks[r : r + 1, :], 0), 1, keepdims=True)
        counts = counts + jnp.where((task == task_lane) & (lane < TASKS * CLASSES), lead, 0.0)
        x_loads[r].wait()
        fx[r * SEGS : (r + 1) * SEGS, :] = mm(pick.astype(F32).astype(BF), x[r * S : (r + 1) * S, :])
    lead_out[...] = fx[...].astype(BF)
    cnt_out[...] = counts
    e1 = [over("heads", d, lead_out, lead_in.at[d], e1_s.at[d], e1_r.at[d]) for d in range(1, G)]
    cnt = [over("rows", d, cnt_out, cnt_in.at[d], cnt_ss.at[d], cnt_rs.at[d]) for d in range(1, NR)]
    for copy in e1 + cnt:
        copy.start()

    gain0, shift0 = gains[0:1, :], shifts[0:1, :]
    prow = iota((places.shape[0], 1), 0)
    BLK = 256

    def norm_row(r, _):
        seg_row = seg[pl.ds(r, 1), :]
        begin = jnp.sum(jnp.where(seg_row == jcol, starts_s[r][:, 0:1], 0), 0, keepdims=True)
        offset = slot - begin
        for b in range(S // BLK):
            one = (prow == offset[:, b * BLK : (b + 1) * BLK]).astype(F32).astype(BF)
            rows = pl.ds(pl.multiple_of(r * S + b * BLK, BLK), BLK)
            hat, _ = normed(mm_l(one, places[...]) + x[rows, :].astype(F32))
            x[rows, :] = (hat * gain0 + shift0).astype(BF)
        return 0

    lax.fori_loop(0, R, norm_row, 0)

    for copy in e1:
        copy.wait()
    word = lead_out[...].astype(F32)
    for d in range(1, G):
        word = word + lead_in[d].astype(F32)
    hat, _ = normed(word + places[0:1, :].astype(F32))
    xz = hat * gain0 + shift0
    xz_s[...] = xz
    xl = xz.astype(BF)
    loads[0].wait()
    latent = mm(xl, va[...])
    latent_s[...] = latent
    loads[1].wait()
    eq_s[...] = mm((latent * scale_d[0:1, :]).astype(BF), vb[...])
    loads[2].wait()

    def tile_at(t):
        return pl.ds(pl.multiple_of(LANES * t, LANES), LANES)

    def absorb(t, _):
        r = mm(xl, qkv[:, pl.ds(pl.multiple_of(384 * t, LANES), 256)])
        at = tile_at(t)
        q = jnp.where(low_half, r[:, :LANES], r[:, LANES:]) + (biases[0:1, at] + scale_b[0:1, at] * eq_s[:, at])
        turned = pltpu.roll(q.astype(BF).astype(F32) * 0.125, HDIM, 1)
        a0 = mm_t(jnp.where(low_half, 0.0, turned).astype(BF), qkv[:, tile_at(3 * t)])
        a1 = mm_t(jnp.where(low_half, turned, 0.0).astype(BF), qkv[:, tile_at(3 * t + 2)])
        both = pl.ds(pl.multiple_of(16 * t, 16), 16)
        for r_ in range(R):
            rows = slice(r_ * SEGS, (r_ + 1) * SEGS)
            qk[r_, both, :] = jnp.concatenate([a0[rows], a1[rows]], 0).astype(BF)
        return 0

    lax.fori_loop(0, PAIRS, absorb, 0)

    Q = HEADS * SEGS
    qj = lax.rem(iota((Q, 1), 0), SEGS)
    hsub = iota((HEADS, SEGS, LANES), 0)
    hlane = iota((HEADS, SEGS, LANES), 2)

    def to_lanes(col):
        return jnp.sum(jnp.where(hsub == hlane, col.reshape(HEADS, SEGS, 1), 0.0), 0)

    def to_col(f):
        wide = jnp.broadcast_to(f[None], (HEADS, SEGS, LANES))
        return jnp.sum(jnp.where(hsub == hlane, wide, 0.0), -1, keepdims=True).reshape(Q, 1)

    def attend(p, _):
        parts = []
        for i in range(2):
            r = 2 * p + i
            xr = x[pl.ds(pl.multiple_of(r * S, S), S), :]
            mask = seg_eff[pl.ds(r, 1), :] == qj
            sc = jnp.where(mask, mm_t(qk[r], xr), NEG)
            top = jnp.max(sc, -1, keepdims=True)
            e = jnp.where(mask, jnp.exp(sc - top), 0.0)
            expo[r] = e
            pack[r, :, D : D + LANES] = to_lanes(top)
            pack[r, :, D + LANES :] = to_lanes(jnp.sum(e, -1, keepdims=True))
            parts.append(mm(e.astype(BF), xr).reshape(HEADS, SEGS, D))
        ub[:, pl.ds(pl.multiple_of(2 * SEGS * p, 2 * SEGS), 2 * SEGS), :] = jnp.concatenate(parts, 1).astype(BF)
        return 0

    lax.fori_loop(0, R // 2, attend, 0)

    NT = 256

    def cols(n):
        return pl.ds(pl.multiple_of(NT * n, NT), NT)

    def latents(n, _):
        ua[:, cols(n)] = mm(ub[...].reshape(HEADS * L, D), va[:, cols(n)])
        return 0

    lax.fori_loop(0, D // NT, latents, 0)

    def two(t):
        return pl.ds(pl.multiple_of(2 * L * t, 2 * L), 2 * L)

    def values(t, _):
        at = tile_at(t)
        v0 = mm(ub[2 * t], qkv[:, tile_at(3 * t + 1)])
        v1 = mm(ub[2 * t + 1], qkv[:, tile_at(3 * t + 2)])
        pair = mm((ua[two(t), :] * scale_d[1:2, :]).astype(BF), vb[:, at])
        extra = jnp.where(low_half, pair[:L], pair[L:])
        ev[:, at] = extra
        mixed = jnp.where(low_half, v0, v1) + scale_b[1:2, at] * extra
        pack[:, :, at] = mixed.reshape(R, SEGS, LANES)
        return 0

    lax.fori_loop(0, PAIRS, values, 0)

    rs = [
        over("heads", d, pack.at[lax.rem(lax.rem(z + d, G), R)], rs_in.at[d], rs_s.at[d], rs_r.at[d])
        for d in range(1, G)
    ]
    for copy in rs:
        copy.start()

    for copy in cnt:
        copy.wait()
    total = cnt_out[...]
    for d in range(1, NR):
        total = total + cnt_in[d]
    count = jnp.sum(total, 0, keepdims=True)
    weights = jnp.zeros((1, LANES), F32)
    for t in range(TASKS):
        weights = jnp.where(task_lane == t, task_w[t].astype(F32), weights)
    coef = weights / jnp.maximum(count, 1.0)
    task = jnp.sum(jnp.where(eye, tasks[pl.ds(own_r, 1), :], 0), 1, keepdims=True)
    label = jnp.sum(jnp.where(eye, labels[pl.ds(own_r, 1), :], 0), 1, keepdims=True)
    picked = (task == task_lane) & (lane < TASKS * CLASSES)
    target = picked & (lane - CLASSES * task_lane == label)
    leads = (starts_s[own_r][:, 0:1] < fill[own_r]) & (z < R)
    weight = jnp.sum(jnp.where(target, coef, 0.0), -1, keepdims=True)
    weight = jnp.where(leads, weight, 0.0)
    tab[...] = jnp.concatenate([table[...], jnp.zeros((LANES - TASKS * CLASSES, D), F32)], 0).astype(BF)

    for copy in rs:
        copy.wait()
    got = [pack[own_r]] + [rs_in[d] for d in range(1, G)]
    top = got[0][:, D : D + LANES]
    for part in got[1:]:
        top = jnp.maximum(top, part[:, D : D + LANES])
    shrink = [jnp.exp(part[:, D : D + LANES] - top) for part in got]
    tot = jnp.zeros((SEGS, LANES), F32)
    for part, s in zip(got, shrink):
        tot = tot + part[:, D + LANES :] * s
    tot = jnp.where(lane < HEADS, tot, 1.0)
    mixed = jnp.zeros((SEGS, D), F32)
    for part, s in zip(got, shrink):
        mixed = mixed + expand(s / tot) * part[:, :D]
    mixed = mixed + biases[1:2, :]
    gpack[:, D : D + LANES] = top + jnp.log(tot)

    loads[3].wait()
    r_one = xz_s[pl.ds(pl.multiple_of(own_r * SEGS, SEGS), SEGS), :] + mm(mixed.astype(BF), outw[...]) + biases[2:3, :]
    hat1, rstd1 = normed(r_one)
    x_one = hat1 * gains[1:2, :] + shifts[1:2, :]
    x_one_low = x_one.astype(BF)
    loads[4].wait()

    def hidden(n, _):
        at = cols(n)
        h = mm(x_one_low, fin[:, at]) + bias_in[:, at]
        half = 0.5 * (1.0 + lax.erf(h * 0.7071067811865476))
        act[:, at] = h * half
        slope[:, at] = half + h * (0.3989422804014327 * jnp.exp(-0.5 * h * h))
        return 0

    lax.fori_loop(0, FF // NT, hidden, 0)
    loads[5].wait()
    act_low = act[...].astype(BF)

    def ffn_out_tile(n, _):
        fx[0:SEGS, cols(n)] = mm(act_low, fout[:, cols(n)])
        return 0

    lax.fori_loop(0, D // NT, ffn_out_tile, 0)
    hat2, rstd2 = normed(x_one + fx[0:SEGS, :] + biases[3:4, :])
    x_two = (hat2 * gains[2:3, :] + shifts[2:3, :]).astype(BF)
    logits = mm_t(x_two, tab[...])
    chosen = jnp.where(picked, logits, NEG)
    peak = jnp.max(chosen, -1, keepdims=True)
    sums = jnp.sum(jnp.where(picked, jnp.exp(chosen - peak), 0.0), -1, keepdims=True)
    log_sum = peak + jnp.log(sums)
    hit = jnp.sum(jnp.where(target, logits, 0.0), -1, keepdims=True)
    loss = jnp.sum(weight * (log_sum - hit), 0, keepdims=True)
    soft = jnp.where(picked, jnp.exp(chosen - log_sum), 0.0) - target.astype(F32)
    g_logits = (weight * soft).astype(BF)
    hs[...] = mm(g_logits.astype(F32).T.astype(BF), x_two)[: CHUNKS * 8, :]
    hs[TASKS * CLASSES : TASKS * CLASSES + 8, :] = jnp.broadcast_to(loss, (8, D))
    g_two = mm(g_logits, tab[...])
    g_r2 = norm_back(hat2, rstd2, gains[2:3, :], g_two)
    g_f = g_r2.astype(BF)

    def back_hidden(n, _):
        at = cols(n)
        gh[:, at] = mm_t(g_f, fout[at, :]) * slope[:, at]
        return 0

    lax.fori_loop(0, FF // NT, back_hidden, 0)
    gh_low = gh[...].astype(BF)

    def back_in(n, _):
        fx[0:SEGS, cols(n)] = mm_t(gh_low, fin[cols(n), :])
        return 0

    lax.fori_loop(0, D // NT, back_in, 0)
    g_r1 = norm_back(hat1, rstd1, gains[1:2, :], g_r2 + fx[0:SEGS, :])
    g_mixed = mm_t(g_r1.astype(BF), outw[...]).astype(BF).astype(F32)
    gpack[:, 0:D] = g_mixed
    gpack[:, D + LANES :] = compress(g_mixed * mixed) - compress(g_mixed * biases[1:2, :])

    def spread(src, dst, send, recv, limit, action):
        for d in range(1, G):
            copy = over("heads", d, src(lax.rem(z + d, G)), dst(d), send.at[d], recv(d))
            cond = limit(lax.rem(z + d, G))
            if cond is None:
                action(copy)
            else:
                pl.when(cond)(functools.partial(action, copy))

    mine = None if G == R else z < R

    def g_from(r):
        return pltpu.make_async_remote_copy(
            src_ref=gpack, dst_ref=g_in.at[r], send_sem=g_s.at[0], recv_sem=g_r.at[r],
            device_id={"heads": z}, device_id_type=MESH,
        )

    spread(lambda _: gpack, lambda d: g_in.at[z] if G == R else g_in.at[own_r], g_s,
           lambda d: g_r.at[own_r], lambda peer: mine, lambda c: c.start())

    def chunk_of(peer):
        return hs.at[pl.ds(pl.multiple_of(8 * lax.rem(peer, CHUNKS), 8), 8)]

    def small(peer):
        return None if G == CHUNKS else peer < CHUNKS

    holder = None if G == CHUNKS else z < CHUNKS

    def guarded(cond, f):
        if cond is None:
            f()
        else:
            pl.when(cond)(f)

    spread(chunk_of, lambda d: h_in.at[d], h_ss, lambda d: h_rs.at[d], small, lambda c: c.start())

    def keep_own():
        g_in[own_r] = gpack[...]

    guarded(mine, keep_own)
    for r in range(R):
        pl.when(z != r)(lambda r=r: g_from(r).wait_recv())

    scale = [jnp.exp(pack[r, :, D : D + LANES] - g_in[r, :, D : D + LANES]) for r in range(R)]
    factor = jnp.concatenate([jnp.where(lane < HEADS, s, 0.0) for s in scale], 0)

    def back_value(t, acc):
        at = tile_at(t)
        g = g_in[:, :, at].reshape(L, LANES)
        z0 = mm_t(jnp.where(low_half, g, 0.0).astype(BF), qkv[:, tile_at(3 * t + 1)])
        z1 = mm_t(jnp.where(low_half, 0.0, g).astype(BF), qkv[:, tile_at(3 * t + 2)])
        zacc[two(t), :] = jnp.concatenate([z0, z1], 0)
        gb = g * scale_b[1:2, at]
        both = jnp.concatenate([jnp.where(low_half, gb, 0.0), jnp.where(low_half, 0.0, gb)], 0).astype(BF)
        back = mm_t(both, vb[:, at])
        f0 = jnp.sum(jnp.where(lane == 2 * t, factor, 0.0), -1, keepdims=True)
        f1 = jnp.sum(jnp.where(lane == 2 * t + 1, factor, 0.0), -1, keepdims=True)
        acc = acc + jnp.sum(jnp.concatenate([f0, f1], 0) * ua[two(t), :] * back, 0, keepdims=True)
        zb[two(t), :] = (back * scale_d[1:2, :]).astype(BF)
        return acc

    grad_d1 = lax.fori_loop(0, PAIRS, back_value, jnp.zeros((1, D), F32))
    grad_b1 = jnp.sum(g_in[:, :, 0:D].reshape(L, D) * ev[...] * expand(factor), 0, keepdims=True)

    def back_latent(n, _):
        at = cols(n)
        part = (zacc[:, at] + mm_t(zb[...], va[at, :])).reshape(HEADS, R, SEGS, NT)
        for r in range(R):
            zq[r, :, at] = part[:, r].reshape(Q, NT).astype(BF)
        return 0

    lax.fori_loop(0, D // NT, back_latent, 0)

    def relay():
        acc = chunk_of(z)[...]
        for d in range(1, G):
            over("heads", d, chunk_of(z), h_in.at[d], h_ss.at[d], h_rs.at[d]).wait_recv()
            acc = acc + h_in[d]
        hr[...] = acc
        for d in range(1, NR):
            over("rows", d, hr, hr_in.at[d], hr_ss.at[d], hr_rs.at[d]).start()

    guarded(holder, relay)

    def attend_back(p, _):
        parts = []
        for i in range(2):
            r = 2 * p + i
            xr = x[pl.ds(pl.multiple_of(r * S, S), S), :]
            f = to_col(jnp.where(lane < HEADS, jnp.exp(pack[r, :, D : D + LANES] - g_in[r, :, D : D + LANES]), 0.0))
            delta = to_col(g_in[r, :, D + LANES :])
            ds = (expo[r] * f) * (mm_t(zq[r], xr) - delta)
            parts.append(mm(ds.astype(BF), xr).reshape(HEADS, SEGS, D))
        ub[:, pl.ds(pl.multiple_of(2 * SEGS * p, 2 * SEGS), 2 * SEGS), :] = jnp.concatenate(parts, 1).astype(BF)
        return 0

    lax.fori_loop(0, R // 2, attend_back, 0)

    def relay_two():
        acc = hr[...]
        for d in range(1, NR):
            over("rows", d, hr, hr_in.at[d], hr_ss.at[d], hr_rs.at[d]).wait()
            acc = acc + hr_in[d]
        ag[lax.rem(z, CHUNKS)] = acc
        for d in range(1, G):
            c = lax.rem(z, CHUNKS)
            over("heads", d, ag.at[c], ag.at[c], ag_ss.at[d], ag_rs.at[c]).start()

    guarded(holder, relay_two)

    def back_query(t, _):
        at = tile_at(t)
        k0 = mm(ub[2 * t], qkv[:, tile_at(3 * t)])
        k1 = mm(ub[2 * t + 1], qkv[:, tile_at(3 * t + 2)])
        gq_s[:, at] = pltpu.roll(jnp.where(low_half, k1, k0), HDIM, 1) * 0.125
        return 0

    lax.fori_loop(0, PAIRS, back_query, 0)
    g_query = gq_s[...]
    grad_b0 = jnp.sum(g_query * eq_s[...], 0, keepdims=True)
    back = mm_t((g_query * scale_b[0:1, :]).astype(BF), vb[...])
    grad_d0 = jnp.sum(latent_s[...] * back, 0, keepdims=True)
    four = jnp.concatenate([grad_d0, grad_d1, grad_b0, grad_b1], 0)
    late[...] = jnp.concatenate([four[:, : D // 2], four[:, D // 2 :]], 0)
    leg = [over("heads", d, late, lz_in.at[d], lz_ss.at[d], lz_rs.at[d]) for d in range(1, G)]
    for copy in leg:
        copy.start()
    for copy in leg:
        copy.wait()
    acc = late[...]
    for d in range(1, G):
        acc = acc + lz_in[d]
    lr[...] = acc
    leg = [over("rows", d, lr, lr_in.at[d], lr_ss.at[d], lr_rs.at[d]) for d in range(1, NR)]
    for copy in leg:
        copy.start()

    for c in range(CHUNKS):
        def arrive(c=c):
            pltpu.make_async_remote_copy(
                src_ref=ag.at[c], dst_ref=ag.at[c], send_sem=ag_ss.at[0], recv_sem=ag_rs.at[c],
                device_id={"heads": z}, device_id_type=MESH,
            ).wait_recv()

        pl.when(z != c)(arrive)
    heads_sum[...] = ag[...].reshape(CHUNKS * 8, D)
    spread(lambda _: gpack, lambda d: g_in.at[own_r], g_s, lambda d: g_r.at[own_r], lambda peer: mine,
           lambda c: c.wait_send())
    spread(chunk_of, lambda d: h_in.at[d], h_ss, lambda d: h_rs.at[d], small, lambda c: c.wait_send())

    def sent():
        for d in range(1, G):
            c = lax.rem(z, CHUNKS)
            over("heads", d, ag.at[c], ag.at[c], ag_ss.at[d], ag_rs.at[c]).wait_send()

    guarded(holder, sent)
    for copy in leg:
        copy.wait()
    acc = lr[...]
    for d in range(1, NR):
        acc = acc + lr_in[d]
    small_sum[...] = acc


def on_device(
    sizes,
    token_ids, segment_ids, row_fill, task_ids, labels, task_weights,
    word_table, position_table, norm_gains, norm_biases, dense_biases,
    qkv_weight, out_weight, ffn_in, ffn_bias, ffn_out, vera_a, vera_b,
    scale_d, scale_b, task_heads, mom_d, mom_b, mom_heads, avg_d, avg_b, avg_heads,
):
    G, NR = sizes
    R, S = token_ids.shape
    V, D = word_table.shape
    FF = ffn_in.shape[1]
    L, Q, T = R * SEGS, HEADS * SEGS, R * S
    WIDE = D + 2 * LANES
    z = lax.axis_index("heads")
    local = jnp.clip(token_ids.reshape(-1) - z * V, 0, V - 1)
    raw = jnp.take(word_table, local, axis=0)
    table = task_heads.reshape(TASKS * CLASSES, D)
    v = pltpu.VMEM
    dma = pltpu.SemaphoreType.DMA
    scratch = [
        v((T, D), BF), v(qkv_weight.shape, BF), v(out_weight.shape, BF), v(ffn_in.shape, BF), v(ffn_out.shape, BF),
        v(vera_a.shape, BF), v(vera_b.shape, BF),
        v((L, D), BF), v((G, L, D), BF), v((R, S), jnp.int32), v((R, SEGS, LANES), jnp.int32), v((L, D), F32),
        v((L, D), F32), v((L, D), F32), v((R, Q, D), BF), v((R, Q, S), F32), v((HEADS, L, D), BF),
        v((HEADS * L, D), F32), v((L, D), F32), v((R, SEGS, WIDE), F32), v((G, SEGS, WIDE), F32),
        v((SEGS, FF), F32), v((SEGS, FF), F32), v((SEGS, FF), F32), v((LANES, D), BF), v((SEGS, WIDE), F32),
        v((R, SEGS, WIDE), F32), v((R, Q, D), BF), v((HEADS * L, D), F32), v((HEADS * L, D), BF), v((L, D), F32),
        v((L, D), F32),
        v((SEGS, LANES), F32), v((NR, SEGS, LANES), F32), v((CHUNKS * 8, D), F32), v((G, 8, D), F32), v((8, D), F32),
        v((NR, 8, D), F32), v((CHUNKS, 8, D), F32), v((8, D // 2), F32), v((G, 8, D // 2), F32), v((8, D // 2), F32),
        v((NR, 8, D // 2), F32),
        dma((6,)), dma((R,)), dma((G,)), dma((G,)), dma((NR,)), dma((NR,)), dma((G,)), dma((G,)),
        dma((G,)), dma((R,)), dma((G,)), dma((G,)), dma((NR,)), dma((NR,)), dma((G,)), dma((CHUNKS,)),
        dma((G,)), dma((G,)), dma((NR,)), dma((NR,)),
    ]
    vm, hbm, sm = (pl.BlockSpec(memory_space=m) for m in (pltpu.VMEM, pl.ANY, pltpu.SMEM))
    heads_sum, small_sum = pl.pallas_call(
        functools.partial(step_kernel, (R, S, G, NR, V)),
        out_shape=(jax.ShapeDtypeStruct((CHUNKS * 8, D), F32), jax.ShapeDtypeStruct((8, D // 2), F32)),
        in_specs=[sm, sm] + [vm] * 12 + [hbm] * 7,
        out_specs=(vm, vm),
        scratch_shapes=scratch,
        compiler_params=pltpu.CompilerParams(
            collective_id=0, has_side_effects=True, vmem_limit_bytes=60 * 1024 * 1024
        ),
    )(
        row_fill, task_weights, token_ids, segment_ids, task_ids, labels, position_table[2:], norm_gains, norm_biases,
        dense_biases, ffn_bias.reshape(1, -1), scale_d, scale_b, table,
        raw, qkv_weight, out_weight, ffn_in, ffn_out, vera_a, vera_b,
    )
    four = jnp.concatenate([small_sum[:4], small_sum[4:]], 1)
    grad_d, grad_b = four[:2], four[2:]
    grad_heads = heads_sum[: TASKS * CLASSES].reshape(TASKS, CLASSES, D)
    loss = heads_sum[TASKS * CLASSES, 0]
    m_d, w_d, a_d = update(scale_d, grad_d, mom_d, avg_d, RATE_D)
    m_b, w_b, a_b = update(scale_b, grad_b, mom_b, avg_b, RATE_B)
    m_h, w_h, a_h = update(task_heads, grad_heads, mom_heads, avg_heads, RATE_HEADS)
    stats = jnp.stack([jnp.sqrt(jnp.mean(w_d * w_d)), jnp.sqrt(jnp.mean(w_b * w_b))])
    return (loss, m_d, m_b, m_h, w_d, w_b, w_h, a_d, a_b, a_h, w_h.astype(BF), stats)


def solution(mesh):
    sizes = (mesh.shape["heads"], mesh.shape["rows"])
    by_row = P("rows", None)
    return jax.shard_map(
        functools.partial(on_device, sizes),
        mesh=mesh,
        in_specs=(by_row, by_row, P("rows"), by_row, by_row, P(), P("heads", None)) + (P(),) * 20,
        out_specs=(P(),) * 12,
        check_vma=False,
    )
```

```python
import functools

import jax
import jax.numpy as jnp
from jax import lax
from jax.experimental import pallas as pl
from jax.experimental.pallas import tpu as pltpu
from jax.sharding import PartitionSpec as P

HEADS = 16
HDIM = 64
TASKS = 8
CLASSES = 3
SEGS = 8
LANES = 128
CHUNKS = 4
BLK = 128
FT = 1024
UNROLL = 2
GROUP = 32
SUB = 8
NBUF = 4
FIXED = 1
AHEAD = 3
EPSILON = 1e-05
MOMENTUM = 0.9
AVERAGE = 0.8
RATE_D = 5.0
RATE_B = 20.0
RATE_HEADS = 0.3
NEG = -1e30
BF = jnp.bfloat16
F32 = jnp.float32
MESH = pl.DeviceIdType.MESH


def mm(left, right):
    return jnp.dot(left, right, preferred_element_type=F32)


def mm_t(left, right):
    return lax.dot_general(left, right, (((1,), (1,)), ((), ())), preferred_element_type=F32)


def mm_l(left, right):
    return lax.dot_general(left, right, (((0,), (0,)), ((), ())), preferred_element_type=F32)


def normed(values):
    centred = values - jnp.mean(values, -1, keepdims=True)
    rstd = lax.rsqrt(jnp.mean(centred * centred, -1, keepdims=True) + EPSILON)
    return centred * rstd, rstd


def norm_back(hat, rstd, gain, grad):
    scaled = grad * gain
    return rstd * (
        scaled
        - jnp.mean(scaled, -1, keepdims=True)
        - hat * jnp.mean(scaled * hat, -1, keepdims=True)
    )


def iota(shape, dim):
    return lax.broadcasted_iota(jnp.int32, shape, dim)


def update(weight, grad, moment, average, rate):
    moment_new = MOMENTUM * moment + grad
    weight_new = weight - rate * (grad + MOMENTUM * moment_new)
    return (moment_new, weight_new, AVERAGE * average + (1.0 - AVERAGE) * weight_new)


def gather_kernel(
    cfg, fill, ids, seg, table, gains, shifts, words, x_out, lead_out,
    places, listv, lists, code, off, begins, buf0, buf1, buf2, buf3, acc0, acc1, lead, stage0, stage1, stage2, stage3,
    list_sem, buf_sem, out_sem,
):
    R, S, V = cfg
    D = x_out.shape[1]
    PER = S // BLK
    NB = R * PER
    bufs, accs, stages = (buf0, buf1, buf2, buf3), (acc0, acc1), (stage0, stage1, stage2, stage3)
    z = lax.axis_index("heads")
    slot = iota((1, S), 1)
    lane = iota((1, LANES), 1)
    jcol = iota((SEGS, 1), 0)

    local = ids[...] - z * V
    segs = seg[...]
    fills = jnp.zeros((R, 1), jnp.int32)
    for r in range(R):
        fills = jnp.where(iota((R, 1), 0) == r, fill[r], fills)
    first = (slot == 0) | (segs != pltpu.roll(segs, 1, 1))
    need = (local >= 0) & (local < V) & (first | (slot < fills))
    need_f = need.astype(F32)
    upper = (iota((LANES, LANES), 0) <= iota((LANES, LANES), 1)).astype(F32).astype(BF)
    tiles = [need_f[:, LANES * k : LANES * (k + 1)] for k in range(S // LANES)]
    prefix = mm(jnp.concatenate(tiles, 0).astype(BF), upper)
    count_row = jnp.zeros((1, LANES), F32)
    row8 = iota((8, 1), 0)
    for r in range(R):
        seg_row = segs[r : r + 1, :]
        starts = jnp.sum((seg_row < jcol).astype(jnp.int32), 1, keepdims=True)
        begins[r] = jnp.broadcast_to(starts, (SEGS, LANES))
        offset = slot - jnp.sum(jnp.where(seg_row == jcol, starts, 0), 0, keepdims=True)
        for p in range(PER):
            b = r * PER + p
            here = slice(BLK * p, BLK * (p + 1))
            run = prefix[p * R + r : p * R + r + 1]
            rank = run.astype(jnp.int32) - 1
            wanted = need_f[r : r + 1, here] > 0.0
            word = local[r : r + 1, here]
            key = jnp.where(wanted, (rank & (GROUP - 1)) * SUB + (word & (SUB - 1)), -1)
            spots = (iota((GROUP * SUB, 1), 0) == key).astype(F32).astype(BF)
            marks = jnp.where((rank // GROUP) == row8, lane + 1, 0).astype(F32).astype(BF)
            code[b] = mm_t(marks, spots)
            spots = (iota((BLK, 1), 0) == jnp.where(wanted, rank, -1)).astype(F32).astype(BF)
            tile = word // SUB
            plane = jnp.where(row8 == 0, tile & 255, tile // 256)
            plane = jnp.where((row8 < 2) & wanted, plane, 0).astype(F32).astype(BF)
            both = mm_t(plane, spots)
            listv[b : b + 1, :] = (both[0:1] + 256.0 * both[1:2]).astype(jnp.int32)
            off[b : b + 1, :] = offset[:, here]
            count_row = jnp.where(lane == b, run[:, LANES - 1 :], count_row)
    listv[NB:, :] = jnp.broadcast_to(count_row.astype(jnp.int32), (8, LANES))
    to_scalar = pltpu.make_async_copy(listv, lists, list_sem.at[0])
    to_scalar.start()
    places[...] = table[2:, :]
    lead[...] = jnp.zeros_like(lead)
    for k in range(NBUF):
        bufs[k][0 : GROUP * FIXED] = jnp.zeros((GROUP * FIXED, SUB, D), BF)
    to_scalar.wait()

    def eights(b):
        n = lists[NB, b]
        return jnp.where(n <= GROUP * FIXED, (n + 7) // 8, (n + GROUP - 1) // GROUP * (GROUP // 8))

    def issue(b, k):
        def eight(i, _):
            for u in range(8):
                word = lists[b, i * 8 + u]
                pltpu.make_async_copy(words.at[word], bufs[k].at[i * 8 + u], buf_sem.at[k]).start()
            return 0

        lax.fori_loop(0, eights(b), eight, 0)

    def arrive(b, k):
        part = bufs[k].at[pl.ds(0, 8)]

        def eight(i, _):
            pltpu.make_async_copy(part, part, buf_sem.at[k]).wait()
            return 0

        lax.fori_loop(0, eights(b), eight, 0)

    for b in range(AHEAD):
        issue(b, b)

    col = iota((BLK, 1), 0) + 1
    prow = iota((places.shape[0], 1), 0)
    gain0, shift0 = gains[0:1, :], shifts[0:1, :]

    def wanted_rows(b):
        r, p = b // PER, lax.rem(b, PER)
        spot = begins[r][:, 0:1] - BLK * p + 1
        spot = jnp.where((spot >= 1) & (spot <= BLK), spot, -5)
        return jnp.concatenate([col, spot, jnp.full((8, 1), -5, jnp.int32)], 0).astype(F32)

    def pick(b, k, g, want):
        one = (want == code[b, pl.ds(g, 1), :]).astype(F32).astype(BF)
        start = g * GROUP if isinstance(g, int) else pl.multiple_of(g * GROUP, GROUP)
        return mm(one, bufs[k][pl.ds(start, GROUP)].reshape(GROUP * SUB, D))

    def add_lead(b, got):
        rows = pl.ds(pl.multiple_of(b // PER * SEGS, SEGS), SEGS)
        lead[rows, :] = lead[rows, :] + got

    def out_copy(b, h):
        return pltpu.make_async_copy(
            stages[h], x_out.at[pl.ds(pl.multiple_of(b * BLK, BLK), BLK)], out_sem.at[h]
        )

    def finish(k):
        for c in range(BLK // 16):
            rows = slice(16 * c, 16 * (c + 1))
            hat, _ = normed(accs[k % 2][rows, :])
            stages[k][rows, :] = (hat * gain0 + shift0).astype(BF)

    def four(i, _):
        for k in range(NBUF):
            b, h = NBUF * i + k, k % 2
            pl.when(b + AHEAD < NB)(lambda b=b, k=k: issue(b + AHEAD, (k + AHEAD) % NBUF))
            arrive(b, k)
            before = (k - 1) % NBUF
            pl.when(b > NBUF)(lambda b=b, k=before: out_copy(b - 1 - NBUF, k).wait())
            want = wanted_rows(b)
            one = (prow == off[pl.ds(b, 1), :]).astype(F32).astype(BF)
            got = pick(b, k, 0, want)
            for g in range(1, FIXED):
                got = got + pick(b, k, g, want)
            accs[h][...] = mm_l(one, places[...]) + got[:BLK]
            add_lead(b, got[BLK : BLK + SEGS])
            finish(before)

            def more(g, _, b=b, k=k, h=h):
                got = pick(b, k, g, wanted_rows(b))
                accs[h][...] = accs[h][...] + got[:BLK]
                add_lead(b, got[BLK : BLK + SEGS])
                return 0

            lax.fori_loop(FIXED, (lists[NB, b] + GROUP - 1) // GROUP, more, 0)
            pl.when(b >= 1)(lambda b=b, k=before: out_copy(b - 1, k).start())
        return 0

    lax.fori_loop(0, NB // NBUF, four, 0)
    out_copy(NB - 1 - NBUF, NBUF - 1).wait()
    finish(NBUF - 1)
    out_copy(NB - 1, NBUF - 1).start()
    lead_out[...] = lead[...].astype(BF)
    for k in range(NBUF):
        out_copy(NB - NBUF + k, k).wait()


def gather(token_ids, segment_ids, row_fill, word_table, position_table, gains, shifts):
    R, S = token_ids.shape
    V, D = word_table.shape
    NB = R * S // BLK
    if V % SUB:
        word_table = jnp.pad(word_table, ((0, -V % SUB), (0, 0)))
    v, dma = pltpu.VMEM, pltpu.SemaphoreType.DMA
    vm, hbm, sm = (pl.BlockSpec(memory_space=m) for m in (pltpu.VMEM, pl.ANY, pltpu.SMEM))
    return pl.pallas_call(
        functools.partial(gather_kernel, (R, S, V)),
        out_shape=(jax.ShapeDtypeStruct((R * S, D), BF), jax.ShapeDtypeStruct((R * SEGS, D), BF)),
        in_specs=[sm, vm, vm, vm, vm, vm, hbm],
        out_specs=(hbm, vm),
        scratch_shapes=[
            v((position_table.shape[0] - 2, D), BF), v((NB + 8, LANES), jnp.int32), pltpu.SMEM((NB + 8, LANES), jnp.int32), v((NB, 8, GROUP * SUB), F32),
            v((NB, BLK), jnp.int32), v((R, SEGS, LANES), jnp.int32), *[v((BLK, SUB, D), BF)] * NBUF, v((BLK, D), F32), v((BLK, D), F32),
            v((R * SEGS, D), F32), *[v((BLK, D), BF)] * NBUF, dma((1,)), dma((NBUF,)), dma((NBUF,)),
        ],
        compiler_params=pltpu.CompilerParams(vmem_limit_bytes=60 * 1024 * 1024),
    )(row_fill, token_ids, segment_ids, position_table, gains, shifts, word_table.reshape(-1, SUB, D))


def step_kernel(
    cfg,
    fill, task_w, ids, seg, tasks, labels, lead_out, gains, shifts, biases, bias_in, scale_d, scale_b, table,
    x_h, place_h, qkv_h, out_h, fin_h, fout_h, va_h, vb_h,
    heads_sum, small_sum,
    x, qkv, outw, fin, fout, va, vb,
    place, lead_in, seg_eff, starts_s, xz_s, latent_s, eq_s, qk, expo, ub, ua, ev, pack, rs_in,
    act, slope, gh, tab, gpack, g_in, zq, zacc, zb, gq_s, fx,
    cnt_out, cnt_in, hs, h_in, hr, hr_in, ag, late, lz_in, lr, lr_in,
    load_sem, e1_s, e1_r, cnt_ss, cnt_rs, rs_s, rs_r, g_s, g_r, h_ss, h_rs, hr_ss, hr_rs, ag_ss, ag_rs,
    lz_ss, lz_rs, lr_ss, lr_rs,
):
    R, S, G, NR, V = cfg
    D = x.shape[1]
    FF = fin.shape[1]
    PAIRS = HEADS // 2
    L = R * SEGS
    z = lax.axis_index("heads")
    rw = lax.axis_index("rows")
    own_r = lax.rem(z, R)

    loads = [
        pltpu.make_async_copy(src, dst, load_sem.at[i])
        for i, (src, dst) in enumerate(
            (
                (va_h, va), (vb_h, vb), (qkv_h, qkv), (out_h, outw), (fin_h, fin), (fout_h, fout),
                (place_h.at[pl.ds(0, 16)], place), (x_h, x),
            )
        )
    ]
    for i in (6, 0, 1, 2, 7, 3, 4, 5):
        loads[i].start()

    barrier = pltpu.get_barrier_semaphore()
    for d in range(1, G):
        pl.semaphore_signal(barrier, inc=1, device_id={"heads": lax.rem(z + d, G)}, device_id_type=MESH)
    for d in range(1, NR):
        pl.semaphore_signal(barrier, inc=1, device_id={"rows": lax.rem(rw + d, NR)}, device_id_type=MESH)
    pl.semaphore_wait(barrier, G - 1 + NR - 1)

    def over(axis, d, src, dst, send, recv):
        me, size = (z, G) if axis == "heads" else (rw, NR)
        return pltpu.make_async_remote_copy(
            src_ref=src, dst_ref=dst, send_sem=send, recv_sem=recv,
            device_id={axis: lax.rem(me + d, size)}, device_id_type=MESH,
        )

    lane = iota((1, LANES), 1)
    low_half = lane < HDIM
    jcol = iota((SEGS, 1), 0)
    slot = iota((1, S), 1)

    def expand(f):
        tiles = [jnp.where(low_half, f[:, 2 * t : 2 * t + 1], f[:, 2 * t + 1 : 2 * t + 2]) for t in range(PAIRS)]
        return jnp.concatenate(tiles, 1)

    def compress(v):
        out = jnp.zeros((v.shape[0], LANES), F32)
        for t in range(PAIRS):
            tile = v[:, LANES * t : LANES * (t + 1)]
            a = jnp.sum(jnp.where(low_half, tile, 0.0), -1, keepdims=True)
            b = jnp.sum(jnp.where(low_half, 0.0, tile), -1, keepdims=True)
            out = jnp.where(lane == 2 * t, a, jnp.where(lane == 2 * t + 1, b, out))
        return out

    e1 = [over("heads", d, lead_out, lead_in.at[d], e1_s.at[d], e1_r.at[d]) for d in range(1, G)]
    for copy in e1:
        copy.start()

    eye = iota((SEGS, SEGS), 0) == iota((SEGS, SEGS), 1)
    task_lane = lane & (TASKS - 1)
    counts = jnp.zeros((SEGS, LANES), F32)
    for r in range(R):
        seg_row = seg[r : r + 1, :]
        local = ids[r : r + 1, :] - z * V
        own = (local >= 0) & (local < V)
        first = (slot == 0) | (seg_row != pltpu.roll(seg_row, 1, 1))
        seg_eff[r : r + 1, :] = jnp.where(own & (first | (slot < fill[r])), seg_row, -1)
        starts = jnp.sum((seg_row < jcol).astype(jnp.int32), 1, keepdims=True)
        starts_s[r] = jnp.broadcast_to(starts, (SEGS, LANES))
        lead = (starts < fill[r]).astype(F32)
        task = jnp.sum(jnp.where(eye, tasks[r : r + 1, :], 0), 1, keepdims=True)
        counts = counts + jnp.where((task == task_lane) & (lane < TASKS * CLASSES), lead, 0.0)
    cnt_out[...] = counts
    cnt = [over("rows", d, cnt_out, cnt_in.at[d], cnt_ss.at[d], cnt_rs.at[d]) for d in range(1, NR)]
    for copy in cnt:
        copy.start()
    gain0, shift0 = gains[0:1, :], shifts[0:1, :]

    for copy in e1:
        copy.wait()
    word = lead_out[...].astype(F32)
    for d in range(1, G):
        word = word + lead_in[d].astype(F32)
    loads[6].wait()
    hat, _ = normed(word + place[2:3, :].astype(F32))
    xz = hat * gain0 + shift0
    xz_s[...] = xz
    xl = xz.astype(BF)
    loads[0].wait()
    latent = mm(xl, va[...])
    latent_s[...] = latent
    loads[1].wait()
    eq_s[...] = mm((latent * scale_d[0:1, :]).astype(BF), vb[...])
    loads[2].wait()

    def tile_at(t):
        return pl.ds(pl.multiple_of(LANES * t, LANES), LANES)

    def absorb(t, _):
        r = mm(xl, qkv[:, pl.ds(pl.multiple_of(384 * t, LANES), 256)])
        at = tile_at(t)
        q = jnp.where(low_half, r[:, :LANES], r[:, LANES:]) + (biases[0:1, at] + scale_b[0:1, at] * eq_s[:, at])
        turned = pltpu.roll(q.astype(BF).astype(F32) * 0.125, HDIM, 1)
        a0 = mm_t(jnp.where(low_half, 0.0, turned).astype(BF), qkv[:, tile_at(3 * t)])
        a1 = mm_t(jnp.where(low_half, turned, 0.0).astype(BF), qkv[:, tile_at(3 * t + 2)])
        both = pl.ds(pl.multiple_of(16 * t, 16), 16)
        for r_ in range(R):
            rows = slice(r_ * SEGS, (r_ + 1) * SEGS)
            qk[r_, both, :] = jnp.concatenate([a0[rows], a1[rows]], 0).astype(BF)
        return 0

    lax.fori_loop(0, PAIRS, absorb, 0, unroll=UNROLL)
    loads[7].wait()

    Q = HEADS * SEGS
    qj = lax.rem(iota((Q, 1), 0), SEGS)
    hsub = iota((HEADS, SEGS, LANES), 0)
    hlane = iota((HEADS, SEGS, LANES), 2)

    def to_lanes(col):
        return jnp.sum(jnp.where(hsub == hlane, col.reshape(HEADS, SEGS, 1), 0.0), 0)

    def to_col(f):
        wide = jnp.broadcast_to(f[None], (HEADS, SEGS, LANES))
        return jnp.sum(jnp.where(hsub == hlane, wide, 0.0), -1, keepdims=True).reshape(Q, 1)

    def attend(p, _):
        parts = []
        for i in range(2):
            r = 2 * p + i
            xr = x[pl.ds(pl.multiple_of(r * S, S), S), :]
            mask = seg_eff[pl.ds(r, 1), :] == qj
            sc = jnp.where(mask, mm_t(qk[r], xr), NEG)
            top = jnp.max(sc, -1, keepdims=True)
            e = jnp.where(mask, jnp.exp(sc - top), 0.0)
            expo[r] = e
            pack[r, :, D : D + LANES] = to_lanes(top)
            pack[r, :, D + LANES :] = to_lanes(jnp.sum(e, -1, keepdims=True))
            parts.append(mm(e.astype(BF), xr).reshape(HEADS, SEGS, D))
        ub[:, pl.ds(pl.multiple_of(2 * SEGS * p, 2 * SEGS), 2 * SEGS), :] = jnp.concatenate(parts, 1).astype(BF)
        return 0

    lax.fori_loop(0, R // 2, attend, 0)

    NT = 256

    def cols(n):
        return pl.ds(pl.multiple_of(NT * n, NT), NT)

    def latents(n, _):
        ua[:, cols(n)] = mm(ub[...].reshape(HEADS * L, D), va[:, cols(n)])
        return 0

    lax.fori_loop(0, D // NT, latents, 0)

    def two(t):
        return pl.ds(pl.multiple_of(2 * L * t, 2 * L), 2 * L)

    def values(t, _):
        at = tile_at(t)
        v0 = mm(ub[2 * t], qkv[:, tile_at(3 * t + 1)])
        v1 = mm(ub[2 * t + 1], qkv[:, tile_at(3 * t + 2)])
        pair = mm((ua[two(t), :] * scale_d[1:2, :]).astype(BF), vb[:, at])
        extra = jnp.where(low_half, pair[:L], pair[L:])
        ev[:, at] = extra
        mixed = jnp.where(low_half, v0, v1) + scale_b[1:2, at] * extra
        pack[:, :, at] = mixed.reshape(R, SEGS, LANES)
        return 0

    lax.fori_loop(0, PAIRS, values, 0, unroll=UNROLL)

    rs = [
        over("heads", d, pack.at[lax.rem(lax.rem(z + d, G), R)], rs_in.at[d], rs_s.at[d], rs_r.at[d])
        for d in range(1, G)
    ]
    for copy in rs:
        copy.start()

    for copy in cnt:
        copy.wait()
    total = cnt_out[...]
    for d in range(1, NR):
        total = total + cnt_in[d]
    count = jnp.sum(total, 0, keepdims=True)
    weights = jnp.zeros((1, LANES), F32)
    for t in range(TASKS):
        weights = jnp.where(task_lane == t, task_w[t].astype(F32), weights)
    coef = weights / jnp.maximum(count, 1.0)
    task = jnp.sum(jnp.where(eye, tasks[pl.ds(own_r, 1), :], 0), 1, keepdims=True)
    label = jnp.sum(jnp.where(eye, labels[pl.ds(own_r, 1), :], 0), 1, keepdims=True)
    picked = (task == task_lane) & (lane < TASKS * CLASSES)
    target = picked & (lane // TASKS == label)
    leads = (starts_s[own_r][:, 0:1] < fill[own_r]) & (z < R)
    weight = jnp.sum(jnp.where(target, coef, 0.0), -1, keepdims=True)
    weight = jnp.where(leads, weight, 0.0)
    tab[...] = jnp.concatenate([table[...], jnp.zeros((LANES - TASKS * CLASSES, D), F32)], 0).astype(BF)

    for copy in rs:
        copy.wait()
    got = [pack[own_r]] + [rs_in[d] for d in range(1, G)]
    top = got[0][:, D : D + LANES]
    for part in got[1:]:
        top = jnp.maximum(top, part[:, D : D + LANES])
    shrink = [jnp.exp(part[:, D : D + LANES] - top) for part in got]
    tot = jnp.zeros((SEGS, LANES), F32)
    for part, s in zip(got, shrink):
        tot = tot + part[:, D + LANES :] * s
    tot = jnp.where(lane < HEADS, tot, 1.0)
    mixed = jnp.zeros((SEGS, D), F32)
    for part, s in zip(got, shrink):
        mixed = mixed + expand(s / tot) * part[:, :D]
    mixed = mixed + biases[1:2, :]
    gpack[:, D : D + LANES] = top + jnp.log(tot)

    loads[3].wait()
    r_one = xz_s[pl.ds(pl.multiple_of(own_r * SEGS, SEGS), SEGS), :] + mm(mixed.astype(BF), outw[...]) + biases[2:3, :]
    hat1, rstd1 = normed(r_one)
    x_one = hat1 * gains[1:2, :] + shifts[1:2, :]
    x_one_low = x_one.astype(BF)
    loads[4].wait()

    for n in range(FF // FT):
        at = slice(FT * n, FT * (n + 1))
        act[:, at] = mm(x_one_low, fin[:, at])
    h = act[...] + bias_in[...]
    half = 0.5 * (1.0 + lax.erf(h * 0.7071067811865476))
    act[...] = h * half
    slope[...] = half + h * (0.3989422804014327 * jnp.exp(-0.5 * h * h))
    loads[5].wait()
    act_low = act[...].astype(BF)

    def ffn_out_tile(n, _):
        fx[0:SEGS, cols(n)] = mm(act_low, fout[:, cols(n)])
        return 0

    lax.fori_loop(0, D // NT, ffn_out_tile, 0)
    hat2, rstd2 = normed(x_one + fx[0:SEGS, :] + biases[3:4, :])
    x_two = (hat2 * gains[2:3, :] + shifts[2:3, :]).astype(BF)
    logits = mm_t(x_two, tab[...])
    chosen = jnp.where(picked, logits, NEG)
    peak = jnp.max(chosen, -1, keepdims=True)
    sums = jnp.sum(jnp.where(picked, jnp.exp(chosen - peak), 0.0), -1, keepdims=True)
    log_sum = peak + jnp.log(sums)
    hit = jnp.sum(jnp.where(target, logits, 0.0), -1, keepdims=True)
    loss = jnp.sum(weight * (log_sum - hit), 0, keepdims=True)
    soft = jnp.where(picked, jnp.exp(chosen - log_sum), 0.0) - target.astype(F32)
    g_logits = (weight * soft).astype(BF)
    hs[...] = mm(g_logits.astype(F32).T.astype(BF), x_two)[: CHUNKS * 8, :]
    hs[TASKS * CLASSES : TASKS * CLASSES + 8, :] = jnp.broadcast_to(loss, (8, D))
    g_two = mm(g_logits, tab[...])
    g_r2 = norm_back(hat2, rstd2, gains[2:3, :], g_two)
    g_f = g_r2.astype(BF)

    for n in range(FF // FT):
        at = slice(FT * n, FT * (n + 1))
        gh[:, at] = mm_t(g_f, fout[at, :]) * slope[:, at]
    gh_low = gh[...].astype(BF)

    def back_in(n, _):
        fx[0:SEGS, cols(n)] = mm_t(gh_low, fin[cols(n), :])
        return 0

    lax.fori_loop(0, D // NT, back_in, 0)
    g_r1 = norm_back(hat1, rstd1, gains[1:2, :], g_r2 + fx[0:SEGS, :])
    g_mixed = mm_t(g_r1.astype(BF), outw[...]).astype(BF).astype(F32)
    gpack[:, 0:D] = g_mixed
    gpack[:, D + LANES :] = compress(g_mixed * mixed) - compress(g_mixed * biases[1:2, :])

    def spread(src, dst, send, recv, limit, action):
        for d in range(1, G):
            copy = over("heads", d, src(lax.rem(z + d, G)), dst(d), send.at[d], recv(d))
            cond = limit(lax.rem(z + d, G))
            if cond is None:
                action(copy)
            else:
                pl.when(cond)(functools.partial(action, copy))

    mine = None if G == R else z < R

    def g_from(r):
        return pltpu.make_async_remote_copy(
            src_ref=gpack, dst_ref=g_in.at[r], send_sem=g_s.at[0], recv_sem=g_r.at[r],
            device_id={"heads": z}, device_id_type=MESH,
        )

    spread(lambda _: gpack, lambda d: g_in.at[z] if G == R else g_in.at[own_r], g_s,
           lambda d: g_r.at[own_r], lambda peer: mine, lambda c: c.start())

    def chunk_of(peer):
        return hs.at[pl.ds(pl.multiple_of(8 * lax.rem(peer, CHUNKS), 8), 8)]

    def small(peer):
        return None if G == CHUNKS else peer < CHUNKS

    holder = None if G == CHUNKS else z < CHUNKS

    def guarded(cond, f):
        if cond is None:
            f()
        else:
            pl.when(cond)(f)

    spread(chunk_of, lambda d: h_in.at[d], h_ss, lambda d: h_rs.at[d], small, lambda c: c.start())

    def keep_own():
        g_in[own_r] = gpack[...]

    guarded(mine, keep_own)
    for r in range(R):
        pl.when(z != r)(lambda r=r: g_from(r).wait_recv())

    scale = [jnp.exp(pack[r, :, D : D + LANES] - g_in[r, :, D : D + LANES]) for r in range(R)]
    factor = jnp.concatenate([jnp.where(lane < HEADS, s, 0.0) for s in scale], 0)

    def back_value(t, acc):
        at = tile_at(t)
        g = g_in[:, :, at].reshape(L, LANES)
        z0 = mm_t(jnp.where(low_half, g, 0.0).astype(BF), qkv[:, tile_at(3 * t + 1)])
        z1 = mm_t(jnp.where(low_half, 0.0, g).astype(BF), qkv[:, tile_at(3 * t + 2)])
        zacc[two(t), :] = jnp.concatenate([z0, z1], 0)
        gb = g * scale_b[1:2, at]
        both = jnp.concatenate([jnp.where(low_half, gb, 0.0), jnp.where(low_half, 0.0, gb)], 0).astype(BF)
        back = mm_t(both, vb[:, at])
        f0 = jnp.sum(jnp.where(lane == 2 * t, factor, 0.0), -1, keepdims=True)
        f1 = jnp.sum(jnp.where(lane == 2 * t + 1, factor, 0.0), -1, keepdims=True)
        acc = acc + jnp.sum(jnp.concatenate([f0, f1], 0) * ua[two(t), :] * back, 0, keepdims=True)
        zb[two(t), :] = (back * scale_d[1:2, :]).astype(BF)
        return acc

    grad_d1 = lax.fori_loop(0, PAIRS, back_value, jnp.zeros((1, D), F32), unroll=UNROLL)
    grad_b1 = jnp.sum(g_in[:, :, 0:D].reshape(L, D) * ev[...] * expand(factor), 0, keepdims=True)

    def back_latent(n, _):
        at = cols(n)
        part = (zacc[:, at] + mm_t(zb[...], va[at, :])).reshape(HEADS, R, SEGS, NT)
        for r in range(R):
            zq[r, :, at] = part[:, r].reshape(Q, NT).astype(BF)
        return 0

    lax.fori_loop(0, D // NT, back_latent, 0)

    def relay():
        acc = chunk_of(z)[...]
        for d in range(1, G):
            over("heads", d, chunk_of(z), h_in.at[d], h_ss.at[d], h_rs.at[d]).wait_recv()
            acc = acc + h_in[d]
        hr[...] = acc
        for d in range(1, NR):
            over("rows", d, hr, hr_in.at[d], hr_ss.at[d], hr_rs.at[d]).start()

    guarded(holder, relay)

    def attend_back(p, _):
        parts = []
        for i in range(2):
            r = 2 * p + i
            xr = x[pl.ds(pl.multiple_of(r * S, S), S), :]
            f = to_col(jnp.where(lane < HEADS, jnp.exp(pack[r, :, D : D + LANES] - g_in[r, :, D : D + LANES]), 0.0))
            delta = to_col(g_in[r, :, D + LANES :])
            ds = (expo[r] * f) * (mm_t(zq[r], xr) - delta)
            parts.append(mm(ds.astype(BF), xr).reshape(HEADS, SEGS, D))
        ub[:, pl.ds(pl.multiple_of(2 * SEGS * p, 2 * SEGS), 2 * SEGS), :] = jnp.concatenate(parts, 1).astype(BF)
        return 0

    lax.fori_loop(0, R // 2, attend_back, 0)

    def relay_two():
        acc = hr[...]
        for d in range(1, NR):
            over("rows", d, hr, hr_in.at[d], hr_ss.at[d], hr_rs.at[d]).wait()
            acc = acc + hr_in[d]
        ag[lax.rem(z, CHUNKS)] = acc
        for d in range(1, G):
            c = lax.rem(z, CHUNKS)
            over("heads", d, ag.at[c], ag.at[c], ag_ss.at[d], ag_rs.at[c]).start()

    guarded(holder, relay_two)

    def back_query(t, _):
        at = tile_at(t)
        k0 = mm(ub[2 * t], qkv[:, tile_at(3 * t)])
        k1 = mm(ub[2 * t + 1], qkv[:, tile_at(3 * t + 2)])
        gq_s[:, at] = pltpu.roll(jnp.where(low_half, k1, k0), HDIM, 1) * 0.125
        return 0

    lax.fori_loop(0, PAIRS, back_query, 0, unroll=UNROLL)
    g_query = gq_s[...]
    grad_b0 = jnp.sum(g_query * eq_s[...], 0, keepdims=True)
    back = mm_t((g_query * scale_b[0:1, :]).astype(BF), vb[...])
    grad_d0 = jnp.sum(latent_s[...] * back, 0, keepdims=True)
    four = jnp.concatenate([grad_d0, grad_d1, grad_b0, grad_b1], 0)
    late[...] = jnp.concatenate([four[:, : D // 2], four[:, D // 2 :]], 0)
    leg = [over("heads", d, late, lz_in.at[d], lz_ss.at[d], lz_rs.at[d]) for d in range(1, G)]
    for copy in leg:
        copy.start()
    for copy in leg:
        copy.wait()
    acc = late[...]
    for d in range(1, G):
        acc = acc + lz_in[d]
    lr[...] = acc
    leg = [over("rows", d, lr, lr_in.at[d], lr_ss.at[d], lr_rs.at[d]) for d in range(1, NR)]
    for copy in leg:
        copy.start()

    for c in range(CHUNKS):
        def arrive(c=c):
            pltpu.make_async_remote_copy(
                src_ref=ag.at[c], dst_ref=ag.at[c], send_sem=ag_ss.at[0], recv_sem=ag_rs.at[c],
                device_id={"heads": z}, device_id_type=MESH,
            ).wait_recv()

        pl.when(z != c)(arrive)
    heads_sum[...] = ag[...].reshape(CHUNKS * 8, D)
    spread(lambda _: gpack, lambda d: g_in.at[own_r], g_s, lambda d: g_r.at[own_r], lambda peer: mine,
           lambda c: c.wait_send())
    spread(chunk_of, lambda d: h_in.at[d], h_ss, lambda d: h_rs.at[d], small, lambda c: c.wait_send())

    def sent():
        for d in range(1, G):
            c = lax.rem(z, CHUNKS)
            over("heads", d, ag.at[c], ag.at[c], ag_ss.at[d], ag_rs.at[c]).wait_send()

    guarded(holder, sent)
    for copy in leg:
        copy.wait()
    acc = lr[...]
    for d in range(1, NR):
        acc = acc + lr_in[d]
    small_sum[...] = acc


def update_kernel(
    heads_sum, small_sum, scale_d, scale_b, table, mom_d, mom_b, mom_h, avg_d, avg_b, avg_h,
    loss, m_d, m_b, m_h, w_d, w_b, w_h, a_d, a_b, a_h, low, stats,
):
    count = table.shape[0]
    four = jnp.concatenate([small_sum[0:4, :], small_sum[4:8, :]], 1)
    m_d[...], new_d, a_d[...] = update(scale_d[...], four[0:2], mom_d[...], avg_d[...], RATE_D)
    m_b[...], new_b, a_b[...] = update(scale_b[...], four[2:4], mom_b[...], avg_b[...], RATE_B)
    m_h[...], new_h, a_h[...] = update(table[...], heads_sum[:count, :], mom_h[...], avg_h[...], RATE_HEADS)
    w_d[...], w_b[...], w_h[...], low[...] = new_d, new_b, new_h, new_h.astype(BF)
    loss[...] = heads_sum[count : count + 1, 0:1]
    rms = [jnp.sqrt(jnp.mean(jnp.mean(v * v, 1, keepdims=True), 0, keepdims=True)) for v in (new_d, new_b)]
    stats[...] = jnp.concatenate(rms, 1)


def on_device(
    sizes,
    token_ids, segment_ids, row_fill, task_ids, labels, task_weights,
    word_table, position_table, norm_gains, norm_biases, dense_biases,
    qkv_weight, out_weight, ffn_in, ffn_bias, ffn_out, vera_a, vera_b,
    scale_d, scale_b, task_heads, mom_d, mom_b, mom_heads, avg_d, avg_b, avg_heads,
):
    G, NR = sizes
    R, S = token_ids.shape
    V, D = word_table.shape
    FF = ffn_in.shape[1]
    L, Q, T = R * SEGS, HEADS * SEGS, R * S
    WIDE = D + 2 * LANES
    x_low, leads = gather(
        token_ids, segment_ids, row_fill, word_table, position_table, norm_gains, norm_biases
    )

    def flat(value):
        return value.transpose(1, 0, 2).reshape(CLASSES * TASKS, D)

    table, mom_h, avg_h = flat(task_heads), flat(mom_heads), flat(avg_heads)
    v = pltpu.VMEM
    dma = pltpu.SemaphoreType.DMA
    scratch = [
        v((T, D), BF), v(qkv_weight.shape, BF), v(out_weight.shape, BF), v(ffn_in.shape, BF), v(ffn_out.shape, BF),
        v(vera_a.shape, BF), v(vera_b.shape, BF),
        v((16, D), BF), v((G, L, D), BF), v((R, S), jnp.int32), v((R, SEGS, LANES), jnp.int32), v((L, D), F32),
        v((L, D), F32), v((L, D), F32), v((R, Q, D), BF), v((R, Q, S), F32), v((HEADS, L, D), BF),
        v((HEADS * L, D), F32), v((L, D), F32), v((R, SEGS, WIDE), F32), v((G, SEGS, WIDE), F32),
        v((SEGS, FF), F32), v((SEGS, FF), F32), v((SEGS, FF), F32), v((LANES, D), BF), v((SEGS, WIDE), F32),
        v((R, SEGS, WIDE), F32), v((R, Q, D), BF), v((HEADS * L, D), F32), v((HEADS * L, D), BF), v((L, D), F32),
        v((L, D), F32),
        v((SEGS, LANES), F32), v((NR, SEGS, LANES), F32), v((CHUNKS * 8, D), F32), v((G, 8, D), F32), v((8, D), F32),
        v((NR, 8, D), F32), v((CHUNKS, 8, D), F32), v((8, D // 2), F32), v((G, 8, D // 2), F32), v((8, D // 2), F32),
        v((NR, 8, D // 2), F32),
        dma((8,)), dma((G,)), dma((G,)), dma((NR,)), dma((NR,)), dma((G,)), dma((G,)),
        dma((G,)), dma((R,)), dma((G,)), dma((G,)), dma((NR,)), dma((NR,)), dma((G,)), dma((CHUNKS,)),
        dma((G,)), dma((G,)), dma((NR,)), dma((NR,)),
    ]
    vm, hbm, sm = (pl.BlockSpec(memory_space=m) for m in (pltpu.VMEM, pl.ANY, pltpu.SMEM))
    heads_sum, small_sum = pl.pallas_call(
        functools.partial(step_kernel, (R, S, G, NR, V)),
        out_shape=(jax.ShapeDtypeStruct((CHUNKS * 8, D), F32), jax.ShapeDtypeStruct((8, D // 2), F32)),
        in_specs=[sm, sm] + [vm] * 12 + [hbm] * 8,
        out_specs=(vm, vm),
        scratch_shapes=scratch,
        compiler_params=pltpu.CompilerParams(
            collective_id=0, has_side_effects=True, vmem_limit_bytes=60 * 1024 * 1024
        ),
    )(
        row_fill, task_weights, token_ids, segment_ids, task_ids, labels, leads, norm_gains, norm_biases,
        dense_biases, ffn_bias.reshape(1, -1), scale_d, scale_b, table,
        x_low, position_table, qkv_weight, out_weight, ffn_in, ffn_out, vera_a, vera_b,
    )
    like = jax.ShapeDtypeStruct
    two, many = like((2, D), F32), like((CLASSES * TASKS, D), F32)
    loss, m_d, m_b, m_h, w_d, w_b, w_h, a_d, a_b, a_h, low, stats = pl.pallas_call(
        update_kernel,
        out_shape=(
            like((1, 1), F32), two, two, many, two, two, many, two, two, many, like((CLASSES * TASKS, D), BF), like((1, 2), F32),
        ),
        in_specs=[vm] * 11,
        out_specs=(vm,) * 12,
    )(heads_sum, small_sum, scale_d, scale_b, table, mom_d, mom_b, mom_h, avg_d, avg_b, avg_h)

    def unflat(value):
        return value.reshape(CLASSES, TASKS, D).transpose(1, 0, 2)

    return (
        loss.reshape(()), m_d, m_b, unflat(m_h), w_d, w_b, unflat(w_h), a_d, a_b, unflat(a_h), unflat(low), stats.reshape(2),
    )


def solution(mesh):
    sizes = (mesh.shape["heads"], mesh.shape["rows"])
    by_row = P("rows", None)
    return jax.shard_map(
        functools.partial(on_device, sizes),
        mesh=mesh,
        in_specs=(by_row, by_row, P("rows"), by_row, by_row, P(), P("heads", None)) + (P(),) * 20,
        out_specs=(P(),) * 12,
        check_vma=False,
    )
```

```python
import functools

import jax
import jax.numpy as jnp
from jax import lax
from jax.experimental import pallas as pl
from jax.experimental.pallas import tpu as pltpu
from jax.sharding import PartitionSpec as P

HEADS = 16
HDIM = 64
TASKS = 8
CLASSES = 3
SEGS = 8
LANES = 128
CHUNKS = 4
BLK = 256
GROUP = 128
SUB = 2
FT = 1024
UNROLL = 8
EPSILON = 1e-05
MOMENTUM = 0.9
AVERAGE = 0.8
RATE_D = 5.0
RATE_B = 20.0
RATE_HEADS = 0.3
NEG = -1e30
BF = jnp.bfloat16
F32 = jnp.float32
MESH = pl.DeviceIdType.MESH


def mm(left, right):
    return jnp.dot(left, right, preferred_element_type=F32)


def mm_t(left, right):
    return lax.dot_general(left, right, (((1,), (1,)), ((), ())), preferred_element_type=F32)


def mm_l(left, right):
    return lax.dot_general(left, right, (((0,), (0,)), ((), ())), preferred_element_type=F32)


def normed(values):
    centred = values - jnp.mean(values, -1, keepdims=True)
    rstd = lax.rsqrt(jnp.mean(centred * centred, -1, keepdims=True) + EPSILON)
    return centred * rstd, rstd


def norm_back(hat, rstd, gain, grad):
    scaled = grad * gain
    return rstd * (
        scaled
        - jnp.mean(scaled, -1, keepdims=True)
        - hat * jnp.mean(scaled * hat, -1, keepdims=True)
    )


def iota(shape, dim):
    return lax.broadcasted_iota(jnp.int32, shape, dim)


def update(weight, grad, moment, average, rate):
    moment_new = MOMENTUM * moment + grad
    weight_new = weight - rate * (grad + MOMENTUM * moment_new)
    return (moment_new, weight_new, AVERAGE * average + (1.0 - AVERAGE) * weight_new)


def gather_kernel(
    cfg, fill, ids, seg, words, x_out, lead_out,
    listv, lists, code, lead, list_sem, buf_sem, out_sem, *big,
):
    R, S, V = cfg
    D = x_out.shape[1]
    PER = S // BLK
    NB = R * PER
    HALVES = BLK // LANES
    bufs, stages = big[:NB], big[NB:]
    z = lax.axis_index("heads")
    slot = iota((1, S), 1)
    lane = iota((1, LANES), 1)
    jcol = iota((SEGS, 1), 0)
    row8 = iota((8, 1), 0)

    local = ids[...] - z * V
    segs = seg[...]
    fills = jnp.zeros((R, 1), jnp.int32)
    for r in range(R):
        fills = jnp.where(iota((R, 1), 0) == r, fill[r], fills)
    first = (slot == 0) | (segs != pltpu.roll(segs, 1, 1))
    need = (local >= 0) & (local < V) & (first | (slot < fills))
    need_f = need.astype(F32)
    upper = (iota((LANES, LANES), 0) <= iota((LANES, LANES), 1)).astype(F32).astype(BF)
    tiles = [need_f[:, LANES * k : LANES * (k + 1)] for k in range(S // LANES)]
    prefix = mm(jnp.concatenate(tiles, 0).astype(BF), upper)
    count_row = jnp.zeros((1, LANES), F32)
    begins = []
    for r in range(R):
        seg_row = segs[r : r + 1, :]
        starts = jnp.sum((seg_row < jcol).astype(jnp.int32), 1, keepdims=True)
        begins.append(starts)
        for p in range(PER):
            b = r * PER + p
            here = slice(BLK * p, BLK * (p + 1))
            runs, total = [], jnp.zeros((1, 1), F32)
            for h in range(HALVES):
                at = (HALVES * p + h) * R + r
                runs.append(prefix[at : at + 1] + total)
                total = total + prefix[at : at + 1, LANES - 1 :]
            wanted = need_f[r : r + 1, here] > 0.0
            rank = jnp.where(wanted, jnp.concatenate(runs, 1).astype(jnp.int32) - 1, -1)
            word = local[r : r + 1, here]
            key = jnp.where(wanted, (rank & (GROUP - 1)) * SUB + (word & (SUB - 1)), -1)
            spots = (iota((GROUP * SUB, 1), 0) == key).astype(F32).astype(BF)
            marks = jnp.where((rank // GROUP) == row8, iota((1, BLK), 1) + 1, 0).astype(F32).astype(BF)
            code[b] = mm_t(marks, spots)
            spots = (iota((LANES, 1), 0) == jnp.where(wanted, rank & (LANES - 1), -1)).astype(F32).astype(BF)
            tile = word // SUB
            plane = jnp.where(row8 < HALVES, tile & 255, tile // 256)
            plane = jnp.where(((rank // LANES) == (row8 & (HALVES - 1))) & (row8 < 2 * HALVES), plane, 0)
            both = mm_t(plane.astype(F32).astype(BF), spots)
            both = both[0:HALVES] + 256.0 * both[HALVES : 2 * HALVES]
            listv[HALVES * b : HALVES * (b + 1), :] = both.astype(jnp.int32)
            count_row = jnp.where(lane == b, total, count_row)
    listv[HALVES * NB :, :] = jnp.broadcast_to(count_row.astype(jnp.int32), (8, LANES))
    to_scalar = pltpu.make_async_copy(listv, lists, list_sem.at[0])
    to_scalar.start()
    lead[...] = jnp.zeros_like(lead)
    for b in range(NB):
        bufs[b][0 : GROUP * SUB // 8] = jnp.zeros((GROUP * SUB // 8, 8, D), BF)
    to_scalar.wait()

    def eights(b):
        n = lists[HALVES * NB, b]
        return jnp.where(n <= GROUP, (n + 7) // 8, (n + GROUP - 1) // GROUP * (GROUP // 8))

    def issue(r):
        for p in range(PER):
            b = r * PER + p

            def eight(i, _, b=b, h=0):
                for u in range(8):
                    word = lists[HALVES * b + h, i * 8 + u]
                    pltpu.make_async_copy(
                        words.at[pl.ds(pl.multiple_of(SUB * word, SUB), SUB)],
                        bufs[b].at[h * GROUP * SUB // 8 + i * SUB + u * SUB // 8, pl.ds(u * SUB % 8, SUB)],
                        buf_sem.at[r],
                    ).start()
                return 0

            lax.fori_loop(0, jnp.minimum(eights(b), GROUP // 8), eight, 0)

            @pl.when(lists[HALVES * NB, b] > GROUP)
            def more(eight=eight):
                lax.fori_loop(0, GROUP // 8, functools.partial(eight, h=1), 0)

    def arrive(r):
        total = eights(r * PER)
        for p in range(1, PER):
            total = total + eights(r * PER + p)
        part = bufs[r * PER].at[pl.ds(0, SUB)]

        def eight(i, _):
            pltpu.make_async_copy(part, part, buf_sem.at[r]).wait()
            return 0

        lax.fori_loop(0, total, eight, 0)

    col = iota((BLK, 1), 0) + 1

    def pick(b, g):
        spot = begins[b // PER] - BLK * (b % PER) + 1
        spot = jnp.where((spot >= 1) & (spot <= BLK), spot, -5)
        want = jnp.concatenate([col, spot, jnp.full((8, 1), -5, jnp.int32)], 0).astype(F32)
        one = (want == code[b, pl.ds(g, 1), :]).astype(F32).astype(BF)
        rows = bufs[b][g * GROUP * SUB // 8 : (g + 1) * GROUP * SUB // 8]
        return mm(one, rows.reshape(GROUP * SUB, D))

    def add_lead(b, got):
        rows = slice(b // PER * SEGS, (b // PER + 1) * SEGS)
        lead[rows, :] = lead[rows, :] + got

    def out_copy(b):
        return pltpu.make_async_copy(stages[b % (2 * PER)], x_out.at[pl.ds(b * BLK, BLK)], out_sem.at[b])

    issue(0)
    for r in range(R):
        if r + 1 < R:
            issue(r + 1)
        arrive(r)
        for b in range(r * PER, (r + 1) * PER):
            if b >= 2 * PER:
                out_copy(b - 2 * PER).wait()
            got = pick(b, 0)
            stages[b % (2 * PER)][...] = got[:BLK].astype(BF)
            add_lead(b, got[BLK : BLK + SEGS])

            @pl.when(lists[HALVES * NB, b] > GROUP)
            def more(b=b):
                got = pick(b, 1)
                stages[b % (2 * PER)][...] = stages[b % (2 * PER)][...] + got[:BLK].astype(BF)
                add_lead(b, got[BLK : BLK + SEGS])

            out_copy(b).start()

    lead_out[...] = lead[...].astype(BF)
    for b in range(max(NB - 2 * PER, 0), NB):
        out_copy(b).wait()


def gather(token_ids, segment_ids, row_fill, word_table):
    R, S = token_ids.shape
    V, D = word_table.shape
    PER = S // BLK
    NB = R * PER
    HALVES = BLK // LANES
    if V % SUB:
        word_table = jnp.pad(word_table, ((0, -V % SUB), (0, 0)))
    v, dma = pltpu.VMEM, pltpu.SemaphoreType.DMA
    vm, hbm, sm = (pl.BlockSpec(memory_space=m) for m in (pltpu.VMEM, pl.ANY, pltpu.SMEM))
    return pl.pallas_call(
        functools.partial(gather_kernel, (R, S, V)),
        out_shape=(jax.ShapeDtypeStruct((R * S, D), BF), jax.ShapeDtypeStruct((R * SEGS, D), BF)),
        in_specs=[sm, vm, vm, hbm],
        out_specs=(hbm, vm),
        scratch_shapes=[
            v((HALVES * NB + 8, LANES), jnp.int32),
            pltpu.SMEM((HALVES * NB + 8, LANES), jnp.int32), v((NB, 8, GROUP * SUB), F32),
            v((R * SEGS, D), F32), dma((1,)), dma((R,)), dma((NB,)),
            *[v((BLK * SUB // 8, 8, D), BF)] * NB, *[v((BLK, D), BF)] * (2 * PER),
        ],
        compiler_params=pltpu.CompilerParams(vmem_limit_bytes=60 * 1024 * 1024),
    )(row_fill, token_ids, segment_ids, word_table)


def step_kernel(
    cfg,
    fill, task_w, ids, seg, tasks, labels, lead_out, gains, shifts, biases, bias_in, scale_d, scale_b, table,
    x_h, place_h, qkv_h, out_h, fin_h, fout_h, va_h, vb_h,
    heads_sum, small_sum,
    x, qkv, outw, fin, fout, va, vb,
    place, places, lead_in, seg_eff, starts_s, xz_s, latent_s, eq_s, qk, expo, ub, ua, ev, pack, st, st_in, pk, pk_in,
    act, slope, gh, tab, lse_out, lse_in, gpk, gpk_in, dlt_out, dlt_in, g_in, zq, zacc, zb, gq_s, fx,
    cnt_out, cnt_in, hs, h_in, hr, hr_in, ag, late, lz_in, lr, lr_in,
    load_sem, x_sem, e1_s, e1_r, cnt_ss, cnt_rs, rs_s, rs_r, g_s, g_r, h_ss, h_rs, hr_ss, hr_rs, ag_ss, ag_rs,
    lz_ss, lz_rs, lr_ss, lr_rs,
):
    R, S, G, NR, V = cfg
    D = x.shape[1]
    FF = fin.shape[1]
    PAIRS = HEADS // 2
    L = R * SEGS
    z = lax.axis_index("heads")
    rw = lax.axis_index("rows")
    own_r = lax.rem(z, R)

    def x_load(r):
        rows = pl.ds(pl.multiple_of(r * S, S), S)
        return pltpu.make_async_copy(x_h.at[rows], x.at[rows], x_sem.at[r])

    loads = [
        pltpu.make_async_copy(src, dst, load_sem.at[i])
        for i, (src, dst) in enumerate(
            (
                (va_h, va), (vb_h, vb), (qkv_h, qkv), (out_h, outw), (fin_h, fin), (fout_h, fout),
                (place_h, place),
            )
        )
    ]
    for copy in [loads[6]] + [x_load(r) for r in range(R)] + loads[:6]:
        copy.start()

    barrier = pltpu.get_barrier_semaphore()
    for d in range(1, G):
        pl.semaphore_signal(barrier, inc=1, device_id={"heads": lax.rem(z + d, G)}, device_id_type=MESH)
    for d in range(1, NR):
        pl.semaphore_signal(barrier, inc=1, device_id={"rows": lax.rem(rw + d, NR)}, device_id_type=MESH)
    pl.semaphore_wait(barrier, G - 1 + NR - 1)

    def over(axis, d, src, dst, send, recv):
        me, size = (z, G) if axis == "heads" else (rw, NR)
        return pltpu.make_async_remote_copy(
            src_ref=src, dst_ref=dst, send_sem=send, recv_sem=recv,
            device_id={axis: lax.rem(me + d, size)}, device_id_type=MESH,
        )

    lane = iota((1, LANES), 1)
    low_half = lane < HDIM
    jcol = iota((SEGS, 1), 0)
    slot = iota((1, S), 1)

    def expand(f):
        tiles = [jnp.where(low_half, f[:, 2 * t : 2 * t + 1], f[:, 2 * t + 1 : 2 * t + 2]) for t in range(PAIRS)]
        return jnp.concatenate(tiles, 1)

    def compress(v):
        out = jnp.zeros((v.shape[0], LANES), F32)
        for t in range(PAIRS):
            tile = v[:, LANES * t : LANES * (t + 1)]
            a = jnp.sum(jnp.where(low_half, tile, 0.0), -1, keepdims=True)
            b = jnp.sum(jnp.where(low_half, 0.0, tile), -1, keepdims=True)
            out = jnp.where(lane == 2 * t, a, jnp.where(lane == 2 * t + 1, b, out))
        return out

    e1 = [over("heads", d, lead_out, lead_in.at[d], e1_s.at[d], e1_r.at[d]) for d in range(1, G)]
    for copy in e1:
        copy.start()

    eye = iota((SEGS, SEGS), 0) == iota((SEGS, SEGS), 1)
    task_lane = lane & (TASKS - 1)
    counts = jnp.zeros((SEGS, LANES), F32)
    for r in range(R):
        seg_row = seg[r : r + 1, :]
        local = ids[r : r + 1, :] - z * V
        own = (local >= 0) & (local < V)
        first = (slot == 0) | (seg_row != pltpu.roll(seg_row, 1, 1))
        seg_eff[r : r + 1, :] = jnp.where(own & (first | (slot < fill[r])), seg_row, -1)
        starts = jnp.sum((seg_row < jcol).astype(jnp.int32), 1, keepdims=True)
        starts_s[r] = jnp.broadcast_to(starts, (SEGS, LANES))
        lead = (starts < fill[r]).astype(F32)
        task = jnp.sum(jnp.where(eye, tasks[r : r + 1, :], 0), 1, keepdims=True)
        counts = counts + jnp.where((task == task_lane) & (lane < TASKS * CLASSES), lead, 0.0)
    cnt_out[...] = counts
    cnt = [over("rows", d, cnt_out, cnt_in.at[d], cnt_ss.at[d], cnt_rs.at[d]) for d in range(1, NR)]
    for copy in cnt:
        copy.start()
    gain0, shift0 = gains[0:1, :], shifts[0:1, :]
    loads[6].wait()
    places[...] = place[2:, :]
    prow = iota((places.shape[0], 1), 0)

    def norm_row(r, _):
        seg_row = seg[pl.ds(r, 1), :]
        begin = jnp.sum(jnp.where(seg_row == jcol, starts_s[r][:, 0:1], 0), 0, keepdims=True)
        offset = slot - begin
        x_load(r).wait()
        for b in range(S // BLK):
            one = (prow == offset[:, b * BLK : (b + 1) * BLK]).astype(F32).astype(BF)
            rows = pl.ds(pl.multiple_of(r * S + b * BLK, BLK), BLK)
            hat, _ = normed(mm_l(one, places[...]) + x[rows, :].astype(F32))
            x[rows, :] = (hat * gain0 + shift0).astype(BF)
        return 0

    lax.fori_loop(0, R, norm_row, 0)

    for copy in e1:
        copy.wait()
    word = lead_out[...].astype(F32)
    for d in range(1, G):
        word = word + lead_in[d].astype(F32)
    hat, _ = normed(word + places[0:1, :].astype(F32))
    xz = hat * gain0 + shift0
    xz_s[...] = xz
    xl = xz.astype(BF)
    loads[0].wait()
    latent = mm(xl, va[...])
    latent_s[...] = latent
    loads[1].wait()
    eq_s[...] = mm((latent * scale_d[0:1, :]).astype(BF), vb[...])
    loads[2].wait()

    def tile_at(t):
        return pl.ds(pl.multiple_of(LANES * t, LANES), LANES)

    def absorb(t, _):
        r = mm(xl, qkv[:, pl.ds(pl.multiple_of(384 * t, LANES), 256)])
        at = tile_at(t)
        q = jnp.where(low_half, r[:, :LANES], r[:, LANES:]) + (biases[0:1, at] + scale_b[0:1, at] * eq_s[:, at])
        turned = pltpu.roll(q.astype(BF).astype(F32) * 0.125, HDIM, 1)
        a0 = mm_t(jnp.where(low_half, 0.0, turned).astype(BF), qkv[:, tile_at(3 * t)])
        a1 = mm_t(jnp.where(low_half, turned, 0.0).astype(BF), qkv[:, tile_at(3 * t + 2)])
        both = pl.ds(pl.multiple_of(16 * t, 16), 16)
        for r_ in range(R):
            rows = slice(r_ * SEGS, (r_ + 1) * SEGS)
            qk[r_, both, :] = jnp.concatenate([a0[rows], a1[rows]], 0).astype(BF)
        return 0

    lax.fori_loop(0, PAIRS, absorb, 0, unroll=UNROLL)

    Q = HEADS * SEGS
    qj = lax.rem(iota((Q, 1), 0), SEGS)
    hsub = iota((HEADS, SEGS, LANES), 0)
    hlane = iota((HEADS, SEGS, LANES), 2)

    def to_lanes(col):
        return jnp.sum(jnp.where(hsub == hlane, col.reshape(HEADS, SEGS, 1), 0.0), 0)

    def to_col(f):
        wide = jnp.broadcast_to(f[None], (HEADS, SEGS, LANES))
        return jnp.sum(jnp.where(hsub == hlane, wide, 0.0), -1, keepdims=True).reshape(Q, 1)

    def attend(p, _):
        parts = []
        for i in range(2):
            r = 2 * p + i
            xr = x[pl.ds(pl.multiple_of(r * S, S), S), :]
            mask = seg_eff[pl.ds(r, 1), :] == qj
            sc = jnp.where(mask, mm_t(qk[r], xr), NEG)
            top = jnp.max(sc, -1, keepdims=True)
            e = jnp.where(mask, jnp.exp(sc - top), 0.0)
            expo[r] = e
            st[r] = to_lanes(top) + pltpu.roll(to_lanes(jnp.sum(e, -1, keepdims=True)), HDIM, 1)
            parts.append(mm(e.astype(BF), xr).reshape(HEADS, SEGS, D))
        ub[:, pl.ds(pl.multiple_of(2 * SEGS * p, 2 * SEGS), 2 * SEGS), :] = jnp.concatenate(parts, 1).astype(BF)
        return 0

    lax.fori_loop(0, R // 2, attend, 0)

    def row_of(d):
        return lax.rem(lax.rem(z + d, G), R)

    rs = [over("heads", d, st.at[row_of(d)], st_in.at[d], rs_s.at[0, d], rs_r.at[0, d]) for d in range(1, G)]
    for copy in rs:
        copy.start()

    NT = 256

    def cols(n):
        return pl.ds(pl.multiple_of(NT * n, NT), NT)

    def latents(n, _):
        ua[:, cols(n)] = mm(ub[...].reshape(HEADS * L, D), va[:, cols(n)])
        return 0

    lax.fori_loop(0, D // NT, latents, 0, unroll=D // NT)

    def two(t):
        return pl.ds(pl.multiple_of(2 * L * t, 2 * L), 2 * L)

    def values(t, _):
        at = tile_at(t)
        v0 = mm(ub[2 * t], qkv[:, tile_at(3 * t + 1)])
        v1 = mm(ub[2 * t + 1], qkv[:, tile_at(3 * t + 2)])
        pair = mm((ua[two(t), :] * scale_d[1:2, :]).astype(BF), vb[:, at])
        extra = jnp.where(low_half, pair[:L], pair[L:])
        ev[:, at] = extra
        mixed = jnp.where(low_half, v0, v1) + scale_b[1:2, at] * extra
        pack[:, :, at] = mixed.reshape(R, SEGS, LANES)
        return 0

    for half in range(2):
        lax.fori_loop(half * PAIRS // 2, (half + 1) * PAIRS // 2, values, 0, unroll=PAIRS // 2)
        left, quarter = half * D // 2, D // 4
        for r in range(R):
            parts = [pack[r, :, left : left + quarter], pack[r, :, left + quarter : left + 2 * quarter]]
            pk[r, half] = jnp.concatenate(parts, 0).astype(BF)
        leg = [
            over("heads", d, pk.at[row_of(d), half], pk_in.at[d, half], rs_s.at[1 + half, d], rs_r.at[1 + half, d])
            for d in range(1, G)
        ]
        for copy in leg:
            copy.start()
        rs = rs + leg

    def widen(halves):
        both = [halves[i].astype(F32) for i in range(2)]
        return jnp.concatenate([v for h in both for v in (h[:SEGS], h[SEGS:])], 1)

    for copy in cnt:
        copy.wait()
    total = cnt_out[...]
    for d in range(1, NR):
        total = total + cnt_in[d]
    count = jnp.sum(total, 0, keepdims=True)
    weights = jnp.zeros((1, LANES), F32)
    for t in range(TASKS):
        weights = jnp.where(task_lane == t, task_w[t].astype(F32), weights)
    coef = weights / jnp.maximum(count, 1.0)
    task = jnp.sum(jnp.where(eye, tasks[pl.ds(own_r, 1), :], 0), 1, keepdims=True)
    label = jnp.sum(jnp.where(eye, labels[pl.ds(own_r, 1), :], 0), 1, keepdims=True)
    picked = (task == task_lane) & (lane < TASKS * CLASSES)
    target = picked & (lane // TASKS == label)
    leads = (starts_s[own_r][:, 0:1] < fill[own_r]) & (z < R)
    weight = jnp.sum(jnp.where(target, coef, 0.0), -1, keepdims=True)
    weight = jnp.where(leads, weight, 0.0)
    tab[...] = jnp.concatenate([table[...], jnp.zeros((LANES - TASKS * CLASSES, D), F32)], 0).astype(BF)

    for copy in rs:
        copy.wait()
    got = [pack[own_r]] + [widen(pk_in[d]) for d in range(1, G)]
    stat = [st[own_r]] + [st_in[d] for d in range(1, G)]
    top = stat[0]
    for part in stat[1:]:
        top = jnp.maximum(top, part)
    shrink = [jnp.exp(part - top) for part in stat]
    tot = jnp.zeros((SEGS, LANES), F32)
    for part, s in zip(stat, shrink):
        tot = tot + pltpu.roll(part, HDIM, 1) * s
    tot = jnp.where(lane < HEADS, tot, 1.0)
    lse_out[...] = top + jnp.log(tot)
    mixed = jnp.zeros((SEGS, D), F32)
    for part, s in zip(got, shrink):
        mixed = mixed + expand(s / tot) * part
    mixed = mixed + biases[1:2, :]

    def guarded(cond, f):
        if cond is None:
            f()
        else:
            pl.when(cond)(f)

    mine = None if G == R else z < R

    def hand_out(k, src, dst):
        def start():
            for d in range(1, G):
                over("heads", d, src, dst.at[own_r], g_s.at[k, d], g_r.at[k, own_r]).start()

        def keep():
            dst[own_r] = src[...]

        guarded(mine, start)
        guarded(mine, keep)

    def take_in(k, src, dst):
        def one(r):
            pltpu.make_async_remote_copy(
                src_ref=src, dst_ref=dst.at[r], send_sem=g_s.at[k, 0], recv_sem=g_r.at[k, r],
                device_id={"heads": z}, device_id_type=MESH,
            ).wait_recv()

        for r in range(R):
            pl.when(z != r)(functools.partial(one, r))

    hand_out(0, lse_out, lse_in)

    loads[3].wait()
    r_one = xz_s[pl.ds(pl.multiple_of(own_r * SEGS, SEGS), SEGS), :] + mm(mixed.astype(BF), outw[...]) + biases[2:3, :]
    hat1, rstd1 = normed(r_one)
    x_one = hat1 * gains[1:2, :] + shifts[1:2, :]
    x_one_low = x_one.astype(BF)
    loads[4].wait()

    for n in range(FF // FT):
        at = slice(FT * n, FT * (n + 1))
        act[:, at] = mm(x_one_low, fin[:, at])
    h = act[...] + bias_in[...]
    half = 0.5 * (1.0 + lax.erf(h * 0.7071067811865476))
    act[...] = h * half
    slope[...] = half + h * (0.3989422804014327 * jnp.exp(-0.5 * h * h))
    loads[5].wait()
    act_low = act[...].astype(BF)

    def ffn_out_tile(n, _):
        fx[0:SEGS, cols(n)] = mm(act_low, fout[:, cols(n)])
        return 0

    lax.fori_loop(0, D // NT, ffn_out_tile, 0, unroll=D // NT)
    hat2, rstd2 = normed(x_one + fx[0:SEGS, :] + biases[3:4, :])
    x_two = (hat2 * gains[2:3, :] + shifts[2:3, :]).astype(BF)
    logits = mm_t(x_two, tab[...])
    chosen = jnp.where(picked, logits, NEG)
    peak = jnp.max(chosen, -1, keepdims=True)
    sums = jnp.sum(jnp.where(picked, jnp.exp(chosen - peak), 0.0), -1, keepdims=True)
    log_sum = peak + jnp.log(sums)
    hit = jnp.sum(jnp.where(target, logits, 0.0), -1, keepdims=True)
    loss = jnp.sum(weight * (log_sum - hit), 0, keepdims=True)
    soft = jnp.where(picked, jnp.exp(chosen - log_sum), 0.0) - target.astype(F32)
    g_logits = (weight * soft).astype(BF)
    hs[...] = mm(g_logits.astype(F32).T.astype(BF), x_two)[: CHUNKS * 8, :]
    hs[TASKS * CLASSES : TASKS * CLASSES + 8, :] = jnp.broadcast_to(loss, (8, D))
    g_two = mm(g_logits, tab[...])
    g_r2 = norm_back(hat2, rstd2, gains[2:3, :], g_two)
    g_f = g_r2.astype(BF)

    for n in range(FF // FT):
        at = slice(FT * n, FT * (n + 1))
        gh[:, at] = mm_t(g_f, fout[at, :]) * slope[:, at]
    gh_low = gh[...].astype(BF)

    def back_in(n, _):
        fx[0:SEGS, cols(n)] = mm_t(gh_low, fin[cols(n), :])
        return 0

    lax.fori_loop(0, D // NT, back_in, 0, unroll=D // NT)
    g_r1 = norm_back(hat1, rstd1, gains[1:2, :], g_r2 + fx[0:SEGS, :])
    g_mixed = mm_t(g_r1.astype(BF), outw[...]).astype(BF).astype(F32)
    quarters = [g_mixed[:, i * D // 4 : (i + 1) * D // 4] for i in range(4)]
    gpk[0] = jnp.concatenate(quarters[0:2], 0).astype(BF)
    gpk[1] = jnp.concatenate(quarters[2:4], 0).astype(BF)
    hand_out(1, gpk, gpk_in)
    dlt_out[...] = compress(g_mixed * mixed) - compress(g_mixed * biases[1:2, :])
    hand_out(2, dlt_out, dlt_in)

    def spread(src, dst, send, recv, limit, action):
        for d in range(1, G):
            copy = over("heads", d, src(lax.rem(z + d, G)), dst(d), send.at[d], recv(d))
            cond = limit(lax.rem(z + d, G))
            if cond is None:
                action(copy)
            else:
                pl.when(cond)(functools.partial(action, copy))

    def chunk_of(peer):
        return hs.at[pl.ds(pl.multiple_of(8 * lax.rem(peer, CHUNKS), 8), 8)]

    def small(peer):
        return None if G == CHUNKS else peer < CHUNKS

    holder = None if G == CHUNKS else z < CHUNKS
    take_in(0, lse_out, lse_in)
    take_in(1, gpk, gpk_in)
    for r in range(R):
        g_in[r] = widen(gpk_in[r])

    scale = [jnp.exp(st[r] - lse_in[r]) for r in range(R)]
    factor = jnp.concatenate([jnp.where(lane < HEADS, s, 0.0) for s in scale], 0)

    def back_value(t, acc):
        at = tile_at(t)
        g = g_in[:, :, at].reshape(L, LANES)
        z0 = mm_t(jnp.where(low_half, g, 0.0).astype(BF), qkv[:, tile_at(3 * t + 1)])
        z1 = mm_t(jnp.where(low_half, 0.0, g).astype(BF), qkv[:, tile_at(3 * t + 2)])
        zacc[two(t), :] = jnp.concatenate([z0, z1], 0)
        gb = g * scale_b[1:2, at]
        both = jnp.concatenate([jnp.where(low_half, gb, 0.0), jnp.where(low_half, 0.0, gb)], 0).astype(BF)
        back = mm_t(both, vb[:, at])
        f0 = jnp.sum(jnp.where(lane == 2 * t, factor, 0.0), -1, keepdims=True)
        f1 = jnp.sum(jnp.where(lane == 2 * t + 1, factor, 0.0), -1, keepdims=True)
        acc = acc + jnp.sum(jnp.concatenate([f0, f1], 0) * ua[two(t), :] * back, 0, keepdims=True)
        zb[two(t), :] = (back * scale_d[1:2, :]).astype(BF)
        return acc

    grad_d1 = lax.fori_loop(0, PAIRS, back_value, jnp.zeros((1, D), F32), unroll=UNROLL)
    grad_b1 = jnp.sum(g_in[...].reshape(L, D) * ev[...] * expand(factor), 0, keepdims=True)
    extra = TASKS * CLASSES + 1
    hs[extra : extra + 2, :] = jnp.concatenate([grad_d1, grad_b1], 0)
    spread(chunk_of, lambda d: h_in.at[d], h_ss, lambda d: h_rs.at[d], small, lambda c: c.start())

    def back_latent(n, _):
        at = cols(n)
        part = (zacc[:, at] + mm_t(zb[...], va[at, :])).reshape(HEADS, R, SEGS, NT)
        for r in range(R):
            zq[r, :, at] = part[:, r].reshape(Q, NT).astype(BF)
        return 0

    lax.fori_loop(0, D // NT, back_latent, 0, unroll=D // NT)

    def relay():
        acc = chunk_of(z)[...]
        for d in range(1, G):
            over("heads", d, chunk_of(z), h_in.at[d], h_ss.at[d], h_rs.at[d]).wait_recv()
            acc = acc + h_in[d]
        hr[...] = acc
        for d in range(1, NR):
            over("rows", d, hr, hr_in.at[d], hr_ss.at[d], hr_rs.at[d]).start()

    def attend_back(p, _):
        parts = []
        for i in range(2):
            r = 2 * p + i
            xr = x[pl.ds(pl.multiple_of(r * S, S), S), :]
            f = to_col(jnp.where(lane < HEADS, jnp.exp(st[r] - lse_in[r]), 0.0))
            delta = to_col(dlt_in[r])
            ds = (expo[r] * f) * (mm_t(zq[r], xr) - delta)
            parts.append(mm(ds.astype(BF), xr).reshape(HEADS, SEGS, D))
        ub[:, pl.ds(pl.multiple_of(2 * SEGS * p, 2 * SEGS), 2 * SEGS), :] = jnp.concatenate(parts, 1).astype(BF)
        return 0

    take_in(2, dlt_out, dlt_in)
    lax.fori_loop(0, R // 4, attend_back, 0)
    guarded(holder, relay)
    lax.fori_loop(R // 4, R // 2, attend_back, 0)

    def relay_two():
        acc = hr[...]
        for d in range(1, NR):
            over("rows", d, hr, hr_in.at[d], hr_ss.at[d], hr_rs.at[d]).wait()
            acc = acc + hr_in[d]
        ag[lax.rem(z, CHUNKS)] = acc
        for d in range(1, G):
            c = lax.rem(z, CHUNKS)
            over("heads", d, ag.at[c], ag.at[c], ag_ss.at[d], ag_rs.at[c]).start()

    def back_query(t, _):
        at = tile_at(t)
        k0 = mm(ub[2 * t], qkv[:, tile_at(3 * t)])
        k1 = mm(ub[2 * t + 1], qkv[:, tile_at(3 * t + 2)])
        gq_s[:, at] = pltpu.roll(jnp.where(low_half, k1, k0), HDIM, 1) * 0.125
        return 0

    lax.fori_loop(0, PAIRS, back_query, 0, unroll=UNROLL)
    g_query = gq_s[...]
    grad_b0 = jnp.sum(g_query * eq_s[...], 0, keepdims=True)
    back = mm_t((g_query * scale_b[0:1, :]).astype(BF), vb[...])
    grad_d0 = jnp.sum(latent_s[...] * back, 0, keepdims=True)
    two_rows = jnp.concatenate([grad_d0, grad_b0], 0)
    late[...] = jnp.concatenate([two_rows[:, i * D // 4 : (i + 1) * D // 4] for i in range(4)], 0)
    leg = [over("heads", d, late, lz_in.at[d], lz_ss.at[d], lz_rs.at[d]) for d in range(1, G)]
    for copy in leg:
        copy.start()
    guarded(holder, relay_two)
    for copy in leg:
        copy.wait()
    acc = late[...]
    for d in range(1, G):
        acc = acc + lz_in[d]
    lr[...] = acc
    leg = [over("rows", d, lr, lr_in.at[d], lr_ss.at[d], lr_rs.at[d]) for d in range(1, NR)]
    for copy in leg:
        copy.start()

    for c in range(CHUNKS):
        def arrive(c=c):
            pltpu.make_async_remote_copy(
                src_ref=ag.at[c], dst_ref=ag.at[c], send_sem=ag_ss.at[0], recv_sem=ag_rs.at[c],
                device_id={"heads": z}, device_id_type=MESH,
            ).wait_recv()

        pl.when(z != c)(arrive)
    heads_sum[...] = ag[...].reshape(CHUNKS * 8, D)
    def handed():
        for k, (src, dst) in enumerate(((lse_out, lse_in), (gpk, gpk_in), (dlt_out, dlt_in))):
            for d in range(1, G):
                over("heads", d, src, dst.at[own_r], g_s.at[k, d], g_r.at[k, own_r]).wait_send()

    guarded(mine, handed)
    spread(chunk_of, lambda d: h_in.at[d], h_ss, lambda d: h_rs.at[d], small, lambda c: c.wait_send())

    def sent():
        for d in range(1, G):
            c = lax.rem(z, CHUNKS)
            over("heads", d, ag.at[c], ag.at[c], ag_ss.at[d], ag_rs.at[c]).wait_send()

    guarded(holder, sent)
    for copy in leg:
        copy.wait()
    acc = lr[...]
    for d in range(1, NR):
        acc = acc + lr_in[d]
    small_sum[...] = acc


def update_kernel(
    heads_sum, small_sum, scale_d, scale_b, table, mom_d, mom_b, mom_h, avg_d, avg_b, avg_h,
    loss, m_d, m_b, m_h, w_d, w_b, w_h, a_d, a_b, a_h, low, stats,
):
    count = table.shape[0]
    pairs = jnp.concatenate([small_sum[2 * i : 2 * i + 2, :] for i in range(4)], 1)
    more = heads_sum[count + 1 : count + 3, :]
    grad_d = jnp.concatenate([pairs[0:1], more[0:1]], 0)
    grad_b = jnp.concatenate([pairs[1:2], more[1:2]], 0)
    m_d[...], new_d, a_d[...] = update(scale_d[...], grad_d, mom_d[...], avg_d[...], RATE_D)
    m_b[...], new_b, a_b[...] = update(scale_b[...], grad_b, mom_b[...], avg_b[...], RATE_B)
    m_h[...], new_h, a_h[...] = update(table[...], heads_sum[:count, :], mom_h[...], avg_h[...], RATE_HEADS)
    w_d[...], w_b[...], w_h[...], low[...] = new_d, new_b, new_h, new_h.astype(BF)
    loss[...] = heads_sum[count : count + 1, 0:1]
    rms = [jnp.sqrt(jnp.mean(jnp.mean(v * v, 1, keepdims=True), 0, keepdims=True)) for v in (new_d, new_b)]
    stats[...] = jnp.concatenate(rms, 1)


def on_device(
    sizes,
    token_ids, segment_ids, row_fill, task_ids, labels, task_weights,
    word_table, position_table, norm_gains, norm_biases, dense_biases,
    qkv_weight, out_weight, ffn_in, ffn_bias, ffn_out, vera_a, vera_b,
    scale_d, scale_b, task_heads, mom_d, mom_b, mom_heads, avg_d, avg_b, avg_heads,
):
    G, NR = sizes
    R, S = token_ids.shape
    V, D = word_table.shape
    FF = ffn_in.shape[1]
    L, Q, T = R * SEGS, HEADS * SEGS, R * S
    raw, leads = gather(token_ids, segment_ids, row_fill, word_table)

    def flat(value):
        return value.transpose(1, 0, 2).reshape(CLASSES * TASKS, D)

    table, mom_h, avg_h = flat(task_heads), flat(mom_heads), flat(avg_heads)
    v = pltpu.VMEM
    dma = pltpu.SemaphoreType.DMA
    scratch = [
        v((T, D), BF), v(qkv_weight.shape, BF), v(out_weight.shape, BF), v(ffn_in.shape, BF), v(ffn_out.shape, BF),
        v(vera_a.shape, BF), v(vera_b.shape, BF),
        v(position_table.shape, BF), v((position_table.shape[0] - 2, D), BF), v((G, L, D), BF), v((R, S), jnp.int32), v((R, SEGS, LANES), jnp.int32), v((L, D), F32),
        v((L, D), F32), v((L, D), F32), v((R, Q, D), BF), v((R, Q, S), F32), v((HEADS, L, D), BF),
        v((HEADS * L, D), F32), v((L, D), F32), v((R, SEGS, D), F32), v((R, SEGS, LANES), F32), v((G, SEGS, LANES), F32),
        v((R, 2, 2 * SEGS, D // 4), BF), v((G, 2, 2 * SEGS, D // 4), BF),
        v((SEGS, FF), F32), v((SEGS, FF), F32), v((SEGS, FF), F32), v((LANES, D), BF), v((SEGS, LANES), F32), v((R, SEGS, LANES), F32),
        v((2, 2 * SEGS, D // 4), BF), v((R, 2, 2 * SEGS, D // 4), BF), v((SEGS, LANES), F32), v((R, SEGS, LANES), F32),
        v((R, SEGS, D), F32), v((R, Q, D), BF), v((HEADS * L, D), F32), v((HEADS * L, D), BF), v((L, D), F32),
        v((L, D), F32),
        v((SEGS, LANES), F32), v((NR, SEGS, LANES), F32), v((CHUNKS * 8, D), F32), v((G, 8, D), F32), v((8, D), F32),
        v((NR, 8, D), F32), v((CHUNKS, 8, D), F32), v((8, D // 4), F32), v((G, 8, D // 4), F32), v((8, D // 4), F32),
        v((NR, 8, D // 4), F32),
        dma((7,)), dma((R,)), dma((G,)), dma((G,)), dma((NR,)), dma((NR,)), dma((3, G)), dma((3, G)),
        dma((3, G)), dma((3, R)), dma((G,)), dma((G,)), dma((NR,)), dma((NR,)), dma((G,)), dma((CHUNKS,)),
        dma((G,)), dma((G,)), dma((NR,)), dma((NR,)),
    ]
    vm, hbm, sm = (pl.BlockSpec(memory_space=m) for m in (pltpu.VMEM, pl.ANY, pltpu.SMEM))
    heads_sum, small_sum = pl.pallas_call(
        functools.partial(step_kernel, (R, S, G, NR, V)),
        out_shape=(jax.ShapeDtypeStruct((CHUNKS * 8, D), F32), jax.ShapeDtypeStruct((8, D // 4), F32)),
        in_specs=[sm, sm] + [vm] * 12 + [hbm] * 8,
        out_specs=(vm, vm),
        scratch_shapes=scratch,
        compiler_params=pltpu.CompilerParams(
            collective_id=0, has_side_effects=True, vmem_limit_bytes=60 * 1024 * 1024
        ),
    )(
        row_fill, task_weights, token_ids, segment_ids, task_ids, labels, leads, norm_gains, norm_biases,
        dense_biases, ffn_bias.reshape(1, -1), scale_d, scale_b, table,
        raw, position_table, qkv_weight, out_weight, ffn_in, ffn_out, vera_a, vera_b,
    )
    like = jax.ShapeDtypeStruct
    two, many = like((2, D), F32), like((CLASSES * TASKS, D), F32)
    loss, m_d, m_b, m_h, w_d, w_b, w_h, a_d, a_b, a_h, low, stats = pl.pallas_call(
        update_kernel,
        out_shape=(
            like((1, 1), F32), two, two, many, two, two, many, two, two, many, like((CLASSES * TASKS, D), BF), like((1, 2), F32),
        ),
        in_specs=[vm] * 11,
        out_specs=(vm,) * 12,
    )(heads_sum, small_sum, scale_d, scale_b, table, mom_d, mom_b, mom_h, avg_d, avg_b, avg_h)

    def unflat(value):
        return value.reshape(CLASSES, TASKS, D).transpose(1, 0, 2)

    return (
        loss.reshape(()), m_d, m_b, unflat(m_h), w_d, w_b, unflat(w_h), a_d, a_b, unflat(a_h), unflat(low), stats.reshape(2),
    )


def solution(mesh):
    sizes = (mesh.shape["heads"], mesh.shape["rows"])
    by_row = P("rows", None)
    return jax.shard_map(
        functools.partial(on_device, sizes),
        mesh=mesh,
        in_specs=(by_row, by_row, P("rows"), by_row, by_row, P(), P("heads", None)) + (P(),) * 20,
        out_specs=(P(),) * 12,
        check_vma=False,
    )
```

```python
import functools

import jax
import jax.numpy as jnp
from jax import lax
from jax.experimental import pallas as pl
from jax.experimental.pallas import tpu as pltpu
from jax.sharding import PartitionSpec as P

HEADS = 16
HDIM = 64
TASKS = 8
CLASSES = 3
SEGS = 8
LANES = 128
CHUNKS = 4
BLK = 256
GROUP = 128
SUB = 2
FT = 1024
UNROLL = 8
PART = 32
EPSILON = 1e-05
MOMENTUM = 0.9
AVERAGE = 0.8
RATE_D = 5.0
RATE_B = 20.0
RATE_HEADS = 0.3
NEG = -1e30
BF = jnp.bfloat16
F32 = jnp.float32
MESH = pl.DeviceIdType.MESH


def mm(left, right):
    return jnp.dot(left, right, preferred_element_type=F32)


def mm_t(left, right):
    return lax.dot_general(left, right, (((1,), (1,)), ((), ())), preferred_element_type=F32)


def mm_l(left, right):
    return lax.dot_general(left, right, (((0,), (0,)), ((), ())), preferred_element_type=F32)


def normed(values):
    centred = values - jnp.mean(values, -1, keepdims=True)
    rstd = lax.rsqrt(jnp.mean(centred * centred, -1, keepdims=True) + EPSILON)
    return centred * rstd, rstd


def norm_back(hat, rstd, gain, grad):
    scaled = grad * gain
    return rstd * (
        scaled
        - jnp.mean(scaled, -1, keepdims=True)
        - hat * jnp.mean(scaled * hat, -1, keepdims=True)
    )


def iota(shape, dim):
    return lax.broadcasted_iota(jnp.int32, shape, dim)


def update(weight, grad, moment, average, rate):
    moment_new = MOMENTUM * moment + grad
    weight_new = weight - rate * (grad + MOMENTUM * moment_new)
    return (moment_new, weight_new, AVERAGE * average + (1.0 - AVERAGE) * weight_new)


def gather_kernel(
    cfg, fill, ids, seg, words, x_out, lead_out,
    listv, lists, code, lead, begins, bufs, stages, list_sem, buf_sem, out_sem,
):
    R, S, V = cfg
    D = x_out.shape[1]
    PER = S // BLK
    NB = R * PER
    HALVES = BLK // LANES
    STAGES = stages.shape[0]
    z = lax.axis_index("heads")
    slot = iota((1, S), 1)
    lane = iota((1, LANES), 1)
    jcol = iota((SEGS, 1), 0)
    row8 = iota((8, 1), 0)

    local = ids[...] - z * V
    segs = seg[...]
    fills = jnp.zeros((R, 1), jnp.int32)
    for r in range(R):
        fills = jnp.where(iota((R, 1), 0) == r, fill[r], fills)
    first = (slot == 0) | (segs != pltpu.roll(segs, 1, 1))
    need = (local >= 0) & (local < V) & (first | (slot < fills))
    need_f = need.astype(F32)
    upper = (iota((LANES, LANES), 0) <= iota((LANES, LANES), 1)).astype(F32).astype(BF)
    tiles = [need_f[:, LANES * k : LANES * (k + 1)] for k in range(S // LANES)]
    prefix = mm(jnp.concatenate(tiles, 0).astype(BF), upper)
    count_row = jnp.zeros((1, LANES), F32)
    for r in range(R):
        seg_row = segs[r : r + 1, :]
        starts = jnp.sum((seg_row < jcol).astype(jnp.int32), 1, keepdims=True)
        begins[r] = jnp.broadcast_to(starts, (SEGS, LANES))
        for p in range(PER):
            b = r * PER + p
            here = slice(BLK * p, BLK * (p + 1))
            runs, total = [], jnp.zeros((1, 1), F32)
            for h in range(HALVES):
                at = (HALVES * p + h) * R + r
                runs.append(prefix[at : at + 1] + total)
                total = total + prefix[at : at + 1, LANES - 1 :]
            wanted = need_f[r : r + 1, here] > 0.0
            rank = jnp.where(wanted, jnp.concatenate(runs, 1).astype(jnp.int32) - 1, -1)
            word = local[r : r + 1, here]
            key = jnp.where(wanted, (rank & (GROUP - 1)) * SUB + (word & (SUB - 1)), -1)
            spots = (iota((GROUP * SUB, 1), 0) == key).astype(F32).astype(BF)
            marks = jnp.where((rank // GROUP) == row8, iota((1, BLK), 1) + 1, 0).astype(F32).astype(BF)
            code[b] = mm_t(marks, spots)
            spots = (iota((LANES, 1), 0) == jnp.where(wanted, rank & (LANES - 1), -1)).astype(F32).astype(BF)
            tile = word // SUB * SUB
            plane = jnp.where(row8 < HALVES, tile & 255, tile // 256)
            plane = jnp.where(((rank // LANES) == (row8 & (HALVES - 1))) & (row8 < 2 * HALVES), plane, 0)
            both = mm_t(plane.astype(F32).astype(BF), spots)
            both = both[0:HALVES] + 256.0 * both[HALVES : 2 * HALVES]
            listv[HALVES * b : HALVES * (b + 1), :] = both.astype(jnp.int32)
            count_row = jnp.where(lane == b, total, count_row)
    listv[HALVES * NB :, :] = jnp.broadcast_to(count_row.astype(jnp.int32), (8, LANES))
    to_scalar = pltpu.make_async_copy(listv, lists, list_sem.at[0])
    to_scalar.start()
    lead[...] = jnp.zeros_like(lead)
    for b in range(NB):
        bufs[b, 0 : GROUP * SUB // 8] = jnp.zeros((GROUP * SUB // 8, 8, D), BF)
    to_scalar.wait()

    def eights(b):
        n = lists[HALVES * NB, b]
        return jnp.where(n <= GROUP, (n + 7) // 8, (n + GROUP - 1) // GROUP * (GROUP // 8))

    def issue(r):
        for p in range(PER):
            b = r * PER + p

            def eight(i, _, b=b, h=0):
                for u in range(8):
                    word = lists[HALVES * b + h, i * 8 + u]
                    pltpu.make_async_copy(
                        words.at[pl.ds(pl.multiple_of(word, SUB), SUB)],
                        bufs.at[b, h * GROUP * SUB // 8 + i * SUB + u * SUB // 8, pl.ds(u * SUB % 8, SUB)],
                        buf_sem.at[r],
                    ).start()
                return 0

            lax.fori_loop(0, jnp.minimum(eights(b), GROUP // 8), eight, 0)

            @pl.when(lists[HALVES * NB, b] > GROUP)
            def more(eight=eight):
                lax.fori_loop(0, GROUP // 8, functools.partial(eight, h=1), 0)

    def arrive(r):
        total = eights(r * PER)
        for p in range(1, PER):
            total = total + eights(r * PER + p)
        part = bufs.at[0, pl.ds(0, SUB)]

        def eight(i, _):
            pltpu.make_async_copy(part, part, buf_sem.at[r]).wait()
            return 0

        lax.fori_loop(0, total, eight, 0)

    col = iota((BLK, 1), 0) + 1

    def pick(b, g):
        spot = begins[b // PER][:, 0:1] - BLK * lax.rem(b, PER) + 1
        spot = jnp.where((spot >= 1) & (spot <= BLK), spot, -5)
        want = jnp.concatenate([col, spot, jnp.full((8, 1), -5, jnp.int32)], 0).astype(F32)
        one = (want == code[b, pl.ds(g, 1), :]).astype(F32).astype(BF)
        rows = bufs[b, g * GROUP * SUB // 8 : (g + 1) * GROUP * SUB // 8]
        return mm(one, rows.reshape(GROUP * SUB, D))

    def add_lead(b, got):
        rows = pl.ds(pl.multiple_of(b // PER * SEGS, SEGS), SEGS)
        lead[rows, :] = lead[rows, :] + got

    def out_copy(b):
        k = lax.rem(b, STAGES)
        rows = pl.ds(pl.multiple_of(b * BLK, BLK), BLK)
        return pltpu.make_async_copy(stages.at[k], x_out.at[rows], out_sem.at[k])

    for r in range(R):
        issue(r)

    def row(r, _):
        arrive(r)

        def block(p, _):
            b = r * PER + p
            k = lax.rem(b, STAGES)
            pl.when(b >= STAGES)(lambda: out_copy(b - STAGES).wait())
            got = pick(b, 0)
            stages[k] = got[:BLK].astype(BF)
            add_lead(b, got[BLK : BLK + SEGS])

            @pl.when(lists[HALVES * NB, b] > GROUP)
            def more():
                got = pick(b, 1)
                stages[k] = stages[k] + got[:BLK].astype(BF)
                add_lead(b, got[BLK : BLK + SEGS])

            out_copy(b).start()
            return 0

        return lax.fori_loop(0, PER, block, 0)

    lax.fori_loop(0, R, row, 0)
    lead_out[...] = lead[...].astype(BF)
    for k in range(STAGES):
        out_copy(NB - STAGES + k).wait()


def gather(token_ids, segment_ids, row_fill, word_table):
    R, S = token_ids.shape
    V, D = word_table.shape
    PER = S // BLK
    NB = R * PER
    HALVES = BLK // LANES
    if V % SUB:
        word_table = jnp.pad(word_table, ((0, -V % SUB), (0, 0)))
    v, dma = pltpu.VMEM, pltpu.SemaphoreType.DMA
    vm, hbm, sm = (pl.BlockSpec(memory_space=m) for m in (pltpu.VMEM, pl.ANY, pltpu.SMEM))
    return pl.pallas_call(
        functools.partial(gather_kernel, (R, S, V)),
        out_shape=(jax.ShapeDtypeStruct((R * S, D), BF), jax.ShapeDtypeStruct((R * SEGS, D), BF)),
        in_specs=[sm, vm, vm, hbm],
        out_specs=(hbm, vm),
        scratch_shapes=[
            v((HALVES * NB + 8, LANES), jnp.int32),
            pltpu.SMEM((HALVES * NB + 8, LANES), jnp.int32), v((NB, 8, GROUP * SUB), F32),
            v((R * SEGS, D), F32), v((R, SEGS, LANES), jnp.int32),
            v((NB, BLK * SUB // 8, 8, D), BF), v((4, BLK, D), BF), dma((1,)), dma((R,)), dma((4,)),
        ],
        compiler_params=pltpu.CompilerParams(vmem_limit_bytes=60 * 1024 * 1024),
    )(row_fill, token_ids, segment_ids, word_table)


def step_kernel(
    cfg,
    fill, task_w, ids, seg, tasks, labels, lead_out, gains, shifts, biases, bias_in, scale_d, scale_b, table,
    x_h, place_h, qkv_h, out_h, fin_h, fout_h, va_h, vb_h,
    heads_sum, small_sum,
    x, qkv, outw, fin, fout, va, vb,
    place, places, lead_in, seg_eff, starts_s, xz_s, latent_s, eq_s, qk, ub, ua, ev, pack, st, st_in, pk, pk_in,
    act, slope, gh, tab, lse_out, lse_in, gpk, gpk_in, dlt_out, dlt_in, g_in, zq, zacc, zb, gq_s, fx,
    cnt_out, cnt_in, hs, h_in, hr, hr_in, ag, late, lz_in, lr, lr_in,
    load_sem, x_sem, e1_s, e1_r, cnt_ss, cnt_rs, rs_s, rs_r, g_s, g_r, h_ss, h_rs, hr_ss, hr_rs, ag_ss, ag_rs,
    lz_ss, lz_rs, lr_ss, lr_rs, *wide,
):
    R, S, G, NR, V = cfg
    expo, gdot, low, words = wide[:R], wide[R : R + 2], wide[R + 2 : 2 * R + 2], wide[2 * R + 2 :]
    D = x.shape[1]
    FF = fin.shape[1]
    PAIRS = HEADS // 2
    L = R * SEGS
    z = lax.axis_index("heads")
    rw = lax.axis_index("rows")
    own_r = lax.rem(z, R)

    def x_load(r, h):
        return pltpu.make_async_copy(x_h.at[pl.ds(pl.multiple_of(r * S, S), S)], words[h], x_sem.at[h])

    loads = [
        pltpu.make_async_copy(src, dst, load_sem.at[i])
        for i, (src, dst) in enumerate(
            (
                (va_h, va), (vb_h, vb), (qkv_h, qkv), (out_h, outw), (fin_h, fin), (fout_h, fout),
                (place_h, place),
            )
        )
    ]
    for copy in [x_load(0, 0), loads[6], x_load(1, 1)]:
        copy.start()

    barrier = pltpu.get_barrier_semaphore()
    for d in range(1, G):
        pl.semaphore_signal(barrier, inc=1, device_id={"heads": lax.rem(z + d, G)}, device_id_type=MESH)
    for d in range(1, NR):
        pl.semaphore_signal(barrier, inc=1, device_id={"rows": lax.rem(rw + d, NR)}, device_id_type=MESH)
    pl.semaphore_wait(barrier, G - 1 + NR - 1)

    def over(axis, d, src, dst, send, recv):
        me, size = (z, G) if axis == "heads" else (rw, NR)
        return pltpu.make_async_remote_copy(
            src_ref=src, dst_ref=dst, send_sem=send, recv_sem=recv,
            device_id={axis: lax.rem(me + d, size)}, device_id_type=MESH,
        )

    lane = iota((1, LANES), 1)
    low_half = lane < HDIM
    jcol = iota((SEGS, 1), 0)
    slot = iota((1, S), 1)

    def expand(f):
        tiles = [jnp.where(low_half, f[:, 2 * t : 2 * t + 1], f[:, 2 * t + 1 : 2 * t + 2]) for t in range(PAIRS)]
        return jnp.concatenate(tiles, 1)

    def compress(v):
        out = jnp.zeros((v.shape[0], LANES), F32)
        for t in range(PAIRS):
            tile = v[:, LANES * t : LANES * (t + 1)]
            a = jnp.sum(jnp.where(low_half, tile, 0.0), -1, keepdims=True)
            b = jnp.sum(jnp.where(low_half, 0.0, tile), -1, keepdims=True)
            out = jnp.where(lane == 2 * t, a, jnp.where(lane == 2 * t + 1, b, out))
        return out

    e1 = [over("heads", d, lead_out, lead_in.at[d], e1_s.at[d], e1_r.at[d]) for d in range(1, G)]
    for copy in e1:
        copy.start()

    eye = iota((SEGS, SEGS), 0) == iota((SEGS, SEGS), 1)
    task_lane = lane & (TASKS - 1)
    counts = jnp.zeros((SEGS, LANES), F32)
    for r in range(R):
        seg_row = seg[r : r + 1, :]
        local = ids[r : r + 1, :] - z * V
        own = (local >= 0) & (local < V)
        first = (slot == 0) | (seg_row != pltpu.roll(seg_row, 1, 1))
        seg_eff[r : r + 1, :] = jnp.where(own & (first | (slot < fill[r])), seg_row, -1)
        starts = jnp.sum((seg_row < jcol).astype(jnp.int32), 1, keepdims=True)
        starts_s[r] = jnp.broadcast_to(starts, (SEGS, LANES))
        lead = (starts < fill[r]).astype(F32)
        task = jnp.sum(jnp.where(eye, tasks[r : r + 1, :], 0), 1, keepdims=True)
        counts = counts + jnp.where((task == task_lane) & (lane < TASKS * CLASSES), lead, 0.0)
    cnt_out[...] = counts
    cnt = [over("rows", d, cnt_out, cnt_in.at[d], cnt_ss.at[d], cnt_rs.at[d]) for d in range(1, NR)]
    for copy in cnt:
        copy.start()
    gain0, shift0 = gains[0:1, :], shifts[0:1, :]
    loads[6].wait()
    places[...] = place[2:, :]
    prow = iota((places.shape[0], 1), 0)

    STEP = expo[0].shape[0]
    blocks = S // STEP

    def norm_row(r, h):
        seg_row = seg[pl.ds(r, 1), :]
        begin = jnp.sum(jnp.where(seg_row == jcol, starts_s[r][:, 0:1], 0), 0, keepdims=True)
        offset = slot - begin
        x_load(r, h).wait()

        def place_rows(b):
            one = (prow == offset[:, b * STEP : (b + 1) * STEP]).astype(F32).astype(BF)
            expo[b % R][...] = mm_l(one, places[...])

        place_rows(0)
        for b in range(blocks):
            if b + 1 < blocks:
                place_rows(b + 1)
            for c in range(0, STEP, PART):
                at = b * STEP + c
                hat, _ = normed(expo[b % R][c : c + PART, :] + words[h][at : at + PART, :].astype(F32))
                x[pl.ds(pl.multiple_of(r * S + at, PART), PART), :] = (hat * gain0 + shift0).astype(BF)

    def norm_two(i, _):
        for h in range(2):
            norm_row(2 * i + h, h)
            pl.when(i + 1 < R // 2)(lambda h=h: x_load(2 * i + 2 + h, h).start())
        return 0

    loads[0].start()
    loads[1].start()
    loads[2].start()
    lax.fori_loop(0, R // 2, norm_two, 0)

    for copy in e1:
        copy.wait()
    word = lead_out[...].astype(F32)
    for d in range(1, G):
        word = word + lead_in[d].astype(F32)
    hat, _ = normed(word + places[0:1, :].astype(F32))
    xz = hat * gain0 + shift0
    xz_s[...] = xz
    xl = xz.astype(BF)
    loads[0].wait()
    latent = mm(xl, va[...])
    latent_s[...] = latent
    loads[1].wait()
    eq_s[...] = mm((latent * scale_d[0:1, :]).astype(BF), vb[...])
    loads[2].wait()
    for copy in loads[3:6]:
        copy.start()

    def tile_at(t):
        return pl.ds(pl.multiple_of(LANES * t, LANES), LANES)

    def absorb(t, _):
        r = mm(xl, qkv[:, pl.ds(pl.multiple_of(384 * t, LANES), 256)])
        at = tile_at(t)
        q = jnp.where(low_half, r[:, :LANES], r[:, LANES:]) + (biases[0:1, at] + scale_b[0:1, at] * eq_s[:, at])
        turned = pltpu.roll(q.astype(BF).astype(F32) * 0.125, HDIM, 1)
        a0 = mm_t(jnp.where(low_half, 0.0, turned).astype(BF), qkv[:, tile_at(3 * t)])
        a1 = mm_t(jnp.where(low_half, turned, 0.0).astype(BF), qkv[:, tile_at(3 * t + 2)])
        both = pl.ds(pl.multiple_of(16 * t, 16), 16)
        for r_ in range(R):
            rows = slice(r_ * SEGS, (r_ + 1) * SEGS)
            qk[r_, both, :] = jnp.concatenate([a0[rows], a1[rows]], 0).astype(BF)
        return 0

    lax.fori_loop(0, PAIRS, absorb, 0, unroll=UNROLL)

    Q = HEADS * SEGS
    qj = lax.rem(iota((Q, 1), 0), SEGS)
    hsub = iota((HEADS, SEGS, LANES), 0)
    hlane = iota((HEADS, SEGS, LANES), 2)

    def to_lanes(col):
        return jnp.sum(jnp.where(hsub == hlane, col.reshape(HEADS, SEGS, 1), 0.0), 0)

    def to_col(f):
        wide = jnp.broadcast_to(f[None], (HEADS, SEGS, LANES))
        return jnp.sum(jnp.where(hsub == hlane, wide, 0.0), -1, keepdims=True).reshape(Q, 1)

    def rows_of(r):
        return x[r * S : (r + 1) * S, :]

    def score(r):
        expo[r][...] = mm_t(qk[r], rows_of(r))

    def soften(r):
        tops, sums = [], []
        for c in range(0, Q, PART):
            rows = slice(c, c + PART)
            mask = seg_eff[r : r + 1, :] == qj[rows]
            sc = jnp.where(mask, expo[r][rows, :], NEG)
            top = jnp.max(sc, -1, keepdims=True)
            e = jnp.where(mask, jnp.exp(sc - top), 0.0)
            expo[r][rows, :] = e
            low[r][rows, :] = e.astype(BF)
            tops.append(top)
            sums.append(jnp.sum(e, -1, keepdims=True))
        top, total = jnp.concatenate(tops, 0), jnp.concatenate(sums, 0)
        st[r] = to_lanes(top) + pltpu.roll(to_lanes(total), HDIM, 1)

    def mix(r):
        return mm(low[r][...], rows_of(r)).reshape(HEADS, SEGS, D)

    def staged(first_part, second_part, between):
        first_part(0)
        held = None
        for r in range(R):
            if r + 1 < R:
                first_part(r + 1)
            second_part(r)
            part = mix(r)
            if r % 2:
                ub[:, SEGS * (r - 1) : SEGS * (r + 1), :] = jnp.concatenate([held, part], 1).astype(BF)
            held = part
            between(r)

    staged(score, soften, lambda r: None)

    def row_of(d):
        return lax.rem(lax.rem(z + d, G), R)

    rs = [over("heads", d, st.at[row_of(d)], st_in.at[d], rs_s.at[0, d], rs_r.at[0, d]) for d in range(1, G)]
    for copy in rs:
        copy.start()

    NT = 256

    def cols(n):
        return pl.ds(pl.multiple_of(NT * n, NT), NT)

    def latents(n, _):
        ua[:, cols(n)] = mm(ub[...].reshape(HEADS * L, D), va[:, cols(n)])
        return 0

    lax.fori_loop(0, D // NT, latents, 0, unroll=D // NT)

    def two(t):
        return pl.ds(pl.multiple_of(2 * L * t, 2 * L), 2 * L)

    def values(t, _):
        at = tile_at(t)
        v0 = mm(ub[2 * t], qkv[:, tile_at(3 * t + 1)])
        v1 = mm(ub[2 * t + 1], qkv[:, tile_at(3 * t + 2)])
        pair = mm((ua[two(t), :] * scale_d[1:2, :]).astype(BF), vb[:, at])
        extra = jnp.where(low_half, pair[:L], pair[L:])
        ev[:, at] = extra
        mixed = jnp.where(low_half, v0, v1) + scale_b[1:2, at] * extra
        pack[:, :, at] = mixed.reshape(R, SEGS, LANES)
        return 0

    for half in range(2):
        lax.fori_loop(half * PAIRS // 2, (half + 1) * PAIRS // 2, values, 0, unroll=PAIRS // 2)
        left, quarter = half * D // 2, D // 4
        for r in range(R):
            parts = [pack[r, :, left : left + quarter], pack[r, :, left + quarter : left + 2 * quarter]]
            pk[r, half] = jnp.concatenate(parts, 0).astype(BF)
        leg = [
            over("heads", d, pk.at[row_of(d), half], pk_in.at[d, half], rs_s.at[1 + half, d], rs_r.at[1 + half, d])
            for d in range(1, G)
        ]
        for copy in leg:
            copy.start()
        rs = rs + leg

    def widen(halves):
        both = [halves[i].astype(F32) for i in range(2)]
        return jnp.concatenate([v for h in both for v in (h[:SEGS], h[SEGS:])], 1)

    for copy in cnt:
        copy.wait()
    total = cnt_out[...]
    for d in range(1, NR):
        total = total + cnt_in[d]
    count = jnp.sum(total, 0, keepdims=True)
    weights = jnp.zeros((1, LANES), F32)
    for t in range(TASKS):
        weights = jnp.where(task_lane == t, task_w[t].astype(F32), weights)
    coef = weights / jnp.maximum(count, 1.0)
    task = jnp.sum(jnp.where(eye, tasks[pl.ds(own_r, 1), :], 0), 1, keepdims=True)
    label = jnp.sum(jnp.where(eye, labels[pl.ds(own_r, 1), :], 0), 1, keepdims=True)
    picked = (task == task_lane) & (lane < TASKS * CLASSES)
    target = picked & (lane // TASKS == label)
    leads = (starts_s[own_r][:, 0:1] < fill[own_r]) & (z < R)
    weight = jnp.sum(jnp.where(target, coef, 0.0), -1, keepdims=True)
    weight = jnp.where(leads, weight, 0.0)
    tab[...] = jnp.concatenate([table[...], jnp.zeros((LANES - TASKS * CLASSES, D), F32)], 0).astype(BF)

    for copy in rs:
        copy.wait()
    got = [pack[own_r]] + [widen(pk_in[d]) for d in range(1, G)]
    stat = [st[own_r]] + [st_in[d] for d in range(1, G)]
    top = stat[0]
    for part in stat[1:]:
        top = jnp.maximum(top, part)
    shrink = [jnp.exp(part - top) for part in stat]
    tot = jnp.zeros((SEGS, LANES), F32)
    for part, s in zip(stat, shrink):
        tot = tot + pltpu.roll(part, HDIM, 1) * s
    tot = jnp.where(lane < HEADS, tot, 1.0)
    lse_out[...] = top + jnp.log(tot)
    mixed = jnp.zeros((SEGS, D), F32)
    for part, s in zip(got, shrink):
        mixed = mixed + expand(s / tot) * part
    mixed = mixed + biases[1:2, :]

    def guarded(cond, f):
        if cond is None:
            f()
        else:
            pl.when(cond)(f)

    mine = None if G == R else z < R

    def hand_out(k, src, dst):
        def start():
            for d in range(1, G):
                over("heads", d, src, dst.at[own_r], g_s.at[k, d], g_r.at[k, own_r]).start()

        def keep():
            dst[own_r] = src[...]

        guarded(mine, start)
        guarded(mine, keep)

    def take_in(k, src, dst):
        def one(r):
            pltpu.make_async_remote_copy(
                src_ref=src, dst_ref=dst.at[r], send_sem=g_s.at[k, 0], recv_sem=g_r.at[k, r],
                device_id={"heads": z}, device_id_type=MESH,
            ).wait_recv()

        for r in range(R):
            pl.when(z != r)(functools.partial(one, r))

    hand_out(0, lse_out, lse_in)

    loads[3].wait()
    r_one = xz_s[pl.ds(pl.multiple_of(own_r * SEGS, SEGS), SEGS), :] + mm(mixed.astype(BF), outw[...]) + biases[2:3, :]
    hat1, rstd1 = normed(r_one)
    x_one = hat1 * gains[1:2, :] + shifts[1:2, :]
    x_one_low = x_one.astype(BF)
    loads[4].wait()

    for n in range(FF // FT):
        at = slice(FT * n, FT * (n + 1))
        act[:, at] = mm(x_one_low, fin[:, at])
    h = act[...] + bias_in[...]
    half = 0.5 * (1.0 + lax.erf(h * 0.7071067811865476))
    act[...] = h * half
    slope[...] = half + h * (0.3989422804014327 * jnp.exp(-0.5 * h * h))
    loads[5].wait()
    act_low = act[...].astype(BF)

    def ffn_out_tile(n, _):
        fx[0:SEGS, cols(n)] = mm(act_low, fout[:, cols(n)])
        return 0

    lax.fori_loop(0, D // NT, ffn_out_tile, 0, unroll=D // NT)
    hat2, rstd2 = normed(x_one + fx[0:SEGS, :] + biases[3:4, :])
    x_two = (hat2 * gains[2:3, :] + shifts[2:3, :]).astype(BF)
    logits = mm_t(x_two, tab[...])
    chosen = jnp.where(picked, logits, NEG)
    peak = jnp.max(chosen, -1, keepdims=True)
    sums = jnp.sum(jnp.where(picked, jnp.exp(chosen - peak), 0.0), -1, keepdims=True)
    log_sum = peak + jnp.log(sums)
    hit = jnp.sum(jnp.where(target, logits, 0.0), -1, keepdims=True)
    loss = jnp.sum(weight * (log_sum - hit), 0, keepdims=True)
    soft = jnp.where(picked, jnp.exp(chosen - log_sum), 0.0) - target.astype(F32)
    g_logits = (weight * soft).astype(BF)
    hs[...] = mm(g_logits.astype(F32).T.astype(BF), x_two)[: CHUNKS * 8, :]
    hs[TASKS * CLASSES : TASKS * CLASSES + 8, :] = jnp.broadcast_to(loss, (8, D))
    g_two = mm(g_logits, tab[...])
    g_r2 = norm_back(hat2, rstd2, gains[2:3, :], g_two)
    g_f = g_r2.astype(BF)

    for n in range(FF // FT):
        at = slice(FT * n, FT * (n + 1))
        gh[:, at] = mm_t(g_f, fout[at, :]) * slope[:, at]
    gh_low = gh[...].astype(BF)

    def back_in(n, _):
        fx[0:SEGS, cols(n)] = mm_t(gh_low, fin[cols(n), :])
        return 0

    lax.fori_loop(0, D // NT, back_in, 0, unroll=D // NT)
    g_r1 = norm_back(hat1, rstd1, gains[1:2, :], g_r2 + fx[0:SEGS, :])
    g_mixed = mm_t(g_r1.astype(BF), outw[...]).astype(BF).astype(F32)
    quarters = [g_mixed[:, i * D // 4 : (i + 1) * D // 4] for i in range(4)]
    gpk[0] = jnp.concatenate(quarters[0:2], 0).astype(BF)
    gpk[1] = jnp.concatenate(quarters[2:4], 0).astype(BF)
    hand_out(1, gpk, gpk_in)
    dlt_out[...] = compress(g_mixed * mixed) - compress(g_mixed * biases[1:2, :])
    hand_out(2, dlt_out, dlt_in)

    def spread(src, dst, send, recv, limit, action):
        for d in range(1, G):
            copy = over("heads", d, src(lax.rem(z + d, G)), dst(d), send.at[d], recv(d))
            cond = limit(lax.rem(z + d, G))
            if cond is None:
                action(copy)
            else:
                pl.when(cond)(functools.partial(action, copy))

    def chunk_of(peer):
        return hs.at[pl.ds(pl.multiple_of(8 * lax.rem(peer, CHUNKS), 8), 8)]

    def small(peer):
        return None if G == CHUNKS else peer < CHUNKS

    holder = None if G == CHUNKS else z < CHUNKS
    take_in(0, lse_out, lse_in)
    take_in(1, gpk, gpk_in)
    for r in range(R):
        g_in[r] = widen(gpk_in[r])

    scale = [jnp.exp(st[r] - lse_in[r]) for r in range(R)]
    factor = jnp.concatenate([jnp.where(lane < HEADS, s, 0.0) for s in scale], 0)

    def back_value(t, acc):
        at = tile_at(t)
        g = g_in[:, :, at].reshape(L, LANES)
        z0 = mm_t(jnp.where(low_half, g, 0.0).astype(BF), qkv[:, tile_at(3 * t + 1)])
        z1 = mm_t(jnp.where(low_half, 0.0, g).astype(BF), qkv[:, tile_at(3 * t + 2)])
        zacc[two(t), :] = jnp.concatenate([z0, z1], 0)
        gb = g * scale_b[1:2, at]
        both = jnp.concatenate([jnp.where(low_half, gb, 0.0), jnp.where(low_half, 0.0, gb)], 0).astype(BF)
        back = mm_t(both, vb[:, at])
        f0 = jnp.sum(jnp.where(lane == 2 * t, factor, 0.0), -1, keepdims=True)
        f1 = jnp.sum(jnp.where(lane == 2 * t + 1, factor, 0.0), -1, keepdims=True)
        acc = acc + jnp.sum(jnp.concatenate([f0, f1], 0) * ua[two(t), :] * back, 0, keepdims=True)
        zb[two(t), :] = (back * scale_d[1:2, :]).astype(BF)
        return acc

    grad_d1 = lax.fori_loop(0, PAIRS, back_value, jnp.zeros((1, D), F32), unroll=UNROLL)
    grad_b1 = jnp.sum(g_in[...].reshape(L, D) * ev[...] * expand(factor), 0, keepdims=True)
    extra = TASKS * CLASSES + 1
    hs[extra : extra + 2, :] = jnp.concatenate([grad_d1, grad_b1], 0)
    spread(chunk_of, lambda d: h_in.at[d], h_ss, lambda d: h_rs.at[d], small, lambda c: c.start())

    def back_latent(n, _):
        at = cols(n)
        part = (zacc[:, at] + mm_t(zb[...], va[at, :])).reshape(HEADS, R, SEGS, NT)
        for r in range(R):
            zq[r, :, at] = part[:, r].reshape(Q, NT).astype(BF)
        return 0

    lax.fori_loop(0, D // NT, back_latent, 0, unroll=D // NT)

    def relay():
        acc = chunk_of(z)[...]
        for d in range(1, G):
            over("heads", d, chunk_of(z), h_in.at[d], h_ss.at[d], h_rs.at[d]).wait_recv()
            acc = acc + h_in[d]
        hr[...] = acc
        for d in range(1, NR):
            over("rows", d, hr, hr_in.at[d], hr_ss.at[d], hr_rs.at[d]).start()

    def slope_of(r):
        gdot[r % 2][...] = mm_t(zq[r], rows_of(r))

    def bend(r):
        f = to_col(jnp.where(lane < HEADS, jnp.exp(st[r] - lse_in[r]), 0.0))
        delta = to_col(dlt_in[r])
        for c in range(0, Q, PART):
            rows = slice(c, c + PART)
            ds = (expo[r][rows, :] * f[rows]) * (gdot[r % 2][rows, :] - delta[rows])
            low[r][rows, :] = ds.astype(BF)

    take_in(2, dlt_out, dlt_in)
    staged(slope_of, bend, lambda r: guarded(holder, relay) if r == R // 2 - 1 else None)

    def relay_two():
        acc = hr[...]
        for d in range(1, NR):
            over("rows", d, hr, hr_in.at[d], hr_ss.at[d], hr_rs.at[d]).wait()
            acc = acc + hr_in[d]
        ag[lax.rem(z, CHUNKS)] = acc
        for d in range(1, G):
            c = lax.rem(z, CHUNKS)
            over("heads", d, ag.at[c], ag.at[c], ag_ss.at[d], ag_rs.at[c]).start()

    def back_query(t, _):
        at = tile_at(t)
        k0 = mm(ub[2 * t], qkv[:, tile_at(3 * t)])
        k1 = mm(ub[2 * t + 1], qkv[:, tile_at(3 * t + 2)])
        gq_s[:, at] = pltpu.roll(jnp.where(low_half, k1, k0), HDIM, 1) * 0.125
        return 0

    lax.fori_loop(0, PAIRS, back_query, 0, unroll=UNROLL)
    g_query = gq_s[...]
    grad_b0 = jnp.sum(g_query * eq_s[...], 0, keepdims=True)
    back = mm_t((g_query * scale_b[0:1, :]).astype(BF), vb[...])
    grad_d0 = jnp.sum(latent_s[...] * back, 0, keepdims=True)
    two_rows = jnp.concatenate([grad_d0, grad_b0], 0)
    late[...] = jnp.concatenate([two_rows[:, i * D // 4 : (i + 1) * D // 4] for i in range(4)], 0)
    leg = [over("heads", d, late, lz_in.at[d], lz_ss.at[d], lz_rs.at[d]) for d in range(1, G)]
    for copy in leg:
        copy.start()
    guarded(holder, relay_two)
    for copy in leg:
        copy.wait()
    acc = late[...]
    for d in range(1, G):
        acc = acc + lz_in[d]
    lr[...] = acc
    leg = [over("rows", d, lr, lr_in.at[d], lr_ss.at[d], lr_rs.at[d]) for d in range(1, NR)]
    for copy in leg:
        copy.start()

    for c in range(CHUNKS):
        def arrive(c=c):
            pltpu.make_async_remote_copy(
                src_ref=ag.at[c], dst_ref=ag.at[c], send_sem=ag_ss.at[0], recv_sem=ag_rs.at[c],
                device_id={"heads": z}, device_id_type=MESH,
            ).wait_recv()

        pl.when(z != c)(arrive)
    heads_sum[...] = ag[...].reshape(CHUNKS * 8, D)
    def handed():
        for k, (src, dst) in enumerate(((lse_out, lse_in), (gpk, gpk_in), (dlt_out, dlt_in))):
            for d in range(1, G):
                over("heads", d, src, dst.at[own_r], g_s.at[k, d], g_r.at[k, own_r]).wait_send()

    guarded(mine, handed)
    spread(chunk_of, lambda d: h_in.at[d], h_ss, lambda d: h_rs.at[d], small, lambda c: c.wait_send())

    def sent():
        for d in range(1, G):
            c = lax.rem(z, CHUNKS)
            over("heads", d, ag.at[c], ag.at[c], ag_ss.at[d], ag_rs.at[c]).wait_send()

    guarded(holder, sent)
    for copy in leg:
        copy.wait()
    acc = lr[...]
    for d in range(1, NR):
        acc = acc + lr_in[d]
    small_sum[...] = acc


def update_kernel(
    heads_sum, small_sum, scale_d, scale_b, table, mom_d, mom_b, mom_h, avg_d, avg_b, avg_h,
    loss, m_d, m_b, m_h, w_d, w_b, w_h, a_d, a_b, a_h, low, stats,
):
    count = table.shape[0]
    pairs = jnp.concatenate([small_sum[2 * i : 2 * i + 2, :] for i in range(4)], 1)
    more = heads_sum[count + 1 : count + 3, :]
    grad_d = jnp.concatenate([pairs[0:1], more[0:1]], 0)
    grad_b = jnp.concatenate([pairs[1:2], more[1:2]], 0)
    m_d[...], new_d, a_d[...] = update(scale_d[...], grad_d, mom_d[...], avg_d[...], RATE_D)
    m_b[...], new_b, a_b[...] = update(scale_b[...], grad_b, mom_b[...], avg_b[...], RATE_B)
    m_h[...], new_h, a_h[...] = update(table[...], heads_sum[:count, :], mom_h[...], avg_h[...], RATE_HEADS)
    w_d[...], w_b[...], w_h[...], low[...] = new_d, new_b, new_h, new_h.astype(BF)
    loss[...] = heads_sum[count : count + 1, 0:1]
    rms = [jnp.sqrt(jnp.mean(jnp.mean(v * v, 1, keepdims=True), 0, keepdims=True)) for v in (new_d, new_b)]
    stats[...] = jnp.concatenate(rms, 1)


def on_device(
    sizes,
    token_ids, segment_ids, row_fill, task_ids, labels, task_weights,
    word_table, position_table, norm_gains, norm_biases, dense_biases,
    qkv_weight, out_weight, ffn_in, ffn_bias, ffn_out, vera_a, vera_b,
    scale_d, scale_b, task_heads, mom_d, mom_b, mom_heads, avg_d, avg_b, avg_heads,
):
    G, NR = sizes
    R, S = token_ids.shape
    V, D = word_table.shape
    FF = ffn_in.shape[1]
    L, Q, T = R * SEGS, HEADS * SEGS, R * S
    raw, leads = gather(token_ids, segment_ids, row_fill, word_table)

    def flat(value):
        return value.transpose(1, 0, 2).reshape(CLASSES * TASKS, D)

    table, mom_h, avg_h = flat(task_heads), flat(mom_heads), flat(avg_heads)
    v = pltpu.VMEM
    dma = pltpu.SemaphoreType.DMA
    scratch = [
        v((T, D), BF), v(qkv_weight.shape, BF), v(out_weight.shape, BF), v(ffn_in.shape, BF), v(ffn_out.shape, BF),
        v(vera_a.shape, BF), v(vera_b.shape, BF),
        v(position_table.shape, BF), v((position_table.shape[0] - 2, D), BF), v((G, L, D), BF), v((R, S), jnp.int32), v((R, SEGS, LANES), jnp.int32), v((L, D), F32),
        v((L, D), F32), v((L, D), F32), v((R, Q, D), BF), v((HEADS, L, D), BF),
        v((HEADS * L, D), F32), v((L, D), F32), v((R, SEGS, D), F32), v((R, SEGS, LANES), F32), v((G, SEGS, LANES), F32),
        v((R, 2, 2 * SEGS, D // 4), BF), v((G, 2, 2 * SEGS, D // 4), BF),
        v((SEGS, FF), F32), v((SEGS, FF), F32), v((SEGS, FF), F32), v((LANES, D), BF), v((SEGS, LANES), F32), v((R, SEGS, LANES), F32),
        v((2, 2 * SEGS, D // 4), BF), v((R, 2, 2 * SEGS, D // 4), BF), v((SEGS, LANES), F32), v((R, SEGS, LANES), F32),
        v((R, SEGS, D), F32), v((R, Q, D), BF), v((HEADS * L, D), F32), v((HEADS * L, D), BF), v((L, D), F32),
        v((L, D), F32),
        v((SEGS, LANES), F32), v((NR, SEGS, LANES), F32), v((CHUNKS * 8, D), F32), v((G, 8, D), F32), v((8, D), F32),
        v((NR, 8, D), F32), v((CHUNKS, 8, D), F32), v((8, D // 4), F32), v((G, 8, D // 4), F32), v((8, D // 4), F32),
        v((NR, 8, D // 4), F32),
        dma((7,)), dma((2,)), dma((G,)), dma((G,)), dma((NR,)), dma((NR,)), dma((3, G)), dma((3, G)),
        dma((3, G)), dma((3, R)), dma((G,)), dma((G,)), dma((NR,)), dma((NR,)), dma((G,)), dma((CHUNKS,)),
        dma((G,)), dma((G,)), dma((NR,)), dma((NR,)), *[v((Q, S), F32)] * (R + 2), *[v((Q, S), BF)] * R,
        v((S, D), BF), v((S, D), BF),
    ]
    vm, hbm, sm = (pl.BlockSpec(memory_space=m) for m in (pltpu.VMEM, pl.ANY, pltpu.SMEM))
    heads_sum, small_sum = pl.pallas_call(
        functools.partial(step_kernel, (R, S, G, NR, V)),
        out_shape=(jax.ShapeDtypeStruct((CHUNKS * 8, D), F32), jax.ShapeDtypeStruct((8, D // 4), F32)),
        in_specs=[sm, sm] + [vm] * 12 + [hbm] * 8,
        out_specs=(vm, vm),
        scratch_shapes=scratch,
        compiler_params=pltpu.CompilerParams(
            collective_id=0, has_side_effects=True, vmem_limit_bytes=60 * 1024 * 1024
        ),
    )(
        row_fill, task_weights, token_ids, segment_ids, task_ids, labels, leads, norm_gains, norm_biases,
        dense_biases, ffn_bias.reshape(1, -1), scale_d, scale_b, table,
        raw, position_table, qkv_weight, out_weight, ffn_in, ffn_out, vera_a, vera_b,
    )
    like = jax.ShapeDtypeStruct
    two, many = like((2, D), F32), like((CLASSES * TASKS, D), F32)
    loss, m_d, m_b, m_h, w_d, w_b, w_h, a_d, a_b, a_h, low, stats = pl.pallas_call(
        update_kernel,
        out_shape=(
            like((1, 1), F32), two, two, many, two, two, many, two, two, many, like((CLASSES * TASKS, D), BF), like((1, 2), F32),
        ),
        in_specs=[vm] * 11,
        out_specs=(vm,) * 12,
    )(heads_sum, small_sum, scale_d, scale_b, table, mom_d, mom_b, mom_h, avg_d, avg_b, avg_h)

    def unflat(value):
        return value.reshape(CLASSES, TASKS, D).transpose(1, 0, 2)

    return (
        loss.reshape(()), m_d, m_b, unflat(m_h), w_d, w_b, unflat(w_h), a_d, a_b, unflat(a_h), unflat(low), stats.reshape(2),
    )


def solution(mesh):
    sizes = (mesh.shape["heads"], mesh.shape["rows"])
    by_row = P("rows", None)
    return jax.shard_map(
        functools.partial(on_device, sizes),
        mesh=mesh,
        in_specs=(by_row, by_row, P("rows"), by_row, by_row, P(), P("heads", None)) + (P(),) * 20,
        out_specs=(P(),) * 12,
        check_vma=False,
    )
```

```python
import functools

import jax
import jax.numpy as jnp
from jax import lax
from jax.experimental import pallas as pl
from jax.experimental.pallas import tpu as pltpu
from jax.sharding import PartitionSpec as P

HEADS = 16
HDIM = 64
TASKS = 8
CLASSES = 3
SEGS = 8
LANES = 128
CHUNKS = 4
BLK = 256
GROUP = 128
SUB = 2
FT = 1024
UNROLL = 8
PART = 32
EPSILON = 1e-05
MOMENTUM = 0.9
AVERAGE = 0.8
RATE_D = 5.0
RATE_B = 20.0
RATE_HEADS = 0.3
NEG = -1e30
BF = jnp.bfloat16
F32 = jnp.float32
MESH = pl.DeviceIdType.MESH


def mm(left, right):
    return jnp.dot(left, right, preferred_element_type=F32)


def mm_t(left, right):
    return lax.dot_general(left, right, (((1,), (1,)), ((), ())), preferred_element_type=F32)


def mm_l(left, right):
    return lax.dot_general(left, right, (((0,), (0,)), ((), ())), preferred_element_type=F32)


def normed(values):
    centred = values - jnp.mean(values, -1, keepdims=True)
    rstd = lax.rsqrt(jnp.mean(centred * centred, -1, keepdims=True) + EPSILON)
    return centred * rstd, rstd


def norm_back(hat, rstd, gain, grad):
    scaled = grad * gain
    return rstd * (
        scaled
        - jnp.mean(scaled, -1, keepdims=True)
        - hat * jnp.mean(scaled * hat, -1, keepdims=True)
    )


def iota(shape, dim):
    return lax.broadcasted_iota(jnp.int32, shape, dim)


def update(weight, grad, moment, average, rate):
    moment_new = MOMENTUM * moment + grad
    weight_new = weight - rate * (grad + MOMENTUM * moment_new)
    return (moment_new, weight_new, AVERAGE * average + (1.0 - AVERAGE) * weight_new)


def gather_kernel(
    cfg, fill, ids, seg, words, x_out, lead_out,
    listv, lists, keyc, lead, bufs, stages, list_sem, buf_sem, out_sem,
):
    R, S, V = cfg
    D = x_out.shape[1]
    PER = S // BLK
    NB = R * PER
    HALVES = BLK // LANES
    STAGES = stages.shape[0]
    z = lax.axis_index("heads")
    slot = iota((1, S), 1)
    lane = iota((1, LANES), 1)
    jcol = iota((SEGS, 1), 0)
    row8 = iota((8, 1), 0)

    local = ids[...] - z * V
    segs = seg[...]
    fills = jnp.zeros((R, 1), jnp.int32)
    for r in range(R):
        fills = jnp.where(iota((R, 1), 0) == r, fill[r], fills)
    first = (slot == 0) | (segs != pltpu.roll(segs, 1, 1))
    need = (local >= 0) & (local < V) & (first | (slot < fills))
    upper = (iota((LANES, LANES), 0) <= iota((LANES, LANES), 1)).astype(F32).astype(BF)
    ahead = iota((BLK, BLK), 0) < iota((BLK, BLK), 1)

    def by_block(value):
        return jnp.concatenate([value[:, BLK * p : BLK * (p + 1)] for p in range(PER)], 0)

    pair = by_block(jnp.where(need, local // SUB, -1).astype(F32))
    half = by_block((local & (SUB - 1)).astype(F32))
    wanted = pair >= 0.0
    pair_col = pair.T
    same = [pair_col[:, q : q + 1] == pair[q : q + 1] for q in range(NB)]
    seen = [jnp.max(jnp.where(same[q] & ahead, 1.0, 0.0), 0, keepdims=True) for q in range(NB)]
    lead_one = jnp.where(wanted, 1.0 - jnp.concatenate(seen, 0), 0.0)
    halves = [lead_one[:, LANES * h : LANES * (h + 1)] for h in range(HALVES)]
    prefix = mm(jnp.concatenate(halves, 0).astype(BF), upper)
    runs, total = [], jnp.zeros((NB, 1), F32)
    for h in range(HALVES):
        run = prefix[NB * h : NB * (h + 1)]
        runs.append(run + total)
        total = total + run[:, LANES - 1 :]
    rank = jnp.where(lead_one > 0.0, jnp.concatenate(runs, 1) - 1.0, -1.0)
    held = jnp.maximum(rank, 0.0)
    count_row = jnp.zeros((1, LANES), F32)
    keys = []
    for q in range(NB):
        share = mm(jnp.broadcast_to(held[q : q + 1], (8, BLK)).astype(BF), same[q].astype(F32).astype(BF))
        keys.append(share[0:1])
    key = jnp.where(wanted, SUB * jnp.concatenate(keys, 0) + half, -1.0)
    key_col = key.T
    for r in range(R):
        starts = jnp.sum((segs[r : r + 1, :] < jcol).astype(jnp.int32), 1, keepdims=True)
        for p in range(PER):
            b, q = r * PER + p, p * R + r
            at_start = iota((1, BLK), 1) + BLK * p == starts
            lead_key = jnp.sum(jnp.where(at_start, key[q : q + 1] + 8.0, 0.0), 1, keepdims=True) - 8.0
            keyc[b] = jnp.concatenate([key_col[:, q : q + 1], lead_key, jnp.full((8, 1), -5.0, F32)], 0)
            order = rank[q : q + 1].astype(jnp.int32)
            spots = (iota((LANES, 1), 0) == jnp.where(order < 0, -1, order & (LANES - 1))).astype(F32).astype(BF)
            row_at = SUB * pair[q : q + 1].astype(jnp.int32)
            plane = jnp.where(row8 < HALVES, row_at & 255, row_at // 256)
            plane = jnp.where(((order // LANES) == (row8 & (HALVES - 1))) & (row8 < 2 * HALVES), plane, 0)
            both = mm_t(plane.astype(F32).astype(BF), spots)
            both = both[0:HALVES] + 256.0 * both[HALVES : 2 * HALVES]
            listv[HALVES * b : HALVES * (b + 1), :] = both.astype(jnp.int32)
            count_row = jnp.where(lane == b, total[q : q + 1], count_row)
    listv[HALVES * NB :, :] = jnp.broadcast_to(count_row.astype(jnp.int32), (8, LANES))
    to_scalar = pltpu.make_async_copy(listv, lists, list_sem.at[0])
    to_scalar.start()
    lead[...] = jnp.zeros_like(lead)
    for b in range(NB):
        bufs[b, 0 : GROUP * SUB // 8] = jnp.zeros((GROUP * SUB // 8, 8, D), BF)
    to_scalar.wait()

    def eights(b):
        n = lists[HALVES * NB, b]
        return jnp.where(n <= GROUP, (n + 7) // 8, (n + GROUP - 1) // GROUP * (GROUP // 8))

    def issue(r):
        for p in range(PER):
            b = r * PER + p

            def eight(i, _, b=b, h=0):
                for u in range(8):
                    word = lists[HALVES * b + h, i * 8 + u]
                    pltpu.make_async_copy(
                        words.at[pl.ds(pl.multiple_of(word, SUB), SUB)],
                        bufs.at[b, h * GROUP * SUB // 8 + i * SUB + u * SUB // 8, pl.ds(u * SUB % 8, SUB)],
                        buf_sem.at[r],
                    ).start()
                return 0

            lax.fori_loop(0, jnp.minimum(eights(b), GROUP // 8), eight, 0)

            @pl.when(lists[HALVES * NB, b] > GROUP)
            def more(eight=eight):
                lax.fori_loop(0, GROUP // 8, functools.partial(eight, h=1), 0)

    def arrive(r):
        total = eights(r * PER)
        for p in range(1, PER):
            total = total + eights(r * PER + p)
        part = bufs.at[0, pl.ds(0, SUB)]

        def eight(i, _):
            pltpu.make_async_copy(part, part, buf_sem.at[r]).wait()
            return 0

        lax.fori_loop(0, total, eight, 0)

    lanes = iota((1, GROUP * SUB), 1).astype(F32)

    def pick(b, g):
        one = (keyc[b] == lanes + float(g * GROUP * SUB)).astype(F32).astype(BF)
        rows = bufs[b, g * GROUP * SUB // 8 : (g + 1) * GROUP * SUB // 8]
        return mm(one, rows.reshape(GROUP * SUB, D))

    def add_lead(b, got):
        rows = pl.ds(pl.multiple_of(b // PER * SEGS, SEGS), SEGS)
        lead[rows, :] = lead[rows, :] + got

    def out_copy(b):
        k = lax.rem(b, STAGES)
        rows = pl.ds(pl.multiple_of(b * BLK, BLK), BLK)
        return pltpu.make_async_copy(stages.at[k], x_out.at[rows], out_sem.at[k])

    for r in range(R):
        issue(r)

    def row(r, _):
        arrive(r)

        def block(p, _):
            b = r * PER + p
            k = lax.rem(b, STAGES)
            pl.when(b >= STAGES)(lambda: out_copy(b - STAGES).wait())
            got = pick(b, 0)
            stages[k] = got[:BLK].astype(BF)
            add_lead(b, got[BLK : BLK + SEGS])

            @pl.when(lists[HALVES * NB, b] > GROUP)
            def more():
                got = pick(b, 1)
                stages[k] = stages[k] + got[:BLK].astype(BF)
                add_lead(b, got[BLK : BLK + SEGS])

            out_copy(b).start()
            return 0

        return lax.fori_loop(0, PER, block, 0)

    lax.fori_loop(0, R, row, 0)
    lead_out[...] = lead[...].astype(BF)
    for k in range(STAGES):
        out_copy(NB - STAGES + k).wait()


def gather(token_ids, segment_ids, row_fill, word_table):
    R, S = token_ids.shape
    V, D = word_table.shape
    PER = S // BLK
    NB = R * PER
    HALVES = BLK // LANES
    if V % SUB:
        word_table = jnp.pad(word_table, ((0, -V % SUB), (0, 0)))
    v, dma = pltpu.VMEM, pltpu.SemaphoreType.DMA
    vm, hbm, sm = (pl.BlockSpec(memory_space=m) for m in (pltpu.VMEM, pl.ANY, pltpu.SMEM))
    return pl.pallas_call(
        functools.partial(gather_kernel, (R, S, V)),
        out_shape=(jax.ShapeDtypeStruct((R * S, D), BF), jax.ShapeDtypeStruct((R * SEGS, D), BF)),
        in_specs=[sm, vm, vm, hbm],
        out_specs=(hbm, vm),
        scratch_shapes=[
            v((HALVES * NB + 8, LANES), jnp.int32),
            pltpu.SMEM((HALVES * NB + 8, LANES), jnp.int32), v((NB, BLK + 2 * SEGS, 1), F32),
            v((R * SEGS, D), F32),
            v((NB, BLK * SUB // 8, 8, D), BF), v((4, BLK, D), BF), dma((1,)), dma((R,)), dma((4,)),
        ],
        compiler_params=pltpu.CompilerParams(vmem_limit_bytes=60 * 1024 * 1024),
    )(row_fill, token_ids, segment_ids, word_table)


def step_kernel(
    cfg,
    fill, task_w, ids, seg, tasks, labels, lead_out, gains, shifts, biases, bias_in, scale_d, scale_b, table,
    x_h, place_h, qkv_h, out_h, fin_h, fout_h, va_h, vb_h,
    heads_sum, small_sum,
    x, qkv, outw, fin, fout, va, vb,
    place, places, lead_in, seg_eff, starts_s, xz_s, latent_s, eq_s, qk, ub, ua, ev, pack, st, st_in, pk, pk_in,
    act, slope, gh, tab, lse_out, lse_in, gpk, gpk_in, dlt_out, dlt_in, g_in, zq, zacc, zb, gq_s, fx,
    cnt_out, cnt_in, hs, h_in, hr, hr_in, ag, late, lz_in, lr, lr_in,
    load_sem, x_sem, e1_s, e1_r, cnt_ss, cnt_rs, rs_s, rs_r, g_s, g_r, h_ss, h_rs, hr_ss, hr_rs, ag_ss, ag_rs,
    lz_ss, lz_rs, lr_ss, lr_rs, *wide,
):
    R, S, G, NR, V = cfg
    expo, gdot, low, words = wide[:R], wide[R : R + 2], wide[R + 2 : 2 * R + 2], wide[2 * R + 2 :]
    D = x.shape[1]
    FF = fin.shape[1]
    PAIRS = HEADS // 2
    L = R * SEGS
    z = lax.axis_index("heads")
    rw = lax.axis_index("rows")
    own_r = lax.rem(z, R)

    def x_load(r, h):
        return pltpu.make_async_copy(x_h.at[pl.ds(pl.multiple_of(r * S, S), S)], words[h], x_sem.at[h])

    loads = [
        pltpu.make_async_copy(src, dst, load_sem.at[i])
        for i, (src, dst) in enumerate(
            (
                (va_h, va), (vb_h, vb), (qkv_h, qkv), (out_h, outw), (fin_h, fin), (fout_h, fout),
                (place_h, place),
            )
        )
    ]
    for copy in [x_load(0, 0), loads[6], x_load(1, 1)]:
        copy.start()

    barrier = pltpu.get_barrier_semaphore()
    for d in range(1, G):
        pl.semaphore_signal(barrier, inc=1, device_id={"heads": lax.rem(z + d, G)}, device_id_type=MESH)
    for d in range(1, NR):
        pl.semaphore_signal(barrier, inc=1, device_id={"rows": lax.rem(rw + d, NR)}, device_id_type=MESH)
    pl.semaphore_wait(barrier, G - 1 + NR - 1)

    def over(axis, d, src, dst, send, recv):
        me, size = (z, G) if axis == "heads" else (rw, NR)
        return pltpu.make_async_remote_copy(
            src_ref=src, dst_ref=dst, send_sem=send, recv_sem=recv,
            device_id={axis: lax.rem(me + d, size)}, device_id_type=MESH,
        )

    lane = iota((1, LANES), 1)
    low_half = lane < HDIM
    jcol = iota((SEGS, 1), 0)
    slot = iota((1, S), 1)

    def expand(f):
        tiles = [jnp.where(low_half, f[:, 2 * t : 2 * t + 1], f[:, 2 * t + 1 : 2 * t + 2]) for t in range(PAIRS)]
        return jnp.concatenate(tiles, 1)

    def compress(v):
        out = jnp.zeros((v.shape[0], LANES), F32)
        for t in range(PAIRS):
            tile = v[:, LANES * t : LANES * (t + 1)]
            a = jnp.sum(jnp.where(low_half, tile, 0.0), -1, keepdims=True)
            b = jnp.sum(jnp.where(low_half, 0.0, tile), -1, keepdims=True)
            out = jnp.where(lane == 2 * t, a, jnp.where(lane == 2 * t + 1, b, out))
        return out

    e1 = [over("heads", d, lead_out, lead_in.at[d], e1_s.at[d], e1_r.at[d]) for d in range(1, G)]
    for copy in e1:
        copy.start()

    eye = iota((SEGS, SEGS), 0) == iota((SEGS, SEGS), 1)
    task_lane = lane & (TASKS - 1)
    counts = jnp.zeros((SEGS, LANES), F32)
    for r in range(R):
        seg_row = seg[r : r + 1, :]
        local = ids[r : r + 1, :] - z * V
        own = (local >= 0) & (local < V)
        first = (slot == 0) | (seg_row != pltpu.roll(seg_row, 1, 1))
        seg_eff[r : r + 1, :] = jnp.where(own & (first | (slot < fill[r])), seg_row, -1)
        starts = jnp.sum((seg_row < jcol).astype(jnp.int32), 1, keepdims=True)
        starts_s[r] = jnp.broadcast_to(starts, (SEGS, LANES))
        lead = (starts < fill[r]).astype(F32)
        task = jnp.sum(jnp.where(eye, tasks[r : r + 1, :], 0), 1, keepdims=True)
        counts = counts + jnp.where((task == task_lane) & (lane < TASKS * CLASSES), lead, 0.0)
    cnt_out[...] = counts
    cnt = [over("rows", d, cnt_out, cnt_in.at[d], cnt_ss.at[d], cnt_rs.at[d]) for d in range(1, NR)]
    for copy in cnt:
        copy.start()
    gain0, shift0 = gains[0:1, :], shifts[0:1, :]
    loads[6].wait()
    places[...] = place[2:, :]
    prow = iota((places.shape[0], 1), 0)

    STEP = expo[0].shape[0]
    blocks = S // STEP

    def norm_row(r, h):
        seg_row = seg[pl.ds(r, 1), :]
        begin = jnp.sum(jnp.where(seg_row == jcol, starts_s[r][:, 0:1], 0), 0, keepdims=True)
        offset = slot - begin
        x_load(r, h).wait()

        def place_rows(b):
            one = (prow == offset[:, b * STEP : (b + 1) * STEP]).astype(F32).astype(BF)
            expo[b % R][...] = mm_l(one, places[...])

        place_rows(0)
        for b in range(blocks):
            if b + 1 < blocks:
                place_rows(b + 1)
            for c in range(0, STEP, PART):
                at = b * STEP + c
                hat, _ = normed(expo[b % R][c : c + PART, :] + words[h][at : at + PART, :].astype(F32))
                x[pl.ds(pl.multiple_of(r * S + at, PART), PART), :] = (hat * gain0 + shift0).astype(BF)

    def norm_two(i, _):
        for h in range(2):
            norm_row(2 * i + h, h)
            pl.when(i + 1 < R // 2)(lambda h=h: x_load(2 * i + 2 + h, h).start())
        return 0

    loads[0].start()
    loads[1].start()
    loads[2].start()
    lax.fori_loop(0, R // 2, norm_two, 0)

    for copy in e1:
        copy.wait()
    word = lead_out[...].astype(F32)
    for d in range(1, G):
        word = word + lead_in[d].astype(F32)
    hat, _ = normed(word + places[0:1, :].astype(F32))
    xz = hat * gain0 + shift0
    xz_s[...] = xz
    xl = xz.astype(BF)
    loads[0].wait()
    latent = mm(xl, va[...])
    latent_s[...] = latent
    loads[1].wait()
    eq_s[...] = mm((latent * scale_d[0:1, :]).astype(BF), vb[...])
    loads[2].wait()
    for copy in loads[3:6]:
        copy.start()

    def tile_at(t):
        return pl.ds(pl.multiple_of(LANES * t, LANES), LANES)

    def absorb(t, _):
        r = mm(xl, qkv[:, pl.ds(pl.multiple_of(384 * t, LANES), 256)])
        at = tile_at(t)
        q = jnp.where(low_half, r[:, :LANES], r[:, LANES:]) + (biases[0:1, at] + scale_b[0:1, at] * eq_s[:, at])
        turned = pltpu.roll(q.astype(BF).astype(F32) * 0.125, HDIM, 1)
        a0 = mm_t(jnp.where(low_half, 0.0, turned).astype(BF), qkv[:, tile_at(3 * t)])
        a1 = mm_t(jnp.where(low_half, turned, 0.0).astype(BF), qkv[:, tile_at(3 * t + 2)])
        both = pl.ds(pl.multiple_of(16 * t, 16), 16)
        for r_ in range(R):
            rows = slice(r_ * SEGS, (r_ + 1) * SEGS)
            qk[r_, both, :] = jnp.concatenate([a0[rows], a1[rows]], 0).astype(BF)
        return 0

    lax.fori_loop(0, PAIRS, absorb, 0, unroll=UNROLL)

    Q = HEADS * SEGS
    qj = lax.rem(iota((Q, 1), 0), SEGS)
    hsub = iota((HEADS, SEGS, LANES), 0)
    hlane = iota((HEADS, SEGS, LANES), 2)

    def to_lanes(col):
        return jnp.sum(jnp.where(hsub == hlane, col.reshape(HEADS, SEGS, 1), 0.0), 0)

    def to_col(f):
        wide = jnp.broadcast_to(f[None], (HEADS, SEGS, LANES))
        return jnp.sum(jnp.where(hsub == hlane, wide, 0.0), -1, keepdims=True).reshape(Q, 1)

    def rows_of(r):
        return x[r * S : (r + 1) * S, :]

    def score(r):
        expo[r][...] = mm_t(qk[r], rows_of(r))

    def soften(r):
        tops, sums = [], []
        for c in range(0, Q, PART):
            rows = slice(c, c + PART)
            mask = seg_eff[r : r + 1, :] == qj[rows]
            sc = jnp.where(mask, expo[r][rows, :], NEG)
            top = jnp.max(sc, -1, keepdims=True)
            e = jnp.where(mask, jnp.exp(sc - top), 0.0)
            expo[r][rows, :] = e
            low[r][rows, :] = e.astype(BF)
            tops.append(top)
            sums.append(jnp.sum(e, -1, keepdims=True))
        top, total = jnp.concatenate(tops, 0), jnp.concatenate(sums, 0)
        st[r] = to_lanes(top) + pltpu.roll(to_lanes(total), HDIM, 1)

    def mix(r):
        return mm(low[r][...], rows_of(r)).reshape(HEADS, SEGS, D)

    def staged(first_part, second_part, between):
        first_part(0)
        held = None
        for r in range(R):
            if r + 1 < R:
                first_part(r + 1)
            second_part(r)
            part = mix(r)
            if r % 2:
                ub[:, SEGS * (r - 1) : SEGS * (r + 1), :] = jnp.concatenate([held, part], 1).astype(BF)
            held = part
            between(r)

    staged(score, soften, lambda r: None)

    def row_of(d):
        return lax.rem(lax.rem(z + d, G), R)

    rs = [over("heads", d, st.at[row_of(d)], st_in.at[d], rs_s.at[0, d], rs_r.at[0, d]) for d in range(1, G)]
    for copy in rs:
        copy.start()

    NT = 256

    def cols(n):
        return pl.ds(pl.multiple_of(NT * n, NT), NT)

    def latents(n, _):
        ua[:, cols(n)] = mm(ub[...].reshape(HEADS * L, D), va[:, cols(n)])
        return 0

    lax.fori_loop(0, D // NT, latents, 0, unroll=D // NT)

    def two(t):
        return pl.ds(pl.multiple_of(2 * L * t, 2 * L), 2 * L)

    def values(t, _):
        at = tile_at(t)
        v0 = mm(ub[2 * t], qkv[:, tile_at(3 * t + 1)])
        v1 = mm(ub[2 * t + 1], qkv[:, tile_at(3 * t + 2)])
        pair = mm((ua[two(t), :] * scale_d[1:2, :]).astype(BF), vb[:, at])
        extra = jnp.where(low_half, pair[:L], pair[L:])
        ev[:, at] = extra
        mixed = jnp.where(low_half, v0, v1) + scale_b[1:2, at] * extra
        pack[:, :, at] = mixed.reshape(R, SEGS, LANES)
        return 0

    for half in range(2):
        lax.fori_loop(half * PAIRS // 2, (half + 1) * PAIRS // 2, values, 0, unroll=PAIRS // 2)
        left, quarter = half * D // 2, D // 4
        for r in range(R):
            parts = [pack[r, :, left : left + quarter], pack[r, :, left + quarter : left + 2 * quarter]]
            pk[r, half] = jnp.concatenate(parts, 0).astype(BF)
        leg = [
            over("heads", d, pk.at[row_of(d), half], pk_in.at[d, half], rs_s.at[1 + half, d], rs_r.at[1 + half, d])
            for d in range(1, G)
        ]
        for copy in leg:
            copy.start()
        rs = rs + leg

    def widen(halves):
        both = [halves[i].astype(F32) for i in range(2)]
        return jnp.concatenate([v for h in both for v in (h[:SEGS], h[SEGS:])], 1)

    for copy in cnt:
        copy.wait()
    total = cnt_out[...]
    for d in range(1, NR):
        total = total + cnt_in[d]
    count = jnp.sum(total, 0, keepdims=True)
    weights = jnp.zeros((1, LANES), F32)
    for t in range(TASKS):
        weights = jnp.where(task_lane == t, task_w[t].astype(F32), weights)
    coef = weights / jnp.maximum(count, 1.0)
    task = jnp.sum(jnp.where(eye, tasks[pl.ds(own_r, 1), :], 0), 1, keepdims=True)
    label = jnp.sum(jnp.where(eye, labels[pl.ds(own_r, 1), :], 0), 1, keepdims=True)
    picked = (task == task_lane) & (lane < TASKS * CLASSES)
    target = picked & (lane // TASKS == label)
    leads = (starts_s[own_r][:, 0:1] < fill[own_r]) & (z < R)
    weight = jnp.sum(jnp.where(target, coef, 0.0), -1, keepdims=True)
    weight = jnp.where(leads, weight, 0.0)
    tab[...] = jnp.concatenate([table[...], jnp.zeros((LANES - TASKS * CLASSES, D), F32)], 0).astype(BF)

    for copy in rs:
        copy.wait()
    got = [pack[own_r]] + [widen(pk_in[d]) for d in range(1, G)]
    stat = [st[own_r]] + [st_in[d] for d in range(1, G)]
    top = stat[0]
    for part in stat[1:]:
        top = jnp.maximum(top, part)
    shrink = [jnp.exp(part - top) for part in stat]
    tot = jnp.zeros((SEGS, LANES), F32)
    for part, s in zip(stat, shrink):
        tot = tot + pltpu.roll(part, HDIM, 1) * s
    tot = jnp.where(lane < HEADS, tot, 1.0)
    lse_out[...] = top + jnp.log(tot)
    mixed = jnp.zeros((SEGS, D), F32)
    for part, s in zip(got, shrink):
        mixed = mixed + expand(s / tot) * part
    mixed = mixed + biases[1:2, :]

    def guarded(cond, f):
        if cond is None:
            f()
        else:
            pl.when(cond)(f)

    mine = None if G == R else z < R

    def hand_out(k, src, dst):
        def start():
            for d in range(1, G):
                over("heads", d, src, dst.at[own_r], g_s.at[k, d], g_r.at[k, own_r]).start()

        def keep():
            dst[own_r] = src[...]

        guarded(mine, start)
        guarded(mine, keep)

    def take_in(k, src, dst):
        def one(r):
            pltpu.make_async_remote_copy(
                src_ref=src, dst_ref=dst.at[r], send_sem=g_s.at[k, 0], recv_sem=g_r.at[k, r],
                device_id={"heads": z}, device_id_type=MESH,
            ).wait_recv()

        for r in range(R):
            pl.when(z != r)(functools.partial(one, r))

    hand_out(0, lse_out, lse_in)

    loads[3].wait()
    r_one = xz_s[pl.ds(pl.multiple_of(own_r * SEGS, SEGS), SEGS), :] + mm(mixed.astype(BF), outw[...]) + biases[2:3, :]
    hat1, rstd1 = normed(r_one)
    x_one = hat1 * gains[1:2, :] + shifts[1:2, :]
    x_one_low = x_one.astype(BF)
    loads[4].wait()

    for n in range(FF // FT):
        at = slice(FT * n, FT * (n + 1))
        act[:, at] = mm(x_one_low, fin[:, at])
    h = act[...] + bias_in[...]
    half = 0.5 * (1.0 + lax.erf(h * 0.7071067811865476))
    act[...] = h * half
    slope[...] = half + h * (0.3989422804014327 * jnp.exp(-0.5 * h * h))
    loads[5].wait()
    act_low = act[...].astype(BF)

    def ffn_out_tile(n, _):
        fx[0:SEGS, cols(n)] = mm(act_low, fout[:, cols(n)])
        return 0

    lax.fori_loop(0, D // NT, ffn_out_tile, 0, unroll=D // NT)
    hat2, rstd2 = normed(x_one + fx[0:SEGS, :] + biases[3:4, :])
    x_two = (hat2 * gains[2:3, :] + shifts[2:3, :]).astype(BF)
    logits = mm_t(x_two, tab[...])
    chosen = jnp.where(picked, logits, NEG)
    peak = jnp.max(chosen, -1, keepdims=True)
    sums = jnp.sum(jnp.where(picked, jnp.exp(chosen - peak), 0.0), -1, keepdims=True)
    log_sum = peak + jnp.log(sums)
    hit = jnp.sum(jnp.where(target, logits, 0.0), -1, keepdims=True)
    loss = jnp.sum(weight * (log_sum - hit), 0, keepdims=True)
    soft = jnp.where(picked, jnp.exp(chosen - log_sum), 0.0) - target.astype(F32)
    g_logits = (weight * soft).astype(BF)
    g_two = mm(g_logits, tab[...])
    g_r2 = norm_back(hat2, rstd2, gains[2:3, :], g_two)
    g_f = g_r2.astype(BF)

    for n in range(FF // FT):
        at = slice(FT * n, FT * (n + 1))
        gh[:, at] = mm_t(g_f, fout[at, :]) * slope[:, at]
    gh_low = gh[...].astype(BF)

    def back_in(n, _):
        fx[0:SEGS, cols(n)] = mm_t(gh_low, fin[cols(n), :])
        return 0

    lax.fori_loop(0, D // NT, back_in, 0, unroll=D // NT)
    g_r1 = norm_back(hat1, rstd1, gains[1:2, :], g_r2 + fx[0:SEGS, :])
    g_mixed = mm_t(g_r1.astype(BF), outw[...]).astype(BF).astype(F32)
    quarters = [g_mixed[:, i * D // 4 : (i + 1) * D // 4] for i in range(4)]
    gpk[0] = jnp.concatenate(quarters[0:2], 0).astype(BF)
    gpk[1] = jnp.concatenate(quarters[2:4], 0).astype(BF)
    hand_out(1, gpk, gpk_in)
    dlt_out[...] = compress(g_mixed * mixed) - compress(g_mixed * biases[1:2, :])
    hand_out(2, dlt_out, dlt_in)
    hs[...] = mm(g_logits.astype(F32).T.astype(BF), x_two)[: CHUNKS * 8, :]
    hs[TASKS * CLASSES : TASKS * CLASSES + 8, :] = jnp.broadcast_to(loss, (8, D))

    def spread(src, dst, send, recv, limit, action):
        for d in range(1, G):
            copy = over("heads", d, src(lax.rem(z + d, G)), dst(d), send.at[d], recv(d))
            cond = limit(lax.rem(z + d, G))
            if cond is None:
                action(copy)
            else:
                pl.when(cond)(functools.partial(action, copy))

    def chunk_of(peer):
        return hs.at[pl.ds(pl.multiple_of(8 * lax.rem(peer, CHUNKS), 8), 8)]

    def small(peer):
        return None if G == CHUNKS else peer < CHUNKS

    holder = None if G == CHUNKS else z < CHUNKS
    take_in(0, lse_out, lse_in)
    take_in(1, gpk, gpk_in)
    for r in range(R):
        g_in[r] = widen(gpk_in[r])

    scale = [jnp.exp(st[r] - lse_in[r]) for r in range(R)]
    factor = jnp.concatenate([jnp.where(lane < HEADS, s, 0.0) for s in scale], 0)

    def back_value(t, acc):
        at = tile_at(t)
        g = g_in[:, :, at].reshape(L, LANES)
        z0 = mm_t(jnp.where(low_half, g, 0.0).astype(BF), qkv[:, tile_at(3 * t + 1)])
        z1 = mm_t(jnp.where(low_half, 0.0, g).astype(BF), qkv[:, tile_at(3 * t + 2)])
        zacc[two(t), :] = jnp.concatenate([z0, z1], 0)
        gb = g * scale_b[1:2, at]
        both = jnp.concatenate([jnp.where(low_half, gb, 0.0), jnp.where(low_half, 0.0, gb)], 0).astype(BF)
        back = mm_t(both, vb[:, at])
        f0 = jnp.sum(jnp.where(lane == 2 * t, factor, 0.0), -1, keepdims=True)
        f1 = jnp.sum(jnp.where(lane == 2 * t + 1, factor, 0.0), -1, keepdims=True)
        acc = acc + jnp.sum(jnp.concatenate([f0, f1], 0) * ua[two(t), :] * back, 0, keepdims=True)
        zb[two(t), :] = (back * scale_d[1:2, :]).astype(BF)
        return acc

    grad_d1 = lax.fori_loop(0, PAIRS, back_value, jnp.zeros((1, D), F32), unroll=UNROLL)
    grad_b1 = jnp.sum(g_in[...].reshape(L, D) * ev[...] * expand(factor), 0, keepdims=True)
    extra = TASKS * CLASSES + 1
    hs[extra : extra + 2, :] = jnp.concatenate([grad_d1, grad_b1], 0)
    spread(chunk_of, lambda d: h_in.at[d], h_ss, lambda d: h_rs.at[d], small, lambda c: c.start())

    def back_latent(n, _):
        at = cols(n)
        part = (zacc[:, at] + mm_t(zb[...], va[at, :])).reshape(HEADS, R, SEGS, NT)
        for r in range(R):
            zq[r, :, at] = part[:, r].reshape(Q, NT).astype(BF)
        return 0

    lax.fori_loop(0, D // NT, back_latent, 0, unroll=D // NT)

    def relay():
        acc = chunk_of(z)[...]
        for d in range(1, G):
            over("heads", d, chunk_of(z), h_in.at[d], h_ss.at[d], h_rs.at[d]).wait_recv()
            acc = acc + h_in[d]
        hr[...] = acc
        for d in range(1, NR):
            over("rows", d, hr, hr_in.at[d], hr_ss.at[d], hr_rs.at[d]).start()

    def slope_of(r):
        gdot[r % 2][...] = mm_t(zq[r], rows_of(r))

    def bend(r):
        f = to_col(jnp.where(lane < HEADS, jnp.exp(st[r] - lse_in[r]), 0.0))
        delta = to_col(dlt_in[r])
        for c in range(0, Q, PART):
            rows = slice(c, c + PART)
            ds = (expo[r][rows, :] * f[rows]) * (gdot[r % 2][rows, :] - delta[rows])
            low[r][rows, :] = ds.astype(BF)

    take_in(2, dlt_out, dlt_in)
    staged(slope_of, bend, lambda r: guarded(holder, relay) if r == R // 2 - 1 else None)

    def relay_two():
        acc = hr[...]
        for d in range(1, NR):
            over("rows", d, hr, hr_in.at[d], hr_ss.at[d], hr_rs.at[d]).wait()
            acc = acc + hr_in[d]
        ag[lax.rem(z, CHUNKS)] = acc
        for d in range(1, G):
            c = lax.rem(z, CHUNKS)
            over("heads", d, ag.at[c], ag.at[c], ag_ss.at[d], ag_rs.at[c]).start()

    def back_query(t, _):
        at = tile_at(t)
        k0 = mm(ub[2 * t], qkv[:, tile_at(3 * t)])
        k1 = mm(ub[2 * t + 1], qkv[:, tile_at(3 * t + 2)])
        gq_s[:, at] = pltpu.roll(jnp.where(low_half, k1, k0), HDIM, 1) * 0.125
        return 0

    lax.fori_loop(0, PAIRS, back_query, 0, unroll=UNROLL)
    g_query = gq_s[...]
    grad_b0 = jnp.sum(g_query * eq_s[...], 0, keepdims=True)
    back = mm_t((g_query * scale_b[0:1, :]).astype(BF), vb[...])
    grad_d0 = jnp.sum(latent_s[...] * back, 0, keepdims=True)
    two_rows = jnp.concatenate([grad_d0, grad_b0], 0)
    late[...] = jnp.concatenate([two_rows[:, i * D // 4 : (i + 1) * D // 4] for i in range(4)], 0)
    leg = [over("heads", d, late, lz_in.at[d], lz_ss.at[d], lz_rs.at[d]) for d in range(1, G)]
    for copy in leg:
        copy.start()
    guarded(holder, relay_two)
    for copy in leg:
        copy.wait()
    acc = late[...]
    for d in range(1, G):
        acc = acc + lz_in[d]
    lr[...] = acc
    leg = [over("rows", d, lr, lr_in.at[d], lr_ss.at[d], lr_rs.at[d]) for d in range(1, NR)]
    for copy in leg:
        copy.start()

    for c in range(CHUNKS):
        def arrive(c=c):
            pltpu.make_async_remote_copy(
                src_ref=ag.at[c], dst_ref=ag.at[c], send_sem=ag_ss.at[0], recv_sem=ag_rs.at[c],
                device_id={"heads": z}, device_id_type=MESH,
            ).wait_recv()

        pl.when(z != c)(arrive)
    heads_sum[...] = ag[...].reshape(CHUNKS * 8, D)
    def handed():
        for k, (src, dst) in enumerate(((lse_out, lse_in), (gpk, gpk_in), (dlt_out, dlt_in))):
            for d in range(1, G):
                over("heads", d, src, dst.at[own_r], g_s.at[k, d], g_r.at[k, own_r]).wait_send()

    guarded(mine, handed)
    spread(chunk_of, lambda d: h_in.at[d], h_ss, lambda d: h_rs.at[d], small, lambda c: c.wait_send())

    def sent():
        for d in range(1, G):
            c = lax.rem(z, CHUNKS)
            over("heads", d, ag.at[c], ag.at[c], ag_ss.at[d], ag_rs.at[c]).wait_send()

    guarded(holder, sent)
    for copy in leg:
        copy.wait()
    acc = lr[...]
    for d in range(1, NR):
        acc = acc + lr_in[d]
    small_sum[...] = acc


def update_kernel(
    heads_sum, small_sum, scale_d, scale_b, table, mom_d, mom_b, mom_h, avg_d, avg_b, avg_h,
    loss, m_d, m_b, m_h, w_d, w_b, w_h, a_d, a_b, a_h, low, stats,
):
    count = table.shape[0]
    pairs = jnp.concatenate([small_sum[2 * i : 2 * i + 2, :] for i in range(4)], 1)
    more = heads_sum[count + 1 : count + 3, :]
    grad_d = jnp.concatenate([pairs[0:1], more[0:1]], 0)
    grad_b = jnp.concatenate([pairs[1:2], more[1:2]], 0)
    m_d[...], new_d, a_d[...] = update(scale_d[...], grad_d, mom_d[...], avg_d[...], RATE_D)
    m_b[...], new_b, a_b[...] = update(scale_b[...], grad_b, mom_b[...], avg_b[...], RATE_B)
    m_h[...], new_h, a_h[...] = update(table[...], heads_sum[:count, :], mom_h[...], avg_h[...], RATE_HEADS)
    w_d[...], w_b[...], w_h[...], low[...] = new_d, new_b, new_h, new_h.astype(BF)
    loss[...] = heads_sum[count : count + 1, 0:1]
    rms = [jnp.sqrt(jnp.mean(jnp.mean(v * v, 1, keepdims=True), 0, keepdims=True)) for v in (new_d, new_b)]
    stats[...] = jnp.concatenate(rms, 1)


def on_device(
    sizes,
    token_ids, segment_ids, row_fill, task_ids, labels, task_weights,
    word_table, position_table, norm_gains, norm_biases, dense_biases,
    qkv_weight, out_weight, ffn_in, ffn_bias, ffn_out, vera_a, vera_b,
    scale_d, scale_b, task_heads, mom_d, mom_b, mom_heads, avg_d, avg_b, avg_heads,
):
    G, NR = sizes
    R, S = token_ids.shape
    V, D = word_table.shape
    FF = ffn_in.shape[1]
    L, Q, T = R * SEGS, HEADS * SEGS, R * S
    raw, leads = gather(token_ids, segment_ids, row_fill, word_table)

    def flat(value):
        return value.transpose(1, 0, 2).reshape(CLASSES * TASKS, D)

    table, mom_h, avg_h = flat(task_heads), flat(mom_heads), flat(avg_heads)
    v = pltpu.VMEM
    dma = pltpu.SemaphoreType.DMA
    scratch = [
        v((T, D), BF), v(qkv_weight.shape, BF), v(out_weight.shape, BF), v(ffn_in.shape, BF), v(ffn_out.shape, BF),
        v(vera_a.shape, BF), v(vera_b.shape, BF),
        v(position_table.shape, BF), v((position_table.shape[0] - 2, D), BF), v((G, L, D), BF), v((R, S), jnp.int32), v((R, SEGS, LANES), jnp.int32), v((L, D), F32),
        v((L, D), F32), v((L, D), F32), v((R, Q, D), BF), v((HEADS, L, D), BF),
        v((HEADS * L, D), F32), v((L, D), F32), v((R, SEGS, D), F32), v((R, SEGS, LANES), F32), v((G, SEGS, LANES), F32),
        v((R, 2, 2 * SEGS, D // 4), BF), v((G, 2, 2 * SEGS, D // 4), BF),
        v((SEGS, FF), F32), v((SEGS, FF), F32), v((SEGS, FF), F32), v((LANES, D), BF), v((SEGS, LANES), F32), v((R, SEGS, LANES), F32),
        v((2, 2 * SEGS, D // 4), BF), v((R, 2, 2 * SEGS, D // 4), BF), v((SEGS, LANES), F32), v((R, SEGS, LANES), F32),
        v((R, SEGS, D), F32), v((R, Q, D), BF), v((HEADS * L, D), F32), v((HEADS * L, D), BF), v((L, D), F32),
        v((L, D), F32),
        v((SEGS, LANES), F32), v((NR, SEGS, LANES), F32), v((CHUNKS * 8, D), F32), v((G, 8, D), F32), v((8, D), F32),
        v((NR, 8, D), F32), v((CHUNKS, 8, D), F32), v((8, D // 4), F32), v((G, 8, D // 4), F32), v((8, D // 4), F32),
        v((NR, 8, D // 4), F32),
        dma((7,)), dma((2,)), dma((G,)), dma((G,)), dma((NR,)), dma((NR,)), dma((3, G)), dma((3, G)),
        dma((3, G)), dma((3, R)), dma((G,)), dma((G,)), dma((NR,)), dma((NR,)), dma((G,)), dma((CHUNKS,)),
        dma((G,)), dma((G,)), dma((NR,)), dma((NR,)), *[v((Q, S), F32)] * (R + 2), *[v((Q, S), BF)] * R,
        v((S, D), BF), v((S, D), BF),
    ]
    vm, hbm, sm = (pl.BlockSpec(memory_space=m) for m in (pltpu.VMEM, pl.ANY, pltpu.SMEM))
    heads_sum, small_sum = pl.pallas_call(
        functools.partial(step_kernel, (R, S, G, NR, V)),
        out_shape=(jax.ShapeDtypeStruct((CHUNKS * 8, D), F32), jax.ShapeDtypeStruct((8, D // 4), F32)),
        in_specs=[sm, sm] + [vm] * 12 + [hbm] * 8,
        out_specs=(vm, vm),
        scratch_shapes=scratch,
        compiler_params=pltpu.CompilerParams(
            collective_id=0, has_side_effects=True, vmem_limit_bytes=60 * 1024 * 1024
        ),
    )(
        row_fill, task_weights, token_ids, segment_ids, task_ids, labels, leads, norm_gains, norm_biases,
        dense_biases, ffn_bias.reshape(1, -1), scale_d, scale_b, table,
        raw, position_table, qkv_weight, out_weight, ffn_in, ffn_out, vera_a, vera_b,
    )
    like = jax.ShapeDtypeStruct
    two, many = like((2, D), F32), like((CLASSES * TASKS, D), F32)
    loss, m_d, m_b, m_h, w_d, w_b, w_h, a_d, a_b, a_h, low, stats = pl.pallas_call(
        update_kernel,
        out_shape=(
            like((1, 1), F32), two, two, many, two, two, many, two, two, many, like((CLASSES * TASKS, D), BF), like((1, 2), F32),
        ),
        in_specs=[vm] * 11,
        out_specs=(vm,) * 12,
    )(heads_sum, small_sum, scale_d, scale_b, table, mom_d, mom_b, mom_h, avg_d, avg_b, avg_h)

    def unflat(value):
        return value.reshape(CLASSES, TASKS, D).transpose(1, 0, 2)

    return (
        loss.reshape(()), m_d, m_b, unflat(m_h), w_d, w_b, unflat(w_h), a_d, a_b, unflat(a_h), unflat(low), stats.reshape(2),
    )


def solution(mesh):
    sizes = (mesh.shape["heads"], mesh.shape["rows"])
    by_row = P("rows", None)
    return jax.shard_map(
        functools.partial(on_device, sizes),
        mesh=mesh,
        in_specs=(by_row, by_row, P("rows"), by_row, by_row, P(), P("heads", None)) + (P(),) * 20,
        out_specs=(P(),) * 12,
        check_vma=False,
    )
```

```python
import functools

import jax
import jax.numpy as jnp
from jax import lax
from jax.experimental import pallas as pl
from jax.experimental.pallas import tpu as pltpu
from jax.sharding import PartitionSpec as P

HEADS = 16
HDIM = 64
TASKS = 8
CLASSES = 3
SEGS = 8
LANES = 128
CHUNKS = 4
BLK = 256
GROUP = 128
SUB = 2
FT = 1024
UNROLL = 8
PART = 32
EPSILON = 1e-05
MOMENTUM = 0.9
AVERAGE = 0.8
RATE_D = 5.0
RATE_B = 20.0
RATE_HEADS = 0.3
NEG = -1e30
BF = jnp.bfloat16
F32 = jnp.float32
MESH = pl.DeviceIdType.MESH


def mm(left, right):
    return jnp.dot(left, right, preferred_element_type=F32)


def mm_t(left, right):
    return lax.dot_general(left, right, (((1,), (1,)), ((), ())), preferred_element_type=F32)


def mm_l(left, right):
    return lax.dot_general(left, right, (((0,), (0,)), ((), ())), preferred_element_type=F32)


def normed(values):
    centred = values - jnp.mean(values, -1, keepdims=True)
    rstd = lax.rsqrt(jnp.mean(centred * centred, -1, keepdims=True) + EPSILON)
    return centred * rstd, rstd


def norm_back(hat, rstd, gain, grad):
    scaled = grad * gain
    return rstd * (
        scaled
        - jnp.mean(scaled, -1, keepdims=True)
        - hat * jnp.mean(scaled * hat, -1, keepdims=True)
    )


def iota(shape, dim):
    return lax.broadcasted_iota(jnp.int32, shape, dim)


def update(weight, grad, moment, average, rate):
    moment_new = MOMENTUM * moment + grad
    weight_new = weight - rate * (grad + MOMENTUM * moment_new)
    return (moment_new, weight_new, AVERAGE * average + (1.0 - AVERAGE) * weight_new)


def gather_kernel(
    cfg, fill, ids, seg, words, x_out, lead_out,
    listv, lists, keyc, lead, bufs, stages, list_sem, buf_sem, out_sem,
):
    R, S, V = cfg
    D = x_out.shape[1]
    PER = S // BLK
    NB = R * PER
    HALVES = BLK // LANES
    STAGES = stages.shape[0]
    z = lax.axis_index("heads")
    slot = iota((1, S), 1)
    lane = iota((1, LANES), 1)
    jcol = iota((SEGS, 1), 0)
    row8 = iota((8, 1), 0)

    local = ids[...] - z * V
    segs = seg[...]
    fills = jnp.zeros((R, 1), jnp.int32)
    for r in range(R):
        fills = jnp.where(iota((R, 1), 0) == r, fill[r], fills)
    first = (slot == 0) | (segs != pltpu.roll(segs, 1, 1))
    need = (local >= 0) & (local < V) & (first | (slot < fills))
    upper = (iota((LANES, LANES), 0) <= iota((LANES, LANES), 1)).astype(F32).astype(BF)
    ahead = iota((BLK, BLK), 0) < iota((BLK, BLK), 1)

    def by_block(value):
        return jnp.concatenate([value[:, BLK * p : BLK * (p + 1)] for p in range(PER)], 0)

    pair = by_block(jnp.where(need, local // SUB, -1).astype(F32))
    half = by_block((local & (SUB - 1)).astype(F32))
    wanted = pair >= 0.0
    pair_col = pair.T
    same = [pair_col[:, q : q + 1] == pair[q : q + 1] for q in range(NB)]
    seen = [jnp.max(jnp.where(same[q] & ahead, 1.0, 0.0), 0, keepdims=True) for q in range(NB)]
    lead_one = jnp.where(wanted, 1.0 - jnp.concatenate(seen, 0), 0.0)
    halves = [lead_one[:, LANES * h : LANES * (h + 1)] for h in range(HALVES)]
    prefix = mm(jnp.concatenate(halves, 0).astype(BF), upper)
    runs, total = [], jnp.zeros((NB, 1), F32)
    for h in range(HALVES):
        run = prefix[NB * h : NB * (h + 1)]
        runs.append(run + total)
        total = total + run[:, LANES - 1 :]
    rank = jnp.where(lead_one > 0.0, jnp.concatenate(runs, 1) - 1.0, -1.0)
    held = jnp.maximum(rank, 0.0)
    count_row = jnp.zeros((1, LANES), F32)
    keys = []
    for q in range(NB):
        share = mm(jnp.broadcast_to(held[q : q + 1], (8, BLK)).astype(BF), same[q].astype(F32).astype(BF))
        keys.append(share[0:1])
    key = jnp.where(wanted, SUB * jnp.concatenate(keys, 0) + half, -1.0)
    key_col = key.T
    for r in range(R):
        starts = jnp.sum((segs[r : r + 1, :] < jcol).astype(jnp.int32), 1, keepdims=True)
        for p in range(PER):
            b, q = r * PER + p, p * R + r
            at_start = iota((1, BLK), 1) + BLK * p == starts
            lead_key = jnp.sum(jnp.where(at_start, key[q : q + 1] + 8.0, 0.0), 1, keepdims=True) - 8.0
            keyc[b] = jnp.concatenate([key_col[:, q : q + 1], lead_key, jnp.full((8, 1), -5.0, F32)], 0)
            order = rank[q : q + 1].astype(jnp.int32)
            spots = (iota((LANES, 1), 0) == jnp.where(order < 0, -1, order & (LANES - 1))).astype(F32).astype(BF)
            row_at = SUB * pair[q : q + 1].astype(jnp.int32)
            plane = jnp.where(row8 < HALVES, row_at & 255, row_at // 256)
            plane = jnp.where(((order // LANES) == (row8 & (HALVES - 1))) & (row8 < 2 * HALVES), plane, 0)
            both = mm_t(plane.astype(F32).astype(BF), spots)
            both = both[0:HALVES] + 256.0 * both[HALVES : 2 * HALVES]
            listv[HALVES * b : HALVES * (b + 1), :] = both.astype(jnp.int32)
            count_row = jnp.where(lane == b, total[q : q + 1], count_row)
    listv[HALVES * NB :, :] = jnp.broadcast_to(count_row.astype(jnp.int32), (8, LANES))
    to_scalar = pltpu.make_async_copy(listv, lists, list_sem.at[0])
    to_scalar.start()
    lead[...] = jnp.zeros_like(lead)
    for b in range(NB):
        bufs[b, 0 : GROUP * SUB // 8] = jnp.zeros((GROUP * SUB // 8, 8, D), BF)
    to_scalar.wait()

    def eights(b):
        n = lists[HALVES * NB, b]
        return jnp.where(n <= GROUP, (n + 7) // 8, (n + GROUP - 1) // GROUP * (GROUP // 8))

    def issue(r):
        for p in range(PER):
            b = r * PER + p

            def eight(i, _, b=b, h=0):
                for u in range(8):
                    word = lists[HALVES * b + h, i * 8 + u]
                    pltpu.make_async_copy(
                        words.at[pl.ds(pl.multiple_of(word, SUB), SUB)],
                        bufs.at[b, h * GROUP * SUB // 8 + i * SUB + u * SUB // 8, pl.ds(u * SUB % 8, SUB)],
                        buf_sem.at[r],
                    ).start()
                return 0

            lax.fori_loop(0, jnp.minimum(eights(b), GROUP // 8), eight, 0)

            @pl.when(lists[HALVES * NB, b] > GROUP)
            def more(eight=eight):
                lax.fori_loop(0, GROUP // 8, functools.partial(eight, h=1), 0)

    def arrive(r):
        total = eights(r * PER)
        for p in range(1, PER):
            total = total + eights(r * PER + p)
        part = bufs.at[0, pl.ds(0, SUB)]

        def eight(i, _):
            pltpu.make_async_copy(part, part, buf_sem.at[r]).wait()
            return 0

        lax.fori_loop(0, total, eight, 0)

    lanes = iota((1, GROUP * SUB), 1).astype(F32)

    def pick(b, g):
        one = (keyc[b] == lanes + float(g * GROUP * SUB)).astype(F32).astype(BF)
        rows = bufs[b, g * GROUP * SUB // 8 : (g + 1) * GROUP * SUB // 8]
        return mm(one, rows.reshape(GROUP * SUB, D))

    def add_lead(b, got):
        rows = pl.ds(pl.multiple_of(b // PER * SEGS, SEGS), SEGS)
        lead[rows, :] = lead[rows, :] + got

    def out_copy(b):
        k = lax.rem(b, STAGES)
        rows = pl.ds(pl.multiple_of(b * BLK, BLK), BLK)
        return pltpu.make_async_copy(stages.at[k], x_out.at[rows], out_sem.at[k])

    for r in range(R):
        issue(r)

    def row(r, _):
        arrive(r)

        def block(p, _):
            b = r * PER + p
            k = lax.rem(b, STAGES)
            pl.when(b >= STAGES)(lambda: out_copy(b - STAGES).wait())
            got = pick(b, 0)
            stages[k] = got[:BLK].astype(BF)
            add_lead(b, got[BLK : BLK + SEGS])

            @pl.when(lists[HALVES * NB, b] > GROUP)
            def more():
                got = pick(b, 1)
                stages[k] = stages[k] + got[:BLK].astype(BF)
                add_lead(b, got[BLK : BLK + SEGS])

            out_copy(b).start()
            return 0

        return lax.fori_loop(0, PER, block, 0)

    lax.fori_loop(0, R, row, 0)
    lead_out[...] = lead[...].astype(BF)
    for k in range(STAGES):
        out_copy(NB - STAGES + k).wait()


def gather(token_ids, segment_ids, row_fill, word_table):
    R, S = token_ids.shape
    V, D = word_table.shape
    PER = S // BLK
    NB = R * PER
    HALVES = BLK // LANES
    if V % SUB:
        word_table = jnp.pad(word_table, ((0, -V % SUB), (0, 0)))
    v, dma = pltpu.VMEM, pltpu.SemaphoreType.DMA
    vm, hbm, sm = (pl.BlockSpec(memory_space=m) for m in (pltpu.VMEM, pl.ANY, pltpu.SMEM))
    return pl.pallas_call(
        functools.partial(gather_kernel, (R, S, V)),
        out_shape=(jax.ShapeDtypeStruct((R * S, D), BF), jax.ShapeDtypeStruct((R * SEGS, D), BF)),
        in_specs=[sm, vm, vm, hbm],
        out_specs=(hbm, vm),
        scratch_shapes=[
            v((HALVES * NB + 8, LANES), jnp.int32),
            pltpu.SMEM((HALVES * NB + 8, LANES), jnp.int32), v((NB, BLK + 2 * SEGS, 1), F32),
            v((R * SEGS, D), F32),
            v((NB, BLK * SUB // 8, 8, D), BF), v((4, BLK, D), BF), dma((1,)), dma((R,)), dma((4,)),
        ],
        compiler_params=pltpu.CompilerParams(vmem_limit_bytes=60 * 1024 * 1024),
    )(row_fill, token_ids, segment_ids, word_table)


def step_kernel(
    cfg,
    fill, task_w, ids, seg, tasks, labels, lead_out, gains, shifts, biases, bias_in, scale_d, scale_b, table,
    x_h, place_h, qkv_h, out_h, fin_h, fout_h, va_h, vb_h,
    heads_sum, small_sum,
    x, qkv, outw, fin, fout, va, vb,
    place, places, lead_in, seg_eff, starts_s, xz_s, latent_s, eq_s, qk, ub, ua, ev, pack, st, st_in, pk, pk_in,
    act, slope, gh, tab, lse_out, lse_in, gpk, gpk_in, dlt_out, dlt_in, g_in, zq, zacc, zb, gq_s, fx,
    cnt_out, cnt_in, hs, h_in, hr, hr_in, ag, late, lz_in, lr, lr_in,
    load_sem, x_sem, e1_s, e1_r, cnt_ss, cnt_rs, rs_s, rs_r, g_s, g_r, h_ss, h_rs, hr_ss, hr_rs, ag_ss, ag_rs,
    lz_ss, lz_rs, lr_ss, lr_rs, *wide,
):
    R, S, G, NR, V = cfg
    expo, gdot, low, words = wide[:R], wide[R : R + 2], wide[R + 2 : 2 * R + 2], wide[2 * R + 2 :]
    D = x.shape[1]
    FF = fin.shape[1]
    PAIRS = HEADS // 2
    L = R * SEGS
    z = lax.axis_index("heads")
    rw = lax.axis_index("rows")
    own_r = lax.rem(z, R)

    def x_load(r, h):
        return pltpu.make_async_copy(x_h.at[pl.ds(pl.multiple_of(r * S, S), S)], words[h], x_sem.at[h])

    loads = [
        pltpu.make_async_copy(src, dst, load_sem.at[i])
        for i, (src, dst) in enumerate(
            (
                (va_h, va), (vb_h, vb), (qkv_h, qkv), (out_h, outw), (fin_h, fin), (fout_h, fout),
                (place_h, place),
            )
        )
    ]
    for copy in [x_load(0, 0), loads[6], x_load(1, 1)]:
        copy.start()

    barrier = pltpu.get_barrier_semaphore()
    for d in range(1, G):
        pl.semaphore_signal(barrier, inc=1, device_id={"heads": lax.rem(z + d, G)}, device_id_type=MESH)
    for d in range(1, NR):
        pl.semaphore_signal(barrier, inc=1, device_id={"rows": lax.rem(rw + d, NR)}, device_id_type=MESH)
    pl.semaphore_wait(barrier, G - 1 + NR - 1)

    def over(axis, d, src, dst, send, recv):
        me, size = (z, G) if axis == "heads" else (rw, NR)
        return pltpu.make_async_remote_copy(
            src_ref=src, dst_ref=dst, send_sem=send, recv_sem=recv,
            device_id={axis: lax.rem(me + d, size)}, device_id_type=MESH,
        )

    lane = iota((1, LANES), 1)
    low_half = lane < HDIM
    jcol = iota((SEGS, 1), 0)
    slot = iota((1, S), 1)

    def expand(f):
        tiles = [jnp.where(low_half, f[:, 2 * t : 2 * t + 1], f[:, 2 * t + 1 : 2 * t + 2]) for t in range(PAIRS)]
        return jnp.concatenate(tiles, 1)

    def compress(v):
        out = jnp.zeros((v.shape[0], LANES), F32)
        for t in range(PAIRS):
            tile = v[:, LANES * t : LANES * (t + 1)]
            a = jnp.sum(jnp.where(low_half, tile, 0.0), -1, keepdims=True)
            b = jnp.sum(jnp.where(low_half, 0.0, tile), -1, keepdims=True)
            out = jnp.where(lane == 2 * t, a, jnp.where(lane == 2 * t + 1, b, out))
        return out

    e1 = [over("heads", d, lead_out, lead_in.at[d], e1_s.at[d], e1_r.at[d]) for d in range(1, G)]
    for copy in e1:
        copy.start()

    eye = iota((SEGS, SEGS), 0) == iota((SEGS, SEGS), 1)
    task_lane = lane & (TASKS - 1)
    counts = jnp.zeros((SEGS, LANES), F32)
    for r in range(R):
        seg_row = seg[r : r + 1, :]
        local = ids[r : r + 1, :] - z * V
        own = (local >= 0) & (local < V)
        first = (slot == 0) | (seg_row != pltpu.roll(seg_row, 1, 1))
        seg_eff[r : r + 1, :] = jnp.where(own & (first | (slot < fill[r])), seg_row, -1)
        starts = jnp.sum((seg_row < jcol).astype(jnp.int32), 1, keepdims=True)
        starts_s[r] = jnp.broadcast_to(starts, (SEGS, LANES))
        lead = (starts < fill[r]).astype(F32)
        task = jnp.sum(jnp.where(eye, tasks[r : r + 1, :], 0), 1, keepdims=True)
        counts = counts + jnp.where((task == task_lane) & (lane < TASKS * CLASSES), lead, 0.0)
    cnt_out[...] = counts
    cnt = [over("rows", d, cnt_out, cnt_in.at[d], cnt_ss.at[d], cnt_rs.at[d]) for d in range(1, NR)]
    for copy in cnt:
        copy.start()
    gain0, shift0 = gains[0:1, :], shifts[0:1, :]
    loads[6].wait()
    places[...] = place[2:, :]
    prow = iota((places.shape[0], 1), 0)

    STEP = expo[0].shape[0]
    blocks = S // STEP

    def norm_row(r, h):
        seg_row = seg[pl.ds(r, 1), :]
        begin = jnp.sum(jnp.where(seg_row == jcol, starts_s[r][:, 0:1], 0), 0, keepdims=True)
        offset = slot - begin
        x_load(r, h).wait()

        def place_rows(b):
            one = (prow == offset[:, b * STEP : (b + 1) * STEP]).astype(F32).astype(BF)
            expo[b % R][...] = mm_l(one, places[...])

        place_rows(0)
        for b in range(blocks):
            if b + 1 < blocks:
                place_rows(b + 1)
            for c in range(0, STEP, PART):
                at = b * STEP + c
                hat, _ = normed(expo[b % R][c : c + PART, :] + words[h][at : at + PART, :].astype(F32))
                x[pl.ds(pl.multiple_of(r * S + at, PART), PART), :] = (hat * gain0 + shift0).astype(BF)

    def norm_two(i, _):
        for h in range(2):
            norm_row(2 * i + h, h)
            pl.when(i + 1 < R // 2)(lambda h=h: x_load(2 * i + 2 + h, h).start())
        return 0

    loads[0].start()
    loads[1].start()
    loads[2].start()
    lax.fori_loop(0, R // 2, norm_two, 0)

    for copy in e1:
        copy.wait()
    word = lead_out[...].astype(F32)
    for d in range(1, G):
        word = word + lead_in[d].astype(F32)
    hat, _ = normed(word + places[0:1, :].astype(F32))
    xz = hat * gain0 + shift0
    xz_s[...] = xz
    xl = xz.astype(BF)
    loads[0].wait()
    latent = mm(xl, va[...])
    latent_s[...] = latent
    loads[1].wait()
    eq_s[...] = mm((latent * scale_d[0:1, :]).astype(BF), vb[...])
    loads[2].wait()
    for copy in loads[3:6]:
        copy.start()

    def tile_at(t):
        return pl.ds(pl.multiple_of(LANES * t, LANES), LANES)

    for t in range(PAIRS):
        r = mm(xl, qkv[:, 384 * t : 384 * t + 256])
        at = slice(LANES * t, LANES * (t + 1))
        q = jnp.where(low_half, r[:, :LANES], r[:, LANES:]) + (biases[0:1, at] + scale_b[0:1, at] * eq_s[:, at])
        gq_s[:, at] = pltpu.roll(q.astype(BF).astype(F32) * 0.125, HDIM, 1)

    def keys_at(t):
        first = max(384 * t - LANES, 0)
        return slice(first, min(384 * t + LANES, 3 * D))

    def both_heads(t):
        parts, none = [], jnp.zeros((L, LANES), F32)
        if t > 0:
            odd = jnp.where(low_half, gq_s[:, LANES * (t - 1) : LANES * t], 0.0)
            parts.append(odd if t == PAIRS else jnp.concatenate([odd, none], 1))
        if t < PAIRS:
            even = jnp.where(low_half, 0.0, gq_s[:, LANES * t : LANES * (t + 1)])
            parts.append(even if t == 0 else jnp.concatenate([none, even], 1))
        return jnp.concatenate(parts, 0).astype(BF)

    even = mm_t(both_heads(0), qkv[:, keys_at(0)])
    for t in range(PAIRS):
        found = mm_t(both_heads(t + 1), qkv[:, keys_at(t + 1)])
        for r_ in range(R):
            rows = slice(r_ * SEGS, (r_ + 1) * SEGS)
            qk[r_, 16 * t : 16 * (t + 1), :] = jnp.concatenate([even[rows], found[:L][rows]], 0).astype(BF)
        even = found[L:]

    Q = HEADS * SEGS
    qj = lax.rem(iota((Q, 1), 0), SEGS)
    hsub = iota((HEADS, SEGS, LANES), 0)
    hlane = iota((HEADS, SEGS, LANES), 2)

    def to_lanes(col):
        return jnp.sum(jnp.where(hsub == hlane, col.reshape(HEADS, SEGS, 1), 0.0), 0)

    def to_col(f):
        wide = jnp.broadcast_to(f[None], (HEADS, SEGS, LANES))
        return jnp.sum(jnp.where(hsub == hlane, wide, 0.0), -1, keepdims=True).reshape(Q, 1)

    def rows_of(r):
        return x[r * S : (r + 1) * S, :]

    def score(r):
        expo[r][...] = mm_t(qk[r], rows_of(r))

    def soften(r):
        tops, sums = [], []
        for c in range(0, Q, PART):
            rows = slice(c, c + PART)
            mask = seg_eff[r : r + 1, :] == qj[rows]
            sc = jnp.where(mask, expo[r][rows, :], NEG)
            top = jnp.max(sc, -1, keepdims=True)
            e = jnp.where(mask, jnp.exp(sc - top), 0.0)
            expo[r][rows, :] = e
            low[r][rows, :] = e.astype(BF)
            tops.append(top)
            sums.append(jnp.sum(e, -1, keepdims=True))
        top, total = jnp.concatenate(tops, 0), jnp.concatenate(sums, 0)
        st[r] = to_lanes(top) + pltpu.roll(to_lanes(total), HDIM, 1)

    def mix(r):
        return mm(low[r][...], rows_of(r)).reshape(HEADS, SEGS, D)

    def staged(first_part, second_part, between):
        first_part(0)
        held = None
        for r in range(R):
            if r + 1 < R:
                first_part(r + 1)
            second_part(r)
            part = mix(r)
            if r % 2:
                ub[:, SEGS * (r - 1) : SEGS * (r + 1), :] = jnp.concatenate([held, part], 1).astype(BF)
            held = part
            between(r)

    staged(score, soften, lambda r: None)

    def row_of(d):
        return lax.rem(lax.rem(z + d, G), R)

    rs = [over("heads", d, st.at[row_of(d)], st_in.at[d], rs_s.at[0, d], rs_r.at[0, d]) for d in range(1, G)]
    for copy in rs:
        copy.start()

    NT = 256

    def cols(n):
        return pl.ds(pl.multiple_of(NT * n, NT), NT)

    def latents(n, _):
        ua[:, cols(n)] = mm(ub[...].reshape(HEADS * L, D), va[:, cols(n)])
        return 0

    lax.fori_loop(0, D // NT, latents, 0, unroll=D // NT)

    def values_at(t):
        return pl.ds(pl.multiple_of(LANES * (3 * t + 1), LANES), 2 * LANES)

    def two(t):
        return pl.ds(pl.multiple_of(2 * L * t, 2 * L), 2 * L)

    def values(t, _):
        at = tile_at(t)
        v = mm(ub[pl.ds(2 * t, 2)].reshape(2 * L, D), qkv[:, values_at(t)])
        pair = mm((ua[two(t), :] * scale_d[1:2, :]).astype(BF), vb[:, at])
        extra = jnp.where(low_half, pair[:L], pair[L:])
        ev[:, at] = extra
        mixed = jnp.where(low_half, v[:L, :LANES], v[L:, LANES:]) + scale_b[1:2, at] * extra
        pack[:, :, at] = mixed.reshape(R, SEGS, LANES)
        return 0

    for half in range(2):
        lax.fori_loop(half * PAIRS // 2, (half + 1) * PAIRS // 2, values, 0, unroll=PAIRS // 2)
        left, quarter = half * D // 2, D // 4
        for r in range(R):
            parts = [pack[r, :, left : left + quarter], pack[r, :, left + quarter : left + 2 * quarter]]
            pk[r, half] = jnp.concatenate(parts, 0).astype(BF)
        leg = [
            over("heads", d, pk.at[row_of(d), half], pk_in.at[d, half], rs_s.at[1 + half, d], rs_r.at[1 + half, d])
            for d in range(1, G)
        ]
        for copy in leg:
            copy.start()
        rs = rs + leg

    def widen(halves):
        both = [halves[i].astype(F32) for i in range(2)]
        return jnp.concatenate([v for h in both for v in (h[:SEGS], h[SEGS:])], 1)

    for copy in cnt:
        copy.wait()
    total = cnt_out[...]
    for d in range(1, NR):
        total = total + cnt_in[d]
    count = jnp.sum(total, 0, keepdims=True)
    weights = jnp.zeros((1, LANES), F32)
    for t in range(TASKS):
        weights = jnp.where(task_lane == t, task_w[t].astype(F32), weights)
    coef = weights / jnp.maximum(count, 1.0)
    task = jnp.sum(jnp.where(eye, tasks[pl.ds(own_r, 1), :], 0), 1, keepdims=True)
    label = jnp.sum(jnp.where(eye, labels[pl.ds(own_r, 1), :], 0), 1, keepdims=True)
    picked = (task == task_lane) & (lane < TASKS * CLASSES)
    target = picked & (lane // TASKS == label)
    leads = (starts_s[own_r][:, 0:1] < fill[own_r]) & (z < R)
    weight = jnp.sum(jnp.where(target, coef, 0.0), -1, keepdims=True)
    weight = jnp.where(leads, weight, 0.0)
    tab[...] = jnp.concatenate([table[...], jnp.zeros((LANES - TASKS * CLASSES, D), F32)], 0).astype(BF)

    for copy in rs:
        copy.wait()
    got = [pack[own_r]] + [widen(pk_in[d]) for d in range(1, G)]
    stat = [st[own_r]] + [st_in[d] for d in range(1, G)]
    top = stat[0]
    for part in stat[1:]:
        top = jnp.maximum(top, part)
    shrink = [jnp.exp(part - top) for part in stat]
    tot = jnp.zeros((SEGS, LANES), F32)
    for part, s in zip(stat, shrink):
        tot = tot + pltpu.roll(part, HDIM, 1) * s
    tot = jnp.where(lane < HEADS, tot, 1.0)
    lse_out[...] = top + jnp.log(tot)
    mixed = jnp.zeros((SEGS, D), F32)
    for part, s in zip(got, shrink):
        mixed = mixed + expand(s / tot) * part
    mixed = mixed + biases[1:2, :]

    def guarded(cond, f):
        if cond is None:
            f()
        else:
            pl.when(cond)(f)

    mine = None if G == R else z < R

    def hand_out(k, src, dst):
        def start():
            for d in range(1, G):
                over("heads", d, src, dst.at[own_r], g_s.at[k, d], g_r.at[k, own_r]).start()

        def keep():
            dst[own_r] = src[...]

        guarded(mine, start)
        guarded(mine, keep)

    def take_in(k, src, dst):
        def one(r):
            pltpu.make_async_remote_copy(
                src_ref=src, dst_ref=dst.at[r], send_sem=g_s.at[k, 0], recv_sem=g_r.at[k, r],
                device_id={"heads": z}, device_id_type=MESH,
            ).wait_recv()

        for r in range(R):
            pl.when(z != r)(functools.partial(one, r))

    hand_out(0, lse_out, lse_in)

    loads[3].wait()
    r_one = xz_s[pl.ds(pl.multiple_of(own_r * SEGS, SEGS), SEGS), :] + mm(mixed.astype(BF), outw[...]) + biases[2:3, :]
    hat1, rstd1 = normed(r_one)
    x_one = hat1 * gains[1:2, :] + shifts[1:2, :]
    x_one_low = x_one.astype(BF)
    loads[4].wait()

    for n in range(FF // FT):
        at = slice(FT * n, FT * (n + 1))
        act[:, at] = mm(x_one_low, fin[:, at])
    h = act[...] + bias_in[...]
    half = 0.5 * (1.0 + lax.erf(h * 0.7071067811865476))
    act[...] = h * half
    slope[...] = half + h * (0.3989422804014327 * jnp.exp(-0.5 * h * h))
    loads[5].wait()
    act_low = act[...].astype(BF)

    def ffn_out_tile(n, _):
        fx[0:SEGS, cols(n)] = mm(act_low, fout[:, cols(n)])
        return 0

    lax.fori_loop(0, D // NT, ffn_out_tile, 0, unroll=D // NT)
    hat2, rstd2 = normed(x_one + fx[0:SEGS, :] + biases[3:4, :])
    x_two = (hat2 * gains[2:3, :] + shifts[2:3, :]).astype(BF)
    logits = mm_t(x_two, tab[...])
    chosen = jnp.where(picked, logits, NEG)
    peak = jnp.max(chosen, -1, keepdims=True)
    sums = jnp.sum(jnp.where(picked, jnp.exp(chosen - peak), 0.0), -1, keepdims=True)
    log_sum = peak + jnp.log(sums)
    hit = jnp.sum(jnp.where(target, logits, 0.0), -1, keepdims=True)
    loss = jnp.sum(weight * (log_sum - hit), 0, keepdims=True)
    soft = jnp.where(picked, jnp.exp(chosen - log_sum), 0.0) - target.astype(F32)
    g_logits = (weight * soft).astype(BF)
    g_two = mm(g_logits, tab[...])
    g_r2 = norm_back(hat2, rstd2, gains[2:3, :], g_two)
    g_f = g_r2.astype(BF)

    for n in range(FF // FT):
        at = slice(FT * n, FT * (n + 1))
        gh[:, at] = mm_t(g_f, fout[at, :]) * slope[:, at]
    gh_low = gh[...].astype(BF)

    def back_in(n, _):
        fx[0:SEGS, cols(n)] = mm_t(gh_low, fin[cols(n), :])
        return 0

    lax.fori_loop(0, D // NT, back_in, 0, unroll=D // NT)
    g_r1 = norm_back(hat1, rstd1, gains[1:2, :], g_r2 + fx[0:SEGS, :])
    g_mixed = mm_t(g_r1.astype(BF), outw[...]).astype(BF).astype(F32)
    quarters = [g_mixed[:, i * D // 4 : (i + 1) * D // 4] for i in range(4)]
    gpk[0] = jnp.concatenate(quarters[0:2], 0).astype(BF)
    gpk[1] = jnp.concatenate(quarters[2:4], 0).astype(BF)
    hand_out(1, gpk, gpk_in)
    dlt_out[...] = compress(g_mixed * mixed) - compress(g_mixed * biases[1:2, :])
    hand_out(2, dlt_out, dlt_in)
    hs[...] = mm(g_logits.astype(F32).T.astype(BF), x_two)[: CHUNKS * 8, :]
    hs[TASKS * CLASSES : TASKS * CLASSES + 8, :] = jnp.broadcast_to(loss, (8, D))

    def spread(src, dst, send, recv, limit, action):
        for d in range(1, G):
            copy = over("heads", d, src(lax.rem(z + d, G)), dst(d), send.at[d], recv(d))
            cond = limit(lax.rem(z + d, G))
            if cond is None:
                action(copy)
            else:
                pl.when(cond)(functools.partial(action, copy))

    def chunk_of(peer):
        return hs.at[pl.ds(pl.multiple_of(8 * lax.rem(peer, CHUNKS), 8), 8)]

    def small(peer):
        return None if G == CHUNKS else peer < CHUNKS

    holder = None if G == CHUNKS else z < CHUNKS
    take_in(0, lse_out, lse_in)
    take_in(1, gpk, gpk_in)
    for r in range(R):
        g_in[r] = widen(gpk_in[r])

    scale = [jnp.exp(st[r] - lse_in[r]) for r in range(R)]
    factor = jnp.concatenate([jnp.where(lane < HEADS, s, 0.0) for s in scale], 0)

    def back_value(t, acc):
        at = tile_at(t)
        g = g_in[:, :, at].reshape(L, LANES)
        none = jnp.zeros((L, LANES), F32)
        upper = jnp.concatenate([jnp.where(low_half, g, 0.0), none], 1)
        lower = jnp.concatenate([none, jnp.where(low_half, 0.0, g)], 1)
        zacc[two(t), :] = mm_t(jnp.concatenate([upper, lower], 0).astype(BF), qkv[:, values_at(t)])
        gb = g * scale_b[1:2, at]
        both = jnp.concatenate([jnp.where(low_half, gb, 0.0), jnp.where(low_half, 0.0, gb)], 0).astype(BF)
        back = mm_t(both, vb[:, at])
        f0 = jnp.sum(jnp.where(lane == 2 * t, factor, 0.0), -1, keepdims=True)
        f1 = jnp.sum(jnp.where(lane == 2 * t + 1, factor, 0.0), -1, keepdims=True)
        acc = acc + jnp.sum(jnp.concatenate([f0, f1], 0) * ua[two(t), :] * back, 0, keepdims=True)
        zb[two(t), :] = (back * scale_d[1:2, :]).astype(BF)
        return acc

    grad_d1 = lax.fori_loop(0, PAIRS, back_value, jnp.zeros((1, D), F32), unroll=UNROLL)
    grad_b1 = jnp.sum(g_in[...].reshape(L, D) * ev[...] * expand(factor), 0, keepdims=True)
    extra = TASKS * CLASSES + 1
    hs[extra : extra + 2, :] = jnp.concatenate([grad_d1, grad_b1], 0)
    spread(chunk_of, lambda d: h_in.at[d], h_ss, lambda d: h_rs.at[d], small, lambda c: c.start())

    def back_latent(n, _):
        at = cols(n)
        part = (zacc[:, at] + mm_t(zb[...], va[at, :])).reshape(HEADS, R, SEGS, NT)
        for r in range(R):
            zq[r, :, at] = part[:, r].reshape(Q, NT).astype(BF)
        return 0

    lax.fori_loop(0, D // NT, back_latent, 0, unroll=D // NT)

    def relay():
        acc = chunk_of(z)[...]
        for d in range(1, G):
            over("heads", d, chunk_of(z), h_in.at[d], h_ss.at[d], h_rs.at[d]).wait_recv()
            acc = acc + h_in[d]
        hr[...] = acc
        for d in range(1, NR):
            over("rows", d, hr, hr_in.at[d], hr_ss.at[d], hr_rs.at[d]).start()

    def slope_of(r):
        gdot[r % 2][...] = mm_t(zq[r], rows_of(r))

    def bend(r):
        f = to_col(jnp.where(lane < HEADS, jnp.exp(st[r] - lse_in[r]), 0.0))
        delta = to_col(dlt_in[r])
        for c in range(0, Q, PART):
            rows = slice(c, c + PART)
            ds = (expo[r][rows, :] * f[rows]) * (gdot[r % 2][rows, :] - delta[rows])
            low[r][rows, :] = ds.astype(BF)

    take_in(2, dlt_out, dlt_in)
    staged(slope_of, bend, lambda r: guarded(holder, relay) if r == R // 2 - 1 else None)

    def relay_two():
        acc = hr[...]
        for d in range(1, NR):
            over("rows", d, hr, hr_in.at[d], hr_ss.at[d], hr_rs.at[d]).wait()
            acc = acc + hr_in[d]
        ag[lax.rem(z, CHUNKS)] = acc
        for d in range(1, G):
            c = lax.rem(z, CHUNKS)
            over("heads", d, ag.at[c], ag.at[c], ag_ss.at[d], ag_rs.at[c]).start()

    even = mm(ub[0], qkv[:, keys_at(0)])
    for t in range(PAIRS):
        heads = slice(2 * t + 1, min(2 * t + 3, HEADS))
        found = mm(ub[heads].reshape(-1, D), qkv[:, keys_at(t + 1)])
        both = jnp.where(low_half, found[:L, :LANES], even)
        gq_s[:, LANES * t : LANES * (t + 1)] = pltpu.roll(both, HDIM, 1) * 0.125
        even = found[L:, LANES:]
    g_query = gq_s[...]
    grad_b0 = jnp.sum(g_query * eq_s[...], 0, keepdims=True)
    back = mm_t((g_query * scale_b[0:1, :]).astype(BF), vb[...])
    grad_d0 = jnp.sum(latent_s[...] * back, 0, keepdims=True)
    two_rows = jnp.concatenate([grad_d0, grad_b0], 0)
    late[...] = jnp.concatenate([two_rows[:, i * D // 4 : (i + 1) * D // 4] for i in range(4)], 0)
    leg = [over("heads", d, late, lz_in.at[d], lz_ss.at[d], lz_rs.at[d]) for d in range(1, G)]
    for copy in leg:
        copy.start()
    guarded(holder, relay_two)
    for copy in leg:
        copy.wait()
    acc = late[...]
    for d in range(1, G):
        acc = acc + lz_in[d]
    lr[...] = acc
    leg = [over("rows", d, lr, lr_in.at[d], lr_ss.at[d], lr_rs.at[d]) for d in range(1, NR)]
    for copy in leg:
        copy.start()

    for c in range(CHUNKS):
        def arrive(c=c):
            pltpu.make_async_remote_copy(
                src_ref=ag.at[c], dst_ref=ag.at[c], send_sem=ag_ss.at[0], recv_sem=ag_rs.at[c],
                device_id={"heads": z}, device_id_type=MESH,
            ).wait_recv()

        pl.when(z != c)(arrive)
    heads_sum[...] = ag[...].reshape(CHUNKS * 8, D)
    def handed():
        for k, (src, dst) in enumerate(((lse_out, lse_in), (gpk, gpk_in), (dlt_out, dlt_in))):
            for d in range(1, G):
                over("heads", d, src, dst.at[own_r], g_s.at[k, d], g_r.at[k, own_r]).wait_send()

    guarded(mine, handed)
    spread(chunk_of, lambda d: h_in.at[d], h_ss, lambda d: h_rs.at[d], small, lambda c: c.wait_send())

    def sent():
        for d in range(1, G):
            c = lax.rem(z, CHUNKS)
            over("heads", d, ag.at[c], ag.at[c], ag_ss.at[d], ag_rs.at[c]).wait_send()

    guarded(holder, sent)
    for copy in leg:
        copy.wait()
    acc = lr[...]
    for d in range(1, NR):
        acc = acc + lr_in[d]
    small_sum[...] = acc


def update_kernel(
    heads_sum, small_sum, scale_d, scale_b, table, mom_d, mom_b, mom_h, avg_d, avg_b, avg_h,
    loss, m_d, m_b, m_h, w_d, w_b, w_h, a_d, a_b, a_h, low, stats,
):
    count = table.shape[0]
    pairs = jnp.concatenate([small_sum[2 * i : 2 * i + 2, :] for i in range(4)], 1)
    more = heads_sum[count + 1 : count + 3, :]
    grad_d = jnp.concatenate([pairs[0:1], more[0:1]], 0)
    grad_b = jnp.concatenate([pairs[1:2], more[1:2]], 0)
    m_d[...], new_d, a_d[...] = update(scale_d[...], grad_d, mom_d[...], avg_d[...], RATE_D)
    m_b[...], new_b, a_b[...] = update(scale_b[...], grad_b, mom_b[...], avg_b[...], RATE_B)
    m_h[...], new_h, a_h[...] = update(table[...], heads_sum[:count, :], mom_h[...], avg_h[...], RATE_HEADS)
    w_d[...], w_b[...], w_h[...], low[...] = new_d, new_b, new_h, new_h.astype(BF)
    loss[...] = heads_sum[count : count + 1, 0:1]
    rms = [jnp.sqrt(jnp.mean(jnp.mean(v * v, 1, keepdims=True), 0, keepdims=True)) for v in (new_d, new_b)]
    stats[...] = jnp.concatenate(rms, 1)


def on_device(
    sizes,
    token_ids, segment_ids, row_fill, task_ids, labels, task_weights,
    word_table, position_table, norm_gains, norm_biases, dense_biases,
    qkv_weight, out_weight, ffn_in, ffn_bias, ffn_out, vera_a, vera_b,
    scale_d, scale_b, task_heads, mom_d, mom_b, mom_heads, avg_d, avg_b, avg_heads,
):
    G, NR = sizes
    R, S = token_ids.shape
    V, D = word_table.shape
    FF = ffn_in.shape[1]
    L, Q, T = R * SEGS, HEADS * SEGS, R * S
    raw, leads = gather(token_ids, segment_ids, row_fill, word_table)

    def flat(value):
        return value.transpose(1, 0, 2).reshape(CLASSES * TASKS, D)

    table, mom_h, avg_h = flat(task_heads), flat(mom_heads), flat(avg_heads)
    v = pltpu.VMEM
    dma = pltpu.SemaphoreType.DMA
    scratch = [
        v((T, D), BF), v(qkv_weight.shape, BF), v(out_weight.shape, BF), v(ffn_in.shape, BF), v(ffn_out.shape, BF),
        v(vera_a.shape, BF), v(vera_b.shape, BF),
        v(position_table.shape, BF), v((position_table.shape[0] - 2, D), BF), v((G, L, D), BF), v((R, S), jnp.int32), v((R, SEGS, LANES), jnp.int32), v((L, D), F32),
        v((L, D), F32), v((L, D), F32), v((R, Q, D), BF), v((HEADS, L, D), BF),
        v((HEADS * L, D), F32), v((L, D), F32), v((R, SEGS, D), F32), v((R, SEGS, LANES), F32), v((G, SEGS, LANES), F32),
        v((R, 2, 2 * SEGS, D // 4), BF), v((G, 2, 2 * SEGS, D // 4), BF),
        v((SEGS, FF), F32), v((SEGS, FF), F32), v((SEGS, FF), F32), v((LANES, D), BF), v((SEGS, LANES), F32), v((R, SEGS, LANES), F32),
        v((2, 2 * SEGS, D // 4), BF), v((R, 2, 2 * SEGS, D // 4), BF), v((SEGS, LANES), F32), v((R, SEGS, LANES), F32),
        v((R, SEGS, D), F32), v((R, Q, D), BF), v((HEADS * L, D), F32), v((HEADS * L, D), BF), v((L, D), F32),
        v((L, D), F32),
        v((SEGS, LANES), F32), v((NR, SEGS, LANES), F32), v((CHUNKS * 8, D), F32), v((G, 8, D), F32), v((8, D), F32),
        v((NR, 8, D), F32), v((CHUNKS, 8, D), F32), v((8, D // 4), F32), v((G, 8, D // 4), F32), v((8, D // 4), F32),
        v((NR, 8, D // 4), F32),
        dma((7,)), dma((2,)), dma((G,)), dma((G,)), dma((NR,)), dma((NR,)), dma((3, G)), dma((3, G)),
        dma((3, G)), dma((3, R)), dma((G,)), dma((G,)), dma((NR,)), dma((NR,)), dma((G,)), dma((CHUNKS,)),
        dma((G,)), dma((G,)), dma((NR,)), dma((NR,)), *[v((Q, S), F32)] * (R + 2), *[v((Q, S), BF)] * R,
        v((S, D), BF), v((S, D), BF),
    ]
    vm, hbm, sm = (pl.BlockSpec(memory_space=m) for m in (pltpu.VMEM, pl.ANY, pltpu.SMEM))
    heads_sum, small_sum = pl.pallas_call(
        functools.partial(step_kernel, (R, S, G, NR, V)),
        out_shape=(jax.ShapeDtypeStruct((CHUNKS * 8, D), F32), jax.ShapeDtypeStruct((8, D // 4), F32)),
        in_specs=[sm, sm] + [vm] * 12 + [hbm] * 8,
        out_specs=(vm, vm),
        scratch_shapes=scratch,
        compiler_params=pltpu.CompilerParams(
            collective_id=0, has_side_effects=True, vmem_limit_bytes=60 * 1024 * 1024
        ),
    )(
        row_fill, task_weights, token_ids, segment_ids, task_ids, labels, leads, norm_gains, norm_biases,
        dense_biases, ffn_bias.reshape(1, -1), scale_d, scale_b, table,
        raw, position_table, qkv_weight, out_weight, ffn_in, ffn_out, vera_a, vera_b,
    )
    like = jax.ShapeDtypeStruct
    two, many = like((2, D), F32), like((CLASSES * TASKS, D), F32)
    loss, m_d, m_b, m_h, w_d, w_b, w_h, a_d, a_b, a_h, low, stats = pl.pallas_call(
        update_kernel,
        out_shape=(
            like((1, 1), F32), two, two, many, two, two, many, two, two, many, like((CLASSES * TASKS, D), BF), like((1, 2), F32),
        ),
        in_specs=[vm] * 11,
        out_specs=(vm,) * 12,
    )(heads_sum, small_sum, scale_d, scale_b, table, mom_d, mom_b, mom_h, avg_d, avg_b, avg_h)

    def unflat(value):
        return value.reshape(CLASSES, TASKS, D).transpose(1, 0, 2)

    return (
        loss.reshape(()), m_d, m_b, unflat(m_h), w_d, w_b, unflat(w_h), a_d, a_b, unflat(a_h), unflat(low), stats.reshape(2),
    )


def solution(mesh):
    sizes = (mesh.shape["heads"], mesh.shape["rows"])
    by_row = P("rows", None)
    return jax.shard_map(
        functools.partial(on_device, sizes),
        mesh=mesh,
        in_specs=(by_row, by_row, P("rows"), by_row, by_row, P(), P("heads", None)) + (P(),) * 20,
        out_specs=(P(),) * 12,
        check_vma=False,
    )
```

```python
import functools

import jax
import jax.numpy as jnp
from jax import lax
from jax.experimental import pallas as pl
from jax.experimental.pallas import tpu as pltpu
from jax.sharding import PartitionSpec as P

HEADS = 16
HDIM = 64
TASKS = 8
CLASSES = 3
SEGS = 8
LANES = 128
CHUNKS = 4
BLK = 256
GROUP = 128
SUB = 2
FT = 1024
UNROLL = 8
PART = 32
EPSILON = 1e-05
MOMENTUM = 0.9
AVERAGE = 0.8
RATE_D = 5.0
RATE_B = 20.0
RATE_HEADS = 0.3
NEG = -1e30
BF = jnp.bfloat16
F32 = jnp.float32
MESH = pl.DeviceIdType.MESH


def mm(left, right):
    return jnp.dot(left, right, preferred_element_type=F32)


def mm_t(left, right):
    return lax.dot_general(left, right, (((1,), (1,)), ((), ())), preferred_element_type=F32)


def mm_l(left, right):
    return lax.dot_general(left, right, (((0,), (0,)), ((), ())), preferred_element_type=F32)


def normed(values):
    centred = values - jnp.mean(values, -1, keepdims=True)
    rstd = lax.rsqrt(jnp.mean(centred * centred, -1, keepdims=True) + EPSILON)
    return centred * rstd, rstd


def norm_back(hat, rstd, gain, grad):
    scaled = grad * gain
    return rstd * (
        scaled
        - jnp.mean(scaled, -1, keepdims=True)
        - hat * jnp.mean(scaled * hat, -1, keepdims=True)
    )


def iota(shape, dim):
    return lax.broadcasted_iota(jnp.int32, shape, dim)


def update(weight, grad, moment, average, rate):
    moment_new = MOMENTUM * moment + grad
    weight_new = weight - rate * (grad + MOMENTUM * moment_new)
    return (moment_new, weight_new, AVERAGE * average + (1.0 - AVERAGE) * weight_new)


def gather_kernel(
    cfg, fill, ids, seg, words, x_out, lead_out,
    listv, lists, keyc, lead, bufs, stages, list_sem, buf_sem, out_sem,
):
    R, S, V = cfg
    D = x_out.shape[1]
    PER = S // BLK
    NB = R * PER
    HALVES = BLK // LANES
    STAGES = stages.shape[0]
    z = lax.axis_index("heads")
    slot = iota((1, S), 1)
    lane = iota((1, LANES), 1)
    jcol = iota((SEGS, 1), 0)
    row8 = iota((8, 1), 0)

    local = ids[...] - z * V
    segs = seg[...]
    fills = jnp.zeros((R, 1), jnp.int32)
    for r in range(R):
        fills = jnp.where(iota((R, 1), 0) == r, fill[r], fills)
    first = (slot == 0) | (segs != pltpu.roll(segs, 1, 1))
    need = (local >= 0) & (local < V) & (first | (slot < fills))
    upper = (iota((LANES, LANES), 0) <= iota((LANES, LANES), 1)).astype(F32).astype(BF)
    ahead = iota((BLK, BLK), 0) < iota((BLK, BLK), 1)

    def by_block(value):
        return jnp.concatenate([value[:, BLK * p : BLK * (p + 1)] for p in range(PER)], 0)

    pair = by_block(jnp.where(need, local // SUB, -1).astype(F32))
    half = by_block((local & (SUB - 1)).astype(F32))
    wanted = pair >= 0.0
    pair_col = pair.T
    same = [pair_col[:, q : q + 1] == pair[q : q + 1] for q in range(NB)]
    seen = [jnp.max(jnp.where(same[q] & ahead, 1.0, 0.0), 0, keepdims=True) for q in range(NB)]
    lead_one = jnp.where(wanted, 1.0 - jnp.concatenate(seen, 0), 0.0)
    halves = [lead_one[:, LANES * h : LANES * (h + 1)] for h in range(HALVES)]
    prefix = mm(jnp.concatenate(halves, 0).astype(BF), upper)
    runs, total = [], jnp.zeros((NB, 1), F32)
    for h in range(HALVES):
        run = prefix[NB * h : NB * (h + 1)]
        runs.append(run + total)
        total = total + run[:, LANES - 1 :]
    rank = jnp.where(lead_one > 0.0, jnp.concatenate(runs, 1) - 1.0, -1.0)
    held = jnp.maximum(rank, 0.0)
    count_row = jnp.zeros((1, LANES), F32)
    keys = []
    for q in range(NB):
        share = mm(jnp.broadcast_to(held[q : q + 1], (8, BLK)).astype(BF), same[q].astype(F32).astype(BF))
        keys.append(share[0:1])
    key = jnp.where(wanted, SUB * jnp.concatenate(keys, 0) + half, -1.0)
    key_col = key.T
    for r in range(R):
        starts = jnp.sum((segs[r : r + 1, :] < jcol).astype(jnp.int32), 1, keepdims=True)
        for p in range(PER):
            b, q = r * PER + p, p * R + r
            at_start = iota((1, BLK), 1) + BLK * p == starts
            lead_key = jnp.sum(jnp.where(at_start, key[q : q + 1] + 8.0, 0.0), 1, keepdims=True) - 8.0
            keyc[b] = jnp.concatenate([key_col[:, q : q + 1], lead_key, jnp.full((8, 1), -5.0, F32)], 0)
            order = rank[q : q + 1].astype(jnp.int32)
            spots = (iota((LANES, 1), 0) == jnp.where(order < 0, -1, order & (LANES - 1))).astype(F32).astype(BF)
            row_at = SUB * pair[q : q + 1].astype(jnp.int32)
            plane = jnp.where(row8 < HALVES, row_at & 255, row_at // 256)
            plane = jnp.where(((order // LANES) == (row8 & (HALVES - 1))) & (row8 < 2 * HALVES), plane, 0)
            both = mm_t(plane.astype(F32).astype(BF), spots)
            both = both[0:HALVES] + 256.0 * both[HALVES : 2 * HALVES]
            listv[HALVES * b : HALVES * (b + 1), :] = both.astype(jnp.int32)
            count_row = jnp.where(lane == b, total[q : q + 1], count_row)
    listv[HALVES * NB :, :] = jnp.broadcast_to(count_row.astype(jnp.int32), (8, LANES))
    to_scalar = pltpu.make_async_copy(listv, lists, list_sem.at[0])
    to_scalar.start()
    lead[...] = jnp.zeros_like(lead)
    for b in range(NB):
        bufs[b, 0 : GROUP * SUB // 8] = jnp.zeros((GROUP * SUB // 8, 8, D), BF)
    to_scalar.wait()

    def eights(b):
        n = lists[HALVES * NB, b]
        return jnp.where(n <= GROUP, (n + 7) // 8, (n + GROUP - 1) // GROUP * (GROUP // 8))

    def issue(r):
        for p in range(PER):
            b = r * PER + p

            def eight(i, _, b=b, h=0):
                for u in range(8):
                    word = lists[HALVES * b + h, i * 8 + u]
                    pltpu.make_async_copy(
                        words.at[pl.ds(pl.multiple_of(word, SUB), SUB)],
                        bufs.at[b, h * GROUP * SUB // 8 + i * SUB + u * SUB // 8, pl.ds(u * SUB % 8, SUB)],
                        buf_sem.at[r],
                    ).start()
                return 0

            lax.fori_loop(0, jnp.minimum(eights(b), GROUP // 8), eight, 0)

            @pl.when(lists[HALVES * NB, b] > GROUP)
            def more(eight=eight):
                lax.fori_loop(0, GROUP // 8, functools.partial(eight, h=1), 0)

    def arrive(r):
        total = eights(r * PER)
        for p in range(1, PER):
            total = total + eights(r * PER + p)
        part = bufs.at[0, pl.ds(0, SUB)]

        def eight(i, _):
            pltpu.make_async_copy(part, part, buf_sem.at[r]).wait()
            return 0

        lax.fori_loop(0, total, eight, 0)

    lanes = iota((1, GROUP * SUB), 1).astype(F32)

    def pick(b, g):
        one = (keyc[b] == lanes + float(g * GROUP * SUB)).astype(F32).astype(BF)
        rows = bufs[b, g * GROUP * SUB // 8 : (g + 1) * GROUP * SUB // 8]
        return mm(one, rows.reshape(GROUP * SUB, D))

    def add_lead(b, got):
        rows = pl.ds(pl.multiple_of(b // PER * SEGS, SEGS), SEGS)
        lead[rows, :] = lead[rows, :] + got

    def out_copy(b):
        k = lax.rem(b, STAGES)
        rows = pl.ds(pl.multiple_of(b * BLK, BLK), BLK)
        return pltpu.make_async_copy(stages.at[k], x_out.at[rows], out_sem.at[k])

    for r in range(R):
        issue(r)

    def row(r, _):
        arrive(r)

        def block(p, _):
            b = r * PER + p
            k = lax.rem(b, STAGES)
            pl.when(b >= STAGES)(lambda: out_copy(b - STAGES).wait())
            got = pick(b, 0)
            stages[k] = got[:BLK].astype(BF)
            add_lead(b, got[BLK : BLK + SEGS])

            @pl.when(lists[HALVES * NB, b] > GROUP)
            def more():
                got = pick(b, 1)
                stages[k] = stages[k] + got[:BLK].astype(BF)
                add_lead(b, got[BLK : BLK + SEGS])

            out_copy(b).start()
            return 0

        return lax.fori_loop(0, PER, block, 0)

    lax.fori_loop(0, R, row, 0)
    lead_out[...] = lead[...].astype(BF)
    for k in range(STAGES):
        out_copy(NB - STAGES + k).wait()


def gather(token_ids, segment_ids, row_fill, word_table):
    R, S = token_ids.shape
    V, D = word_table.shape
    PER = S // BLK
    NB = R * PER
    HALVES = BLK // LANES
    if V % SUB:
        word_table = jnp.pad(word_table, ((0, -V % SUB), (0, 0)))
    v, dma = pltpu.VMEM, pltpu.SemaphoreType.DMA
    vm, hbm, sm = (pl.BlockSpec(memory_space=m) for m in (pltpu.VMEM, pl.ANY, pltpu.SMEM))
    return pl.pallas_call(
        functools.partial(gather_kernel, (R, S, V)),
        out_shape=(jax.ShapeDtypeStruct((R * S, D), BF), jax.ShapeDtypeStruct((R * SEGS, D), BF)),
        in_specs=[sm, vm, vm, hbm],
        out_specs=(hbm, vm),
        scratch_shapes=[
            v((HALVES * NB + 8, LANES), jnp.int32),
            pltpu.SMEM((HALVES * NB + 8, LANES), jnp.int32), v((NB, BLK + 2 * SEGS, 1), F32),
            v((R * SEGS, D), F32),
            v((NB, BLK * SUB // 8, 8, D), BF), v((4, BLK, D), BF), dma((1,)), dma((R,)), dma((4,)),
        ],
        compiler_params=pltpu.CompilerParams(vmem_limit_bytes=60 * 1024 * 1024),
    )(row_fill, token_ids, segment_ids, word_table)


def step_kernel(
    cfg,
    fill, task_w, ids, seg, tasks, labels, lead_out, gains, shifts, biases, bias_in, scale_d, scale_b, table,
    x_h, place_h, qkv_h, out_h, fin_h, fout_h, va_h, vb_h,
    heads_sum, small_sum,
    x, qkv, outw, fin, fout, va, vb,
    place, places, lead_in, seg_eff, starts_s, xz_s, latent_s, eq_s, qk, ub, ua, ev, pack, st, st_in, pk, pk_in,
    act, slope, gh, tab, lse_out, lse_in, gpk, gpk_in, dlt_out, dlt_in, g_in, zq, zacc, zb, gq_s, fx,
    cnt_out, cnt_in, hs, h_in, hr, hr_in, ag, late, lz_in, lr, lr_in,
    load_sem, x_sem, e1_s, e1_r, cnt_ss, cnt_rs, rs_s, rs_r, g_s, g_r, h_ss, h_rs, hr_ss, hr_rs, ag_ss, ag_rs,
    lz_ss, lz_rs, lr_ss, lr_rs, *wide,
):
    R, S, G, NR, V = cfg
    expo, gdot, low, words = wide[:R], wide[R : R + 2], wide[R + 2 : 2 * R + 2], wide[2 * R + 2 :]
    D = x.shape[1]
    FF = fin.shape[1]
    PAIRS = HEADS // 2
    L = R * SEGS
    z = lax.axis_index("heads")
    rw = lax.axis_index("rows")
    own_r = lax.rem(z, R)

    def x_load(r, h):
        return pltpu.make_async_copy(x_h.at[pl.ds(pl.multiple_of(r * S, S), S)], words[h], x_sem.at[h])

    loads = [
        pltpu.make_async_copy(src, dst, load_sem.at[i])
        for i, (src, dst) in enumerate(
            (
                (va_h, va), (vb_h, vb), (qkv_h, qkv), (out_h, outw), (fin_h, fin), (fout_h, fout),
                (place_h, place),
            )
        )
    ]
    for copy in [x_load(0, 0), loads[6], x_load(1, 1)]:
        copy.start()

    barrier = pltpu.get_barrier_semaphore()
    for d in range(1, G):
        pl.semaphore_signal(barrier, inc=1, device_id={"heads": lax.rem(z + d, G)}, device_id_type=MESH)
    for d in range(1, NR):
        pl.semaphore_signal(barrier, inc=1, device_id={"rows": lax.rem(rw + d, NR)}, device_id_type=MESH)
    pl.semaphore_wait(barrier, G - 1 + NR - 1)

    def over(axis, d, src, dst, send, recv):
        me, size = (z, G) if axis == "heads" else (rw, NR)
        return pltpu.make_async_remote_copy(
            src_ref=src, dst_ref=dst, send_sem=send, recv_sem=recv,
            device_id={axis: lax.rem(me + d, size)}, device_id_type=MESH,
        )

    lane = iota((1, LANES), 1)
    low_half = lane < HDIM
    jcol = iota((SEGS, 1), 0)
    slot = iota((1, S), 1)

    def expand(f):
        tiles = [jnp.where(low_half, f[:, 2 * t : 2 * t + 1], f[:, 2 * t + 1 : 2 * t + 2]) for t in range(PAIRS)]
        return jnp.concatenate(tiles, 1)

    def compress(v):
        out = jnp.zeros((v.shape[0], LANES), F32)
        for t in range(PAIRS):
            tile = v[:, LANES * t : LANES * (t + 1)]
            a = jnp.sum(jnp.where(low_half, tile, 0.0), -1, keepdims=True)
            b = jnp.sum(jnp.where(low_half, 0.0, tile), -1, keepdims=True)
            out = jnp.where(lane == 2 * t, a, jnp.where(lane == 2 * t + 1, b, out))
        return out

    e1 = [over("heads", d, lead_out, lead_in.at[d], e1_s.at[d], e1_r.at[d]) for d in range(1, G)]
    for copy in e1:
        copy.start()

    eye = iota((SEGS, SEGS), 0) == iota((SEGS, SEGS), 1)
    task_lane = lane & (TASKS - 1)
    counts = jnp.zeros((SEGS, LANES), F32)
    for r in range(R):
        seg_row = seg[r : r + 1, :]
        local = ids[r : r + 1, :] - z * V
        own = (local >= 0) & (local < V)
        first = (slot == 0) | (seg_row != pltpu.roll(seg_row, 1, 1))
        seg_eff[r : r + 1, :] = jnp.where(own & (first | (slot < fill[r])), seg_row, -1)
        starts = jnp.sum((seg_row < jcol).astype(jnp.int32), 1, keepdims=True)
        starts_s[r] = jnp.broadcast_to(starts, (SEGS, LANES))
        lead = (starts < fill[r]).astype(F32)
        task = jnp.sum(jnp.where(eye, tasks[r : r + 1, :], 0), 1, keepdims=True)
        counts = counts + jnp.where((task == task_lane) & (lane < TASKS * CLASSES), lead, 0.0)
    cnt_out[...] = counts
    cnt = [over("rows", d, cnt_out, cnt_in.at[d], cnt_ss.at[d], cnt_rs.at[d]) for d in range(1, NR)]
    for copy in cnt:
        copy.start()
    gain0, shift0 = gains[0:1, :], shifts[0:1, :]
    loads[6].wait()
    places[...] = place[2:, :]
    prow = iota((places.shape[0], 1), 0)

    STEP = expo[0].shape[0]
    blocks = S // STEP

    def norm_row(r, h):
        seg_row = seg[pl.ds(r, 1), :]
        begin = jnp.sum(jnp.where(seg_row == jcol, starts_s[r][:, 0:1], 0), 0, keepdims=True)
        offset = slot - begin
        x_load(r, h).wait()

        def place_rows(b):
            one = (prow == offset[:, b * STEP : (b + 1) * STEP]).astype(F32).astype(BF)
            expo[b % R][...] = mm_l(one, places[...])

        place_rows(0)
        for b in range(blocks):
            if b + 1 < blocks:
                place_rows(b + 1)
            for c in range(0, STEP, PART):
                at = b * STEP + c
                hat, _ = normed(expo[b % R][c : c + PART, :] + words[h][at : at + PART, :].astype(F32))
                x[pl.ds(pl.multiple_of(r * S + at, PART), PART), :] = (hat * gain0 + shift0).astype(BF)

    def norm_two(i, _):
        for h in range(2):
            norm_row(2 * i + h, h)
            pl.when(i + 1 < R // 2)(lambda h=h: x_load(2 * i + 2 + h, h).start())
        return 0

    loads[0].start()
    loads[1].start()
    loads[2].start()
    lax.fori_loop(0, R // 2, norm_two, 0)

    for copy in e1:
        copy.wait()
    word = lead_out[...].astype(F32)
    for d in range(1, G):
        word = word + lead_in[d].astype(F32)
    hat, _ = normed(word + places[0:1, :].astype(F32))
    xz = hat * gain0 + shift0
    xz_s[...] = xz
    xl = xz.astype(BF)
    loads[0].wait()
    latent = mm(xl, va[...])
    latent_s[...] = latent
    loads[1].wait()
    eq_s[...] = mm((latent * scale_d[0:1, :]).astype(BF), vb[...])
    loads[2].wait()
    for copy in loads[3:6]:
        copy.start()

    def tile_at(t):
        return pl.ds(pl.multiple_of(LANES * t, LANES), LANES)

    for t in range(PAIRS):
        r = mm(xl, qkv[:, 384 * t : 384 * t + 256])
        at = slice(LANES * t, LANES * (t + 1))
        q = jnp.where(low_half, r[:, :LANES], r[:, LANES:]) + (biases[0:1, at] + scale_b[0:1, at] * eq_s[:, at])
        gq_s[:, at] = pltpu.roll(q.astype(BF).astype(F32) * 0.125, HDIM, 1)

    def keys_at(t):
        first = max(384 * t - LANES, 0)
        return slice(first, min(384 * t + LANES, 3 * D))

    def both_heads(t):
        parts, none = [], jnp.zeros((L, LANES), F32)
        if t > 0:
            odd = jnp.where(low_half, gq_s[:, LANES * (t - 1) : LANES * t], 0.0)
            parts.append(odd if t == PAIRS else jnp.concatenate([odd, none], 1))
        if t < PAIRS:
            even = jnp.where(low_half, 0.0, gq_s[:, LANES * t : LANES * (t + 1)])
            parts.append(even if t == 0 else jnp.concatenate([none, even], 1))
        return jnp.concatenate(parts, 0).astype(BF)

    even = mm_t(both_heads(0), qkv[:, keys_at(0)])
    for t in range(PAIRS):
        found = mm_t(both_heads(t + 1), qkv[:, keys_at(t + 1)])
        for r_ in range(R):
            rows = slice(r_ * SEGS, (r_ + 1) * SEGS)
            qk[r_, 16 * t : 16 * (t + 1), :] = jnp.concatenate([even[rows], found[:L][rows]], 0).astype(BF)
        even = found[L:]

    Q = HEADS * SEGS
    qj = lax.rem(iota((Q, 1), 0), SEGS)
    hsub = iota((HEADS, SEGS, LANES), 0)
    hlane = iota((HEADS, SEGS, LANES), 2)

    def to_lanes(col):
        return jnp.sum(jnp.where(hsub == hlane, col.reshape(HEADS, SEGS, 1), 0.0), 0)

    def to_col(f):
        wide = jnp.broadcast_to(f[None], (HEADS, SEGS, LANES))
        return jnp.sum(jnp.where(hsub == hlane, wide, 0.0), -1, keepdims=True).reshape(Q, 1)

    def rows_of(r):
        return x[r * S : (r + 1) * S, :]

    def score(r):
        expo[r][...] = mm_t(qk[r], rows_of(r))

    def soften(r):
        tops, sums = [], []
        for c in range(0, Q, PART):
            rows = slice(c, c + PART)
            mask = seg_eff[r : r + 1, :] == qj[rows]
            sc = jnp.where(mask, expo[r][rows, :], NEG)
            top = jnp.max(sc, -1, keepdims=True)
            e = jnp.where(mask, jnp.exp(sc - top), 0.0)
            expo[r][rows, :] = e
            low[r][rows, :] = e.astype(BF)
            tops.append(top)
            sums.append(jnp.sum(e, -1, keepdims=True))
        top, total = jnp.concatenate(tops, 0), jnp.concatenate(sums, 0)
        st[r] = to_lanes(top) + pltpu.roll(to_lanes(total), HDIM, 1)

    def mix(r):
        return mm(low[r][...], rows_of(r)).reshape(HEADS, SEGS, D)

    def staged(first_part, second_part, between):
        first_part(0)
        held = None
        for r in range(R):
            if r + 1 < R:
                first_part(r + 1)
            second_part(r)
            part = mix(r)
            if r % 2:
                ub[:, SEGS * (r - 1) : SEGS * (r + 1), :] = jnp.concatenate([held, part], 1).astype(BF)
            held = part
            between(r)

    staged(score, soften, lambda r: None)

    def row_of(d):
        return lax.rem(lax.rem(z + d, G), R)

    rs = [over("heads", d, st.at[row_of(d)], st_in.at[d], rs_s.at[0, d], rs_r.at[0, d]) for d in range(1, G)]
    for copy in rs:
        copy.start()

    NT = 256

    def cols(n):
        return pl.ds(pl.multiple_of(NT * n, NT), NT)

    def latents(n, _):
        ua[:, cols(n)] = mm(ub[...].reshape(HEADS * L, D), va[:, cols(n)])
        return 0

    lax.fori_loop(0, D // NT, latents, 0, unroll=D // NT)

    def values_at(t):
        return pl.ds(pl.multiple_of(LANES * (3 * t + 1), LANES), 2 * LANES)

    def two(t):
        return pl.ds(pl.multiple_of(2 * L * t, 2 * L), 2 * L)

    def values(t, _):
        at = tile_at(t)
        v = mm(ub[pl.ds(2 * t, 2)].reshape(2 * L, D), qkv[:, values_at(t)])
        pair = mm((ua[two(t), :] * scale_d[1:2, :]).astype(BF), vb[:, at])
        extra = jnp.where(low_half, pair[:L], pair[L:])
        ev[:, at] = extra
        mixed = jnp.where(low_half, v[:L, :LANES], v[L:, LANES:]) + scale_b[1:2, at] * extra
        pack[:, :, at] = mixed.reshape(R, SEGS, LANES)
        return 0

    for half in range(2):
        lax.fori_loop(half * PAIRS // 2, (half + 1) * PAIRS // 2, values, 0, unroll=PAIRS // 2)
        left, quarter = half * D // 2, D // 4
        for r in range(R):
            parts = [pack[r, :, left : left + quarter], pack[r, :, left + quarter : left + 2 * quarter]]
            pk[r, half] = jnp.concatenate(parts, 0).astype(BF)
        leg = [
            over("heads", d, pk.at[row_of(d), half], pk_in.at[d, half], rs_s.at[1 + half, d], rs_r.at[1 + half, d])
            for d in range(1, G)
        ]
        for copy in leg:
            copy.start()
        rs = rs + leg

    def widen(halves):
        both = [halves[i].astype(F32) for i in range(2)]
        return jnp.concatenate([v for h in both for v in (h[:SEGS], h[SEGS:])], 1)

    for copy in cnt:
        copy.wait()
    total = cnt_out[...]
    for d in range(1, NR):
        total = total + cnt_in[d]
    count = jnp.sum(total, 0, keepdims=True)
    weights = jnp.zeros((1, LANES), F32)
    for t in range(TASKS):
        weights = jnp.where(task_lane == t, task_w[t].astype(F32), weights)
    coef = weights / jnp.maximum(count, 1.0)
    task = jnp.sum(jnp.where(eye, tasks[pl.ds(own_r, 1), :], 0), 1, keepdims=True)
    label = jnp.sum(jnp.where(eye, labels[pl.ds(own_r, 1), :], 0), 1, keepdims=True)
    picked = (task == task_lane) & (lane < TASKS * CLASSES)
    target = picked & (lane // TASKS == label)
    leads = (starts_s[own_r][:, 0:1] < fill[own_r]) & (z < R)
    weight = jnp.sum(jnp.where(target, coef, 0.0), -1, keepdims=True)
    weight = jnp.where(leads, weight, 0.0)
    tab[...] = jnp.concatenate([table[...], jnp.zeros((LANES - TASKS * CLASSES, D), F32)], 0).astype(BF)

    for copy in rs:
        copy.wait()
    got = [pack[own_r]] + [widen(pk_in[d]) for d in range(1, G)]
    stat = [st[own_r]] + [st_in[d] for d in range(1, G)]
    top = stat[0]
    for part in stat[1:]:
        top = jnp.maximum(top, part)
    shrink = [jnp.exp(part - top) for part in stat]
    tot = jnp.zeros((SEGS, LANES), F32)
    for part, s in zip(stat, shrink):
        tot = tot + pltpu.roll(part, HDIM, 1) * s
    tot = jnp.where(lane < HEADS, tot, 1.0)
    lse_out[...] = top + jnp.log(tot)
    mixed = jnp.zeros((SEGS, D), F32)
    for part, s in zip(got, shrink):
        mixed = mixed + expand(s / tot) * part
    mixed = mixed + biases[1:2, :]

    def guarded(cond, f):
        if cond is None:
            f()
        else:
            pl.when(cond)(f)

    mine = None if G == R else z < R

    def hand_out(k, src, dst):
        def start():
            for d in range(1, G):
                over("heads", d, src, dst.at[own_r], g_s.at[k, d], g_r.at[k, own_r]).start()

        def keep():
            dst[own_r] = src[...]

        guarded(mine, start)
        guarded(mine, keep)

    def take_in(k, src, dst):
        def one(r):
            pltpu.make_async_remote_copy(
                src_ref=src, dst_ref=dst.at[r], send_sem=g_s.at[k, 0], recv_sem=g_r.at[k, r],
                device_id={"heads": z}, device_id_type=MESH,
            ).wait_recv()

        for r in range(R):
            pl.when(z != r)(functools.partial(one, r))

    hand_out(0, lse_out, lse_in)

    loads[3].wait()
    r_one = xz_s[pl.ds(pl.multiple_of(own_r * SEGS, SEGS), SEGS), :] + mm(mixed.astype(BF), outw[...]) + biases[2:3, :]
    hat1, rstd1 = normed(r_one)
    x_one = hat1 * gains[1:2, :] + shifts[1:2, :]
    x_one_low = x_one.astype(BF)
    loads[4].wait()

    for n in range(FF // FT):
        at = slice(FT * n, FT * (n + 1))
        act[:, at] = mm(x_one_low, fin[:, at])
    h = act[...] + bias_in[...]
    half = 0.5 * (1.0 + lax.erf(h * 0.7071067811865476))
    act[...] = h * half
    slope[...] = half + h * (0.3989422804014327 * jnp.exp(-0.5 * h * h))
    loads[5].wait()
    act_low = act[...].astype(BF)

    def ffn_out_tile(n, _):
        fx[0:SEGS, cols(n)] = mm(act_low, fout[:, cols(n)])
        return 0

    lax.fori_loop(0, D // NT, ffn_out_tile, 0, unroll=D // NT)
    hat2, rstd2 = normed(x_one + fx[0:SEGS, :] + biases[3:4, :])
    x_two = (hat2 * gains[2:3, :] + shifts[2:3, :]).astype(BF)
    logits = mm_t(x_two, tab[...])
    chosen = jnp.where(picked, logits, NEG)
    peak = jnp.max(chosen, -1, keepdims=True)
    sums = jnp.sum(jnp.where(picked, jnp.exp(chosen - peak), 0.0), -1, keepdims=True)
    log_sum = peak + jnp.log(sums)
    hit = jnp.sum(jnp.where(target, logits, 0.0), -1, keepdims=True)
    loss = jnp.sum(weight * (log_sum - hit), 0, keepdims=True)
    soft = jnp.where(picked, jnp.exp(chosen - log_sum), 0.0) - target.astype(F32)
    g_logits = (weight * soft).astype(BF)
    g_two = mm(g_logits, tab[...])
    g_r2 = norm_back(hat2, rstd2, gains[2:3, :], g_two)
    g_f = g_r2.astype(BF)

    for n in range(FF // FT):
        at = slice(FT * n, FT * (n + 1))
        gh[:, at] = mm_t(g_f, fout[at, :]) * slope[:, at]
    gh_low = gh[...].astype(BF)

    def back_in(n, _):
        fx[0:SEGS, cols(n)] = mm_t(gh_low, fin[cols(n), :])
        return 0

    lax.fori_loop(0, D // NT, back_in, 0, unroll=D // NT)
    g_r1 = norm_back(hat1, rstd1, gains[1:2, :], g_r2 + fx[0:SEGS, :])
    g_mixed = mm_t(g_r1.astype(BF), outw[...]).astype(BF).astype(F32)
    quarters = [g_mixed[:, i * D // 4 : (i + 1) * D // 4] for i in range(4)]
    gpk[0] = jnp.concatenate(quarters[0:2], 0).astype(BF)
    gpk[1] = jnp.concatenate(quarters[2:4], 0).astype(BF)
    hand_out(1, gpk, gpk_in)
    dlt_out[...] = compress(g_mixed * mixed) - compress(g_mixed * biases[1:2, :])
    hand_out(2, dlt_out, dlt_in)
    hs[...] = mm(g_logits.astype(F32).T.astype(BF), x_two)[: CHUNKS * 8, :]
    hs[TASKS * CLASSES : TASKS * CLASSES + 8, :] = jnp.broadcast_to(loss, (8, D))

    def spread(src, dst, send, recv, limit, action):
        for d in range(1, G):
            copy = over("heads", d, src(lax.rem(z + d, G)), dst(d), send.at[d], recv(d))
            cond = limit(lax.rem(z + d, G))
            if cond is None:
                action(copy)
            else:
                pl.when(cond)(functools.partial(action, copy))

    def chunk_of(peer):
        return hs.at[pl.ds(pl.multiple_of(8 * lax.rem(peer, CHUNKS), 8), 8)]

    def small(peer):
        return None if G == CHUNKS else peer < CHUNKS

    holder = None if G == CHUNKS else z < CHUNKS
    take_in(0, lse_out, lse_in)
    scale = [jnp.exp(st[r] - lse_in[r]) for r in range(R)]
    factor = jnp.concatenate([jnp.where(lane < HEADS, s, 0.0) for s in scale], 0)
    ev[...] = ev[...] * expand(factor)
    for r in range(R):
        f = to_col(factor[r * SEGS : (r + 1) * SEGS])
        for c in range(0, Q, PART):
            rows = slice(c, c + PART)
            expo[r][rows, :] = expo[r][rows, :] * f[rows]
    take_in(1, gpk, gpk_in)
    for r in range(R):
        g_in[r] = widen(gpk_in[r])


    def back_value(t, acc):
        at = tile_at(t)
        g = g_in[:, :, at].reshape(L, LANES)
        none = jnp.zeros((L, LANES), F32)
        upper = jnp.concatenate([jnp.where(low_half, g, 0.0), none], 1)
        lower = jnp.concatenate([none, jnp.where(low_half, 0.0, g)], 1)
        zacc[two(t), :] = mm_t(jnp.concatenate([upper, lower], 0).astype(BF), qkv[:, values_at(t)])
        gb = g * scale_b[1:2, at]
        both = jnp.concatenate([jnp.where(low_half, gb, 0.0), jnp.where(low_half, 0.0, gb)], 0).astype(BF)
        back = mm_t(both, vb[:, at])
        f0 = jnp.sum(jnp.where(lane == 2 * t, factor, 0.0), -1, keepdims=True)
        f1 = jnp.sum(jnp.where(lane == 2 * t + 1, factor, 0.0), -1, keepdims=True)
        acc = acc + jnp.sum(jnp.concatenate([f0, f1], 0) * ua[two(t), :] * back, 0, keepdims=True)
        zb[two(t), :] = (back * scale_d[1:2, :]).astype(BF)
        return acc

    grad_d1 = lax.fori_loop(0, PAIRS, back_value, jnp.zeros((1, D), F32), unroll=UNROLL)
    grad_b1 = jnp.sum(g_in[...].reshape(L, D) * ev[...], 0, keepdims=True)
    extra = TASKS * CLASSES + 1
    hs[extra : extra + 2, :] = jnp.concatenate([grad_d1, grad_b1], 0)
    spread(chunk_of, lambda d: h_in.at[d], h_ss, lambda d: h_rs.at[d], small, lambda c: c.start())

    def back_latent(n, _):
        at = cols(n)
        part = (zacc[:, at] + mm_t(zb[...], va[at, :])).reshape(HEADS, R, SEGS, NT)
        for r in range(R):
            zq[r, :, at] = part[:, r].reshape(Q, NT).astype(BF)
        return 0

    lax.fori_loop(0, D // NT, back_latent, 0, unroll=D // NT)

    def relay():
        acc = chunk_of(z)[...]
        for d in range(1, G):
            over("heads", d, chunk_of(z), h_in.at[d], h_ss.at[d], h_rs.at[d]).wait_recv()
            acc = acc + h_in[d]
        hr[...] = acc
        for d in range(1, NR):
            over("rows", d, hr, hr_in.at[d], hr_ss.at[d], hr_rs.at[d]).start()

    def slope_of(r):
        gdot[r % 2][...] = mm_t(zq[r], rows_of(r))

    def bend(r):
        delta = to_col(dlt_in[r])
        for c in range(0, Q, PART):
            rows = slice(c, c + PART)
            ds = expo[r][rows, :] * (gdot[r % 2][rows, :] - delta[rows])
            low[r][rows, :] = ds.astype(BF)

    take_in(2, dlt_out, dlt_in)
    staged(slope_of, bend, lambda r: guarded(holder, relay) if r == R // 2 - 1 else None)

    def relay_two():
        acc = hr[...]
        for d in range(1, NR):
            over("rows", d, hr, hr_in.at[d], hr_ss.at[d], hr_rs.at[d]).wait()
            acc = acc + hr_in[d]
        ag[lax.rem(z, CHUNKS)] = acc
        for d in range(1, G):
            c = lax.rem(z, CHUNKS)
            over("heads", d, ag.at[c], ag.at[c], ag_ss.at[d], ag_rs.at[c]).start()

    even = mm(ub[0], qkv[:, keys_at(0)])
    for t in range(PAIRS):
        heads = slice(2 * t + 1, min(2 * t + 3, HEADS))
        found = mm(ub[heads].reshape(-1, D), qkv[:, keys_at(t + 1)])
        both = jnp.where(low_half, found[:L, :LANES], even)
        gq_s[:, LANES * t : LANES * (t + 1)] = pltpu.roll(both, HDIM, 1) * 0.125
        even = found[L:, LANES:]
    g_query = gq_s[...]
    grad_b0 = jnp.sum(g_query * eq_s[...], 0, keepdims=True)
    back = mm_t((g_query * scale_b[0:1, :]).astype(BF), vb[...])
    grad_d0 = jnp.sum(latent_s[...] * back, 0, keepdims=True)
    two_rows = jnp.concatenate([grad_d0, grad_b0], 0)
    late[...] = jnp.concatenate([two_rows[:, i * D // 4 : (i + 1) * D // 4] for i in range(4)], 0)
    leg = [over("heads", d, late, lz_in.at[d], lz_ss.at[d], lz_rs.at[d]) for d in range(1, G)]
    for copy in leg:
        copy.start()
    guarded(holder, relay_two)
    for copy in leg:
        copy.wait()
    acc = late[...]
    for d in range(1, G):
        acc = acc + lz_in[d]
    lr[...] = acc
    leg = [over("rows", d, lr, lr_in.at[d], lr_ss.at[d], lr_rs.at[d]) for d in range(1, NR)]
    for copy in leg:
        copy.start()

    for c in range(CHUNKS):
        def arrive(c=c):
            pltpu.make_async_remote_copy(
                src_ref=ag.at[c], dst_ref=ag.at[c], send_sem=ag_ss.at[0], recv_sem=ag_rs.at[c],
                device_id={"heads": z}, device_id_type=MESH,
            ).wait_recv()

        pl.when(z != c)(arrive)
    heads_sum[...] = ag[...].reshape(CHUNKS * 8, D)
    def handed():
        for k, (src, dst) in enumerate(((lse_out, lse_in), (gpk, gpk_in), (dlt_out, dlt_in))):
            for d in range(1, G):
                over("heads", d, src, dst.at[own_r], g_s.at[k, d], g_r.at[k, own_r]).wait_send()

    guarded(mine, handed)
    spread(chunk_of, lambda d: h_in.at[d], h_ss, lambda d: h_rs.at[d], small, lambda c: c.wait_send())

    def sent():
        for d in range(1, G):
            c = lax.rem(z, CHUNKS)
            over("heads", d, ag.at[c], ag.at[c], ag_ss.at[d], ag_rs.at[c]).wait_send()

    guarded(holder, sent)
    for copy in leg:
        copy.wait()
    acc = lr[...]
    for d in range(1, NR):
        acc = acc + lr_in[d]
    small_sum[...] = acc


def update_kernel(
    heads_sum, small_sum, scale_d, scale_b, table, mom_d, mom_b, mom_h, avg_d, avg_b, avg_h,
    loss, m_d, m_b, m_h, w_d, w_b, w_h, a_d, a_b, a_h, low, stats,
):
    count = table.shape[0]
    pairs = jnp.concatenate([small_sum[2 * i : 2 * i + 2, :] for i in range(4)], 1)
    more = heads_sum[count + 1 : count + 3, :]
    grad_d = jnp.concatenate([pairs[0:1], more[0:1]], 0)
    grad_b = jnp.concatenate([pairs[1:2], more[1:2]], 0)
    m_d[...], new_d, a_d[...] = update(scale_d[...], grad_d, mom_d[...], avg_d[...], RATE_D)
    m_b[...], new_b, a_b[...] = update(scale_b[...], grad_b, mom_b[...], avg_b[...], RATE_B)
    m_h[...], new_h, a_h[...] = update(table[...], heads_sum[:count, :], mom_h[...], avg_h[...], RATE_HEADS)
    w_d[...], w_b[...], w_h[...], low[...] = new_d, new_b, new_h, new_h.astype(BF)
    loss[...] = heads_sum[count : count + 1, 0:1]
    rms = [jnp.sqrt(jnp.mean(jnp.mean(v * v, 1, keepdims=True), 0, keepdims=True)) for v in (new_d, new_b)]
    stats[...] = jnp.concatenate(rms, 1)


def on_device(
    sizes,
    token_ids, segment_ids, row_fill, task_ids, labels, task_weights,
    word_table, position_table, norm_gains, norm_biases, dense_biases,
    qkv_weight, out_weight, ffn_in, ffn_bias, ffn_out, vera_a, vera_b,
    scale_d, scale_b, task_heads, mom_d, mom_b, mom_heads, avg_d, avg_b, avg_heads,
):
    G, NR = sizes
    R, S = token_ids.shape
    V, D = word_table.shape
    FF = ffn_in.shape[1]
    L, Q, T = R * SEGS, HEADS * SEGS, R * S
    raw, leads = gather(token_ids, segment_ids, row_fill, word_table)

    def flat(value):
        return value.transpose(1, 0, 2).reshape(CLASSES * TASKS, D)

    table, mom_h, avg_h = flat(task_heads), flat(mom_heads), flat(avg_heads)
    v = pltpu.VMEM
    dma = pltpu.SemaphoreType.DMA
    scratch = [
        v((T, D), BF), v(qkv_weight.shape, BF), v(out_weight.shape, BF), v(ffn_in.shape, BF), v(ffn_out.shape, BF),
        v(vera_a.shape, BF), v(vera_b.shape, BF),
        v(position_table.shape, BF), v((position_table.shape[0] - 2, D), BF), v((G, L, D), BF), v((R, S), jnp.int32), v((R, SEGS, LANES), jnp.int32), v((L, D), F32),
        v((L, D), F32), v((L, D), F32), v((R, Q, D), BF), v((HEADS, L, D), BF),
        v((HEADS * L, D), F32), v((L, D), F32), v((R, SEGS, D), F32), v((R, SEGS, LANES), F32), v((G, SEGS, LANES), F32),
        v((R, 2, 2 * SEGS, D // 4), BF), v((G, 2, 2 * SEGS, D // 4), BF),
        v((SEGS, FF), F32), v((SEGS, FF), F32), v((SEGS, FF), F32), v((LANES, D), BF), v((SEGS, LANES), F32), v((R, SEGS, LANES), F32),
        v((2, 2 * SEGS, D // 4), BF), v((R, 2, 2 * SEGS, D // 4), BF), v((SEGS, LANES), F32), v((R, SEGS, LANES), F32),
        v((R, SEGS, D), F32), v((R, Q, D), BF), v((HEADS * L, D), F32), v((HEADS * L, D), BF), v((L, D), F32),
        v((L, D), F32),
        v((SEGS, LANES), F32), v((NR, SEGS, LANES), F32), v((CHUNKS * 8, D), F32), v((G, 8, D), F32), v((8, D), F32),
        v((NR, 8, D), F32), v((CHUNKS, 8, D), F32), v((8, D // 4), F32), v((G, 8, D // 4), F32), v((8, D // 4), F32),
        v((NR, 8, D // 4), F32),
        dma((7,)), dma((2,)), dma((G,)), dma((G,)), dma((NR,)), dma((NR,)), dma((3, G)), dma((3, G)),
        dma((3, G)), dma((3, R)), dma((G,)), dma((G,)), dma((NR,)), dma((NR,)), dma((G,)), dma((CHUNKS,)),
        dma((G,)), dma((G,)), dma((NR,)), dma((NR,)), *[v((Q, S), F32)] * (R + 2), *[v((Q, S), BF)] * R,
        v((S, D), BF), v((S, D), BF),
    ]
    vm, hbm, sm = (pl.BlockSpec(memory_space=m) for m in (pltpu.VMEM, pl.ANY, pltpu.SMEM))
    heads_sum, small_sum = pl.pallas_call(
        functools.partial(step_kernel, (R, S, G, NR, V)),
        out_shape=(jax.ShapeDtypeStruct((CHUNKS * 8, D), F32), jax.ShapeDtypeStruct((8, D // 4), F32)),
        in_specs=[sm, sm] + [vm] * 12 + [hbm] * 8,
        out_specs=(vm, vm),
        scratch_shapes=scratch,
        compiler_params=pltpu.CompilerParams(
            collective_id=0, has_side_effects=True, vmem_limit_bytes=60 * 1024 * 1024
        ),
    )(
        row_fill, task_weights, token_ids, segment_ids, task_ids, labels, leads, norm_gains, norm_biases,
        dense_biases, ffn_bias.reshape(1, -1), scale_d, scale_b, table,
        raw, position_table, qkv_weight, out_weight, ffn_in, ffn_out, vera_a, vera_b,
    )
    like = jax.ShapeDtypeStruct
    two, many = like((2, D), F32), like((CLASSES * TASKS, D), F32)
    loss, m_d, m_b, m_h, w_d, w_b, w_h, a_d, a_b, a_h, low, stats = pl.pallas_call(
        update_kernel,
        out_shape=(
            like((1, 1), F32), two, two, many, two, two, many, two, two, many, like((CLASSES * TASKS, D), BF), like((1, 2), F32),
        ),
        in_specs=[vm] * 11,
        out_specs=(vm,) * 12,
    )(heads_sum, small_sum, scale_d, scale_b, table, mom_d, mom_b, mom_h, avg_d, avg_b, avg_h)

    def unflat(value):
        return value.reshape(CLASSES, TASKS, D).transpose(1, 0, 2)

    return (
        loss.reshape(()), m_d, m_b, unflat(m_h), w_d, w_b, unflat(w_h), a_d, a_b, unflat(a_h), unflat(low), stats.reshape(2),
    )


def solution(mesh):
    sizes = (mesh.shape["heads"], mesh.shape["rows"])
    by_row = P("rows", None)
    return jax.shard_map(
        functools.partial(on_device, sizes),
        mesh=mesh,
        in_specs=(by_row, by_row, P("rows"), by_row, by_row, P(), P("heads", None)) + (P(),) * 20,
        out_specs=(P(),) * 12,
        check_vma=False,
    )
```
